256 devices in a mesh: node: 32 (over z_hi, y, x), local: 8 (over z_lo, core).
Axes of the slice: x: 4, y: 4, z: 8 (z_hi: 2, z_lo: 4; z = z_hi * 4 + z_lo), core: 2. Of those that a mesh axis runs over, the one named last changes fastest.
Arguments:
- tokens: bfloat16 [131072, 4096], P(('node', 'local')), may hold values from -24 to 24
- out_grad: bfloat16 [131072, 1024], P(('node', 'local')), may hold values from -8.9375 to 8.9375
- next_tokens: bfloat16 [131072, 4096], P(('node', 'local')), may hold values from -6 to 6
- overflow: int32 [256], P(('node', 'local')), may hold values from 0 to 1, as said below
- master: float32 [4096, 1024], P(('node', 'local')), may hold values from -0.09375 to 0.09375
- first_moment: float32 [4096, 1024], P(('node', 'local')), may hold values from -12 to 12
- second_moment: float32 [4096, 1024], P(('node', 'local')), may hold values from 1 to 16
Outputs:
- new_master: float32 [4096, 1024], P(('node', 'local'))
- new_first: float32 [4096, 1024], P(('node', 'local'))
- new_second: float32 [4096, 1024], P(('node', 'local'))
- secondary: bfloat16 [32, 128, 1024], P(None, 'local')
- next_projection: bfloat16 [131072, 1024], P(('node', 'local'))
The draws below stay inside these ranges and needn't reach their ends.
Inputs may be any that keep to these rules, and one draw needn't show every extreme that they name: At least one device has overflow 0 and at least one has overflow 1.
All inputs are finite; a program needn't handle non-finite values.
Results may differ from the reference program's by a relative error of at most 0.0049.
Values may be sent and summed in bfloat16 or wider, within the bound.
A program may use at most 128 MiB of HBM per device.

```python
import math
import jax
import jax.numpy as jnp

DIN = 4096
TOK_DEV = 512
STEP = 10
KV = 1024
TOKENS = 131072
NODE_ROWS = 128
N_NODE = 32
DEVICES = 256


def draw_overflow(key, part):
    key = jax.random.fold_in(key, 5)
    span = max(DEVICES - 1, 1)
    ticket = jax.random.randint(key, (DEVICES,), 0, 4 * span)
    position = jnp.arange(DEVICES, dtype=jnp.int32)
    flagged = (ticket < span + 2 * position).astype(jnp.int32)
    where_zero = jax.random.randint(jax.random.fold_in(key, 1), (), 0, DEVICES)
    flagged = flagged.at[where_zero].set(0)
    flagged = flagged.at[(where_zero + 1) % DEVICES].set(1)
    return flagged.astype(jnp.int32)


def raised(drawn, key, source, target, parts, factor):
    def block_of(axis_at):
        return (jnp.arange(drawn.shape[axis_at]) // (drawn.shape[axis_at] // parts)).reshape((-1,) + (1,) * (drawn.ndim - 1 - axis_at))

    first = jax.random.permutation(key, parts)[block_of(target)]
    second = (block_of(target) + parts // 2) % parts
    return jnp.where((block_of(source) == first) | (block_of(source) == second), factor * drawn, drawn)


def levels(own_key, dims, pieces, least, high):
    level, own = 1.0, jax.random.fold_in(own_key, 6)
    for dim, shards_of in pieces:
        draws = jnp.exp(jax.random.uniform(jax.random.fold_in(own, dim), (shards_of,), jnp.float32, least / len(pieces), high / len(pieces)))
        level = level * jnp.repeat(draws, dims[dim] // shards_of).reshape([-1 if axis == dim else 1 for axis in range(len(dims))])
    return level


def centred(stream_key, extent, scale, limit, shards=(), kind=jnp.bfloat16):
    result = scale * jax.random.normal(stream_key, extent, jnp.float32)
    if shards:
        result = result * levels(stream_key, extent, shards, -0.22, 0.18)
    return jnp.clip(result, -limit, limit).astype(kind)


def heavy_noise(rng, dims, scale, limit, pieces, heavy, kind=jnp.bfloat16):
    array = scale * jax.random.normal(rng, dims, jnp.float32)
    if pieces:
        array = array * levels(rng, dims, pieces, -0.22, 0.18)
    return jnp.clip(raised(array, jax.random.fold_in(rng, 3), *heavy), -limit, limit).astype(kind)


def setup_inputs(seed: int = 0) -> dict:
    arg_keys = jax.random.split(jax.random.key(seed), 8)
    return {
        "tokens": heavy_noise(arg_keys[0], (TOKENS, DIN), 1.0, 24.0, ((0, 256),), (0, 1, 256, 6.0)),
        "out_grad": centred(arg_keys[1], (TOKENS, KV), (2.12 * DEVICES ** 0.5 / TOK_DEV ** 0.5), 8.9375, ((0, 256),)),
        "next_tokens": centred(arg_keys[2], (TOKENS, DIN), 1.0, 6.0, ((0, 256),)),
        "overflow": draw_overflow(jax.random.fold_in(arg_keys[7], 71), 0),
        "master": centred(arg_keys[4], (DIN, KV), DIN ** -0.5, 0.09375, ((0, 256),), jnp.float32),
        "first_moment": centred(arg_keys[5], (DIN, KV), 2.0, 12.0, ((0, 256),), jnp.float32),
        "second_moment": jnp.clip(jnp.exp(math.log(16.0) - 2.7725887 * jax.random.uniform(arg_keys[6], (DIN, KV), jnp.float32) ** levels(arg_keys[6], (DIN, KV), ((0, 256),), -0.2, 0.2)), 1.0, 16.0),
    }


def reference(tokens, out_grad, next_tokens, overflow, master, first_moment, second_moment):
    kept_dev = 1 - overflow
    count = jnp.sum(kept_dev).astype(jnp.float32)
    kept = jnp.repeat(kept_dev, TOK_DEV).astype(jnp.bfloat16)
    masked = tokens * kept[:, None]
    grad = jnp.dot(masked.T, out_grad, preferred_element_type=jnp.float32) / count
    new_first = 0.9 * first_moment + 0.1 * grad
    new_second = 0.95 * second_moment + 0.05 * grad * grad
    update = new_first / (1.0 - 0.9 ** STEP) / (jnp.sqrt(new_second / (1.0 - 0.95 ** STEP)) + 1e-08)
    new_master = master - 0.001 * (update + 0.1 * master)
    weights = new_master.astype(jnp.bfloat16)
    secondary = weights.reshape(N_NODE, NODE_ROWS, KV)
    next_projection = jnp.dot(next_tokens, weights, preferred_element_type=jnp.float32).astype(jnp.bfloat16)
    return (new_master, new_first, new_second, secondary, next_projection)
```

```python
import functools

import jax
import jax.numpy as jnp
from jax import lax
from jax.experimental import pallas as pl
from jax.experimental.pallas import tpu as pltpu
from jax.sharding import PartitionSpec as P

STEP = 10
MESH = pl.DeviceIdType.MESH
NH, NY, NX, NL, NC = 2, 4, 4, 4, 2
NZ = NH * NL
F32, BF16 = jnp.float32, jnp.bfloat16


def kernel(
    ov, tok_hbm, og_hbm, nxt_hbm, master, first, second,
    o_master, o_first, o_second, o_sec, o_proj,
    tok, og, nxt, own, sib_out, sib_in, s1,
    r1x, r1y, r1z, s2x, s2y, s2z, r2x, r2y, r2z, s3a, s3z, r3a, r3z,
    cnt, cnt_in, w, acc,
    in_sem, tok_sem, out_sem, sib_send, sib_recv, cnt_send, cnt_recv,
    p1_send, p1x_recv, p1y_recv, p1z_recv,
    p2_send, p2x_recv, p2y_recv, p2z_recv, p3_send, p3a_recv, p3z_recv,
    a3_send, a3a_recv, a3z_recv, a2_send, a2x_recv, a2y_recv, a2z_recv,
    a1_send, a1x_recv, a1y_recv, a1z_recv, f_send, fx_recv, fy_recv, fz_recv,
):
    rows, kv = master.shape
    ca, cb = r1x.shape[-1], r1x.shape[-1] + r1y.shape[-1]
    colx, coly, colz, colxy = pl.ds(0, ca), pl.ds(ca, cb - ca), pl.ds(cb, kv - cb), pl.ds(0, cb)
    node, loc = lax.axis_index("node"), lax.axis_index("local")
    x, y, h = lax.rem(node, NX), lax.rem(lax.div(node, NX), NY), lax.div(node, NX * NY)
    c, l = lax.rem(loc, NC), lax.div(loc, NC)

    def dev(hh=h, yy=y, xx=x, ll=l, cc=c):
        return ((hh * NY + yy) * NX + xx, ll * NC + cc)

    def xs(d):
        return lax.rem(x + d, NX)

    def ys(d):
        return lax.rem(y + d, NY)

    def hs(e):
        return lax.rem(h + e, NH)

    def ls(f):
        return lax.rem(l + f, NL)

    xd, yd = range(1, NX), range(1, NY)
    zd = [(e, f) for e in range(NH) for f in range(NL)][1:]
    sib = dev(cc=1 - c)

    def remote(src, dst, send, recv, to):
        return pltpu.make_async_remote_copy(
            src_ref=src, dst_ref=dst, send_sem=send, recv_sem=recv, device_id=to, device_id_type=MESH
        )

    def wait_recv(ref, sem):
        remote(ref, ref, sem, sem, sib).wait_recv()

    def wait_send(ref, sem):
        remote(ref, ref, sem, sem, sib).wait_send()

    og_copy = pltpu.make_async_copy(og_hbm, og, in_sem.at[0])
    nxt_copy = pltpu.make_async_copy(nxt_hbm, nxt, in_sem.at[1])
    og_copy.start()
    width = NX * NL * NC * rows
    steps = NH * NY

    def place(it):
        e, d = lax.rem(it, NH), lax.rem(lax.div(it, NH) + 1, NY)
        return e, d, hs(e), ys(d)

    def tok_copy(it):
        _, _, hh, yy = place(it)
        cols = pl.ds(pl.multiple_of((hh * NY + yy) * width, width), width)
        return pltpu.make_async_copy(tok_hbm.at[:, cols], tok.at[it], tok_sem.at[it])

    @pl.loop(0, steps)
    def _(it):
        tok_copy(it).start()

    nxt_copy.start()
    peers = [sib]
    peers += [dev(xx=xs(d)) for d in xd] + [dev(yy=ys(d)) for d in yd]
    peers += [dev(hh=hs(e), ll=ls(f)) for e, f in zd]
    barrier = pltpu.get_barrier_semaphore()
    for to in peers:
        pl.semaphore_signal(barrier, inc=1, device_id=to, device_id_type=MESH)
    kept = (1 - ov[0]).astype(F32)
    cnt[0] = jnp.full(cnt.shape[1:], kept, F32)
    og_copy.wait()
    og[...] = og[...] * kept.astype(BF16)
    pl.semaphore_wait(barrier, len(peers))
    remote(cnt.at[0], cnt_in.at[0], cnt_send.at[0], cnt_recv.at[0], sib).start()

    def exchange_first(it):
        e, d, hh, yy = place(it)
        wait_recv(sib_in.at[hh, yy], sib_recv.at[it])
        s1[hh, yy] = (own[hh, yy] + sib_in[hh, yy].astype(F32)).astype(BF16)
        for k in xd:
            remote(
                s1.at[hh, yy, xs(k), :, :, colx], r1x.at[k - 1, hh, yy],
                p1_send.at[0], p1x_recv.at[k - 1], dev(xx=xs(k)),
            ).start()

        @pl.when(d > 0)
        def _():
            remote(
                s1.at[hh, yy, :, :, :, coly], r1y.at[d - 1, hh],
                p1_send.at[1], p1y_recv.at[d - 1], dev(yy=yy),
            ).start()

        def send_z(f):
            ll = ls(f)
            slot = e * NL + f - 1
            remote(
                s1.at[hh, yy, :, ll, :, colz], r1z.at[slot, yy],
                p1_send.at[2], p1z_recv.at[slot], dev(hh=hh, ll=ll),
            ).start()

        for f in range(1, NL):
            send_z(f)

        @pl.when(e > 0)
        def _():
            send_z(0)

    @pl.loop(0, steps)
    def _(it):
        _, _, hh, yy = place(it)
        tok_copy(it).wait()
        part = lax.dot_general(tok[it], og[...], (((0,), (0,)), ((), ())), preferred_element_type=F32)
        part = part.reshape(NX, NL, NC, rows, kv)
        even, odd = part[:, :, 0], part[:, :, 1]
        own[hh, yy] = jnp.where(c == 0, even, odd)
        sib_out[hh, yy] = jnp.where(c == 0, odd, even).astype(BF16)
        remote(sib_out.at[hh, yy], sib_in.at[hh, yy], sib_send.at[0], sib_recv.at[it], sib).start()

        @pl.when(it > 0)
        def _():
            exchange_first(it - 1)

    exchange_first(jnp.int32(steps - 1))

    wait_recv(cnt_in.at[0], cnt_recv.at[0])
    cnt[1] = cnt[0] + cnt_in[0]
    for k in xd:
        remote(cnt.at[1], cnt_in.at[k], cnt_send.at[1], cnt_recv.at[k], dev(xx=xs(k))).start()

    for k in xd:
        wait_recv(r1x.at[k - 1], p1x_recv.at[k - 1])

    @pl.loop(0, NH * NY)
    def _(i):
        hh, yy = lax.div(i, NY), lax.rem(i, NY)
        total = s1[hh, yy, x, :, :, colx].astype(F32)
        for k in xd:
            total += r1x[k - 1, hh, yy].astype(F32)
        s2x[hh, yy] = total.astype(BF16)

    for k in yd:
        remote(s2x.at[:, ys(k)], r2x.at[k - 1], p2_send.at[0], p2x_recv.at[k - 1], dev(yy=ys(k))).start()

    for k in yd:
        wait_recv(r1y.at[k - 1], p1y_recv.at[k - 1])

    @pl.loop(0, NH * NX)
    def _(i):
        hh, xx = lax.div(i, NX), lax.rem(i, NX)
        total = s1[hh, y, xx, :, :, coly].astype(F32)
        for k in yd:
            total += r1y[k - 1, hh, xx].astype(F32)
        s2y[hh, xx] = total.astype(BF16)

    for k in xd:
        remote(s2y.at[:, xs(k)], r2y.at[k - 1], p2_send.at[1], p2y_recv.at[k - 1], dev(xx=xs(k))).start()

    for k in range(1, NZ):
        wait_recv(r1z.at[k - 1], p1z_recv.at[k - 1])

    @pl.loop(0, NY)
    def _(yy):
        total = s1[h, yy, :, l, :, colz].astype(F32)
        for k in range(1, NZ):
            total += r1z[k - 1, yy].astype(F32)
        s2z[yy] = total.astype(BF16)

    for k in xd:
        remote(s2z.at[:, xs(k)], r2z.at[k - 1], p2_send.at[2], p2z_recv.at[k - 1], dev(xx=xs(k))).start()

    for k in xd:
        wait_recv(cnt_in.at[k], cnt_recv.at[k])
    cnt[2] = cnt[1] + cnt_in[1] + cnt_in[2] + cnt_in[3]
    for k in yd:
        remote(cnt.at[2], cnt_in.at[NX - 1 + k], cnt_send.at[2], cnt_recv.at[NX - 1 + k], dev(yy=ys(k))).start()

    for k in yd:
        wait_recv(r2x.at[k - 1], p2x_recv.at[k - 1])
    total = s2x[:, y].astype(F32)
    for k in yd:
        total += r2x[k - 1].astype(F32)
    s3a[:, :, :, colx] = total.astype(BF16)
    for k in xd:
        wait_recv(r2y.at[k - 1], p2y_recv.at[k - 1])
    total = s2y[:, x].astype(F32)
    for k in xd:
        total += r2y[k - 1].astype(F32)
    s3a[:, :, :, coly] = total.astype(BF16)
    for e, f in zd:
        slot = e * NL + f - 1
        remote(
            s3a.at[hs(e), ls(f)], r3a.at[slot], p3_send.at[0], p3a_recv.at[slot], dev(hh=hs(e), ll=ls(f))
        ).start()
    for k in xd:
        wait_recv(r2z.at[k - 1], p2z_recv.at[k - 1])
    total = s2z[:, x].astype(F32)
    for k in xd:
        total += r2z[k - 1].astype(F32)
    s3z[...] = total.astype(BF16)
    for k in yd:
        remote(s3z.at[ys(k)], r3z.at[k - 1], p3_send.at[1], p3z_recv.at[k - 1], dev(yy=ys(k))).start()

    base = NX + NY - 1
    for k in yd:
        wait_recv(cnt_in.at[NX - 1 + k], cnt_recv.at[NX - 1 + k])
    cnt[3] = cnt[2] + cnt_in[NX] + cnt_in[NX + 1] + cnt_in[NX + 2]
    for e, f in zd:
        slot = base + e * NL + f - 1
        remote(cnt.at[3], cnt_in.at[slot], cnt_send.at[3], cnt_recv.at[slot], dev(hh=hs(e), ll=ls(f))).start()

    for k in range(1, NZ):
        wait_recv(r3a.at[k - 1], p3a_recv.at[k - 1])
    sum_a = s3a[h, l].astype(F32)
    for k in range(1, NZ):
        sum_a += r3a[k - 1].astype(F32)
    for k in yd:
        wait_recv(r3z.at[k - 1], p3z_recv.at[k - 1])
    sum_z = s3z[y].astype(F32)
    for k in yd:
        sum_z += r3z[k - 1].astype(F32)
    for k in range(1, NZ):
        wait_recv(cnt_in.at[base + k - 1], cnt_recv.at[base + k - 1])
    count = cnt[3]
    for k in range(1, NZ):
        count += cnt_in[base + k - 1]
    count = count[0:1, 0:1]

    def adam(cols, summed):
        grad = summed / count
        new_first = 0.9 * first[:, cols] + 0.1 * grad
        new_second = 0.95 * second[:, cols] + 0.05 * grad * grad
        update = new_first / (1.0 - 0.9**STEP) / (jnp.sqrt(new_second / (1.0 - 0.95**STEP)) + 1e-08)
        new_master = master[:, cols] - 0.001 * (update + 0.1 * master[:, cols])
        o_first[:, cols] = new_first
        o_second[:, cols] = new_second
        o_master[:, cols] = new_master
        w[h, y, x, l, c, :, cols] = new_master.astype(BF16)

    adam(colxy, sum_a)
    adam(colz, sum_z)

    def gather(ref, send, recv, to):
        remote(ref, ref, send, recv, to).start()

    for e, f in zd:
        gather(w.at[h, y, x, l, c, :, colxy], a3_send.at[0], a3a_recv.at[e * NL + f - 1], dev(hh=hs(e), ll=ls(f)))
    for k in yd:
        gather(w.at[h, y, x, l, c, :, colz], a3_send.at[1], a3z_recv.at[k - 1], dev(yy=ys(k)))
    for k in range(1, NZ):
        wait_recv(r3a.at[k - 1], a3a_recv.at[k - 1])
    for k in yd:
        gather(w.at[:, y, x, :, c, :, colx], a2_send.at[0], a2x_recv.at[k - 1], dev(yy=ys(k)))
    for k in xd:
        gather(w.at[:, y, x, :, c, :, coly], a2_send.at[1], a2y_recv.at[k - 1], dev(xx=xs(k)))
    for k in yd:
        wait_recv(r3z.at[k - 1], a3z_recv.at[k - 1])
    for k in xd:
        gather(w.at[h, :, x, l, c, :, colz], a2_send.at[2], a2z_recv.at[k - 1], dev(xx=xs(k)))

    for k in yd:
        wait_recv(r2x.at[k - 1], a2x_recv.at[k - 1])
    for k in xd:
        gather(w.at[:, :, x, :, c, :, colx], a1_send.at[0], a1x_recv.at[k - 1], dev(xx=xs(k)))
    for k in xd:
        wait_recv(r2y.at[k - 1], a2y_recv.at[k - 1])
    for k in yd:
        gather(w.at[:, y, :, :, c, :, coly], a1_send.at[1], a1y_recv.at[k - 1], dev(yy=ys(k)))
    for k in xd:
        wait_recv(r2z.at[k - 1], a2z_recv.at[k - 1])
    for e, f in zd:
        gather(w.at[h, :, :, l, c, :, colz], a1_send.at[2], a1z_recv.at[e * NL + f - 1], dev(hh=hs(e), ll=ls(f)))

    gather(w.at[:, :, x, :, c, :, colx], f_send.at[0], fx_recv.at[0], sib)
    gather(w.at[:, y, :, :, c, :, coly], f_send.at[1], fy_recv.at[0], sib)
    gather(w.at[h, :, :, l, c, :, colz], f_send.at[2], fz_recv.at[0], sib)
    for k in xd:
        wait_recv(r1x.at[k - 1], a1x_recv.at[k - 1])
        gather(w.at[:, :, xs(NX - k), :, c, :, colx], f_send.at[0], fx_recv.at[k], sib)
    for k in yd:
        wait_recv(r1y.at[k - 1], a1y_recv.at[k - 1])
        gather(w.at[:, ys(NY - k), :, :, c, :, coly], f_send.at[1], fy_recv.at[k], sib)
    for e, f in zd:
        slot = e * NL + f - 1
        wait_recv(r1z.at[slot], a1z_recv.at[slot])
        gather(w.at[hs(NH - e), :, :, ls(NL - f), c, :, colz], f_send.at[2], fz_recv.at[slot + 1], sib)

    sec_copy = pltpu.make_async_copy(w.at[:, :, :, l, c], o_sec, out_sem.at[0])
    sec_copy.start()

    nxt_copy.wait()
    for k in range(NX):
        wait_recv(r1x.at[0], fx_recv.at[k])
    for k in range(NY):
        wait_recv(r1y.at[0], fy_recv.at[k])
    for k in range(NZ):
        wait_recv(r1z.at[0], fz_recv.at[k])

    acc[...] = jnp.zeros_like(acc)

    @pl.loop(0, steps)
    def _(i):
        hh, yy = lax.div(i, NY), lax.rem(i, NY)
        cols = pl.ds(pl.multiple_of(i * width, width), width)
        acc[...] += jnp.dot(nxt[:, cols], w[hh, yy].reshape(width, kv), preferred_element_type=F32)

    o_proj[...] = acc[...].astype(BF16)
    sec_copy.wait()

    wait_send(sib_out, sib_send.at[0])
    wait_send(cnt.at[0], cnt_send.at[0])
    wait_send(cnt_in.at[pl.ds(0, NX - 1)], cnt_send.at[1])
    wait_send(cnt_in.at[pl.ds(0, NY - 1)], cnt_send.at[2])
    wait_send(cnt_in.at[pl.ds(0, NZ - 1)], cnt_send.at[3])
    for i, ref in enumerate((r1x, r1y, r1z)):
        wait_send(ref, p1_send.at[i])
        wait_send(ref, a1_send.at[i])
    for i, ref in enumerate((r2x, r2y, r2z)):
        wait_send(ref, p2_send.at[i])
        wait_send(ref, a2_send.at[i])
    for i, ref in enumerate((r3a, r3z)):
        wait_send(ref, p3_send.at[i])
        wait_send(ref, a3_send.at[i])
    for i, cols in enumerate((colx, coly, colz)):
        wait_send(w.at[:, :, :, :, c, :, cols], f_send.at[i])


def body(tokens, out_grad, next_tokens, overflow, master, first_moment, second_moment):
    toks, din = tokens.shape
    rows, kv = master.shape
    ca, cb = 3 * kv // 8, 6 * kv // 8
    cx, cy, cz = ca, cb - ca, kv - cb
    width = NX * NL * NC * rows
    vmem, anym = pl.BlockSpec(memory_space=pltpu.VMEM), pl.BlockSpec(memory_space=pl.ANY)
    dma = pltpu.SemaphoreType.DMA
    shapes = (
        jax.ShapeDtypeStruct((rows, kv), F32),
        jax.ShapeDtypeStruct((rows, kv), F32),
        jax.ShapeDtypeStruct((rows, kv), F32),
        jax.ShapeDtypeStruct((NH, NY, NX, rows, kv), BF16),
        jax.ShapeDtypeStruct((toks, kv), BF16),
    )
    scratch = [
        pltpu.VMEM((NH * NY, toks, width), BF16),
        pltpu.VMEM((toks, kv), BF16),
        pltpu.VMEM((toks, din), BF16),
        pltpu.VMEM((NH, NY, NX, NL, rows, kv), F32),
        pltpu.VMEM((NH, NY, NX, NL, rows, kv), BF16),
        pltpu.VMEM((NH, NY, NX, NL, rows, kv), BF16),
        pltpu.VMEM((NH, NY, NX, NL, rows, kv), BF16),
        pltpu.VMEM((NX - 1, NH, NY, NL, rows, cx), BF16),
        pltpu.VMEM((NY - 1, NH, NX, NL, rows, cy), BF16),
        pltpu.VMEM((NZ - 1, NY, NX, rows, cz), BF16),
        pltpu.VMEM((NH, NY, NL, rows, cx), BF16),
        pltpu.VMEM((NH, NX, NL, rows, cy), BF16),
        pltpu.VMEM((NY, NX, rows, cz), BF16),
        pltpu.VMEM((NY - 1, NH, NL, rows, cx), BF16),
        pltpu.VMEM((NX - 1, NH, NL, rows, cy), BF16),
        pltpu.VMEM((NX - 1, NY, rows, cz), BF16),
        pltpu.VMEM((NH, NL, rows, cx + cy), BF16),
        pltpu.VMEM((NY, rows, cz), BF16),
        pltpu.VMEM((NZ - 1, rows, cx + cy), BF16),
        pltpu.VMEM((NY - 1, rows, cz), BF16),
        pltpu.VMEM((4, 8, 128), F32),
        pltpu.VMEM((1 + NX - 1 + NY - 1 + NZ - 1, 8, 128), F32),
        pltpu.VMEM((NH, NY, NX, NL, NC, rows, kv), BF16),
        pltpu.VMEM((toks, kv), F32),
    ]
    sems = (
        [2, NH * NY, 1, 1, NH * NY, 4, NX + NY + NZ - 2]
        + [3, NX - 1, NY - 1, NZ - 1]
        + [3, NY - 1, NX - 1, NX - 1]
        + [2, NZ - 1, NY - 1]
        + [2, NZ - 1, NY - 1]
        + [3, NY - 1, NX - 1, NX - 1]
        + [3, NX - 1, NY - 1, NZ - 1]
        + [3, NX, NY, NZ]
    )
    new_master, new_first, new_second, sec, proj = pl.pallas_call(
        kernel,
        out_shape=shapes,
        in_specs=[pl.BlockSpec(memory_space=pltpu.SMEM), anym, anym, anym, vmem, vmem, vmem],
        out_specs=(vmem, vmem, vmem, anym, vmem),
        scratch_shapes=scratch + [dma((n,)) for n in sems],
        compiler_params=pltpu.CompilerParams(
            collective_id=0, has_side_effects=True, vmem_limit_bytes=58 * 2**20
        ),
        cost_estimate=pl.CostEstimate(flops=4 * toks * din * kv, bytes_accessed=12 * 2**20, transcendentals=rows * kv),
    )(overflow, tokens, out_grad, next_tokens, master, first_moment, second_moment)
    return (new_master, new_first, new_second, sec.reshape(NH * NY * NX, rows, kv), proj)


def solution(mesh):
    return jax.shard_map(
        body,
        mesh=mesh,
        in_specs=(
            P(("node", "local"), None),
            P(("node", "local"), None),
            P(("node", "local"), None),
            P(("node", "local")),
            P(("node", "local"), None),
            P(("node", "local"), None),
            P(("node", "local"), None),
        ),
        out_specs=(
            P(("node", "local"), None),
            P(("node", "local"), None),
            P(("node", "local"), None),
            P(None, "local", None),
            P(("node", "local"), None),
        ),
        check_vma=False,
    )
```

```python
import functools

import jax
import jax.numpy as jnp
from jax import lax
from jax.experimental import pallas as pl
from jax.experimental.pallas import tpu as pltpu
from jax.sharding import PartitionSpec as P

STEP = 10
MESH = pl.DeviceIdType.MESH
NH, NY, NX, NL, NC = 2, 4, 4, 4, 2
NZ = NH * NL
F32, BF16 = jnp.float32, jnp.bfloat16


def kernel(
    ov, tok_hbm, og_hbm, nxt_hbm, master, first, second,
    o_master, o_first, o_second, o_sec, o_proj,
    tok, og, nxt, own, sib_out, sib_in, s1,
    m1x, m1y, f1x, f1y, f1z, r1x, r1y, r1z, s2x, s2y, s2z, r2x, r2y, r2z, s3a, s3z, r3a, r3z,
    cnt, cnt_in, w, acc,
    in_sem, tok_sem, nxt_sem, out_sem, sib_send, sib_recv, cnt_send, cnt_recv,
    p1_send, m1x_recv, m1y_recv, p1x_recv, p1y_recv, p1z_recv,
    p2_send, p2x_recv, p2y_recv, p2z_recv, p3_send, p3a_recv, p3z_recv,
    a3_send, a3a_recv, a3z_recv, a2_send, a2x_recv, a2y_recv, a2z_recv,
    a1_send, a1x_recv, a1y_recv, a1z_recv, f_send, fx_recv, fy_recv, fz_recv,
):
    rows, kv = master.shape
    ca, cb = r1x.shape[-1], r1x.shape[-1] + r1y.shape[-1]
    colx, coly, colz, colxy = pl.ds(0, ca), pl.ds(ca, cb - ca), pl.ds(cb, kv - cb), pl.ds(0, cb)
    node, loc = lax.axis_index("node"), lax.axis_index("local")
    x, y, h = lax.rem(node, NX), lax.rem(lax.div(node, NX), NY), lax.div(node, NX * NY)
    c, l = lax.rem(loc, NC), lax.div(loc, NC)

    def dev(hh=h, yy=y, xx=x, ll=l, cc=c):
        return ((hh * NY + yy) * NX + xx, ll * NC + cc)

    def xs(d):
        return lax.rem(x + d, NX)

    def ys(d):
        return lax.rem(y + d, NY)

    def hs(e):
        return lax.rem(h + e, NH)

    def ls(f):
        return lax.rem(l + f, NL)

    def zdev(k):
        zz = lax.rem(h * NL + l + k + NZ, NZ)
        return dev(hh=lax.div(zz, NL), ll=lax.rem(zz, NL))

    def zat(k):
        zz = lax.rem(h * NL + l + k + NZ, NZ)
        return lax.div(zz, NL), lax.rem(zz, NL)

    xd, yd = range(1, NX), range(1, NY)
    zd = [(e, f) for e in range(NH) for f in range(NL)][1:]
    sib = dev(cc=1 - c)

    def remote(src, dst, send, recv, to):
        return pltpu.make_async_remote_copy(
            src_ref=src, dst_ref=dst, send_sem=send, recv_sem=recv, device_id=to, device_id_type=MESH
        )

    def wait_recv(ref, sem):
        remote(ref, ref, sem, sem, sib).wait_recv()

    def wait_send(ref, sem):
        remote(ref, ref, sem, sem, sib).wait_send()

    og_copy = pltpu.make_async_copy(og_hbm, og, in_sem.at[0])

    def nxt_copy(i):
        cols = pl.ds(pl.multiple_of(i * NL * NC * rows, NL * NC * rows), NL * NC * rows)
        return pltpu.make_async_copy(nxt_hbm.at[:, cols], nxt.at[i], nxt_sem.at[i])

    og_copy.start()
    width = NX * NL * NC * rows
    steps = NH * NY

    def place(it):
        e, d = lax.rem(it, NH), lax.rem(2 + NY - lax.div(it, NH), NY)
        return e, d, hs(e), ys(d)

    def tok_copy(it):
        _, _, hh, yy = place(it)
        cols = pl.ds(pl.multiple_of((hh * NY + yy) * width, width), width)
        return pltpu.make_async_copy(tok_hbm.at[:, cols], tok.at[it], tok_sem.at[it])

    @pl.loop(0, steps)
    def _(it):
        tok_copy(it).start()

    @pl.loop(0, NH * NY * NX)
    def _(i):
        nxt_copy(i).start()

    peers = [sib]
    peers += [dev(xx=xs(d)) for d in xd] + [dev(yy=ys(d)) for d in yd]
    peers += [dev(hh=hs(e), ll=ls(f)) for e, f in zd]
    barrier = pltpu.get_barrier_semaphore()
    for to in peers:
        pl.semaphore_signal(barrier, inc=1, device_id=to, device_id_type=MESH)
    kept = (1 - ov[0]).astype(F32)
    cnt[0] = jnp.full(cnt.shape[1:], kept, F32)
    og_copy.wait()
    og[...] = og[...] * kept.astype(BF16)
    pl.semaphore_wait(barrier, len(peers))
    remote(cnt.at[0], cnt_in.at[0], cnt_send.at[0], cnt_recv.at[0], sib).start()

    def exchange_first(it):
        e, d, hh, yy = place(it)
        wait_recv(sib_in.at[hh, yy], sib_recv.at[it])
        s1[hh, yy] = (own[hh, yy] + sib_in[hh, yy].astype(F32)).astype(BF16)
        go, back = 1 + 2 * hh, NX - 1 - 2 * hh
        remote(
            s1.at[hh, yy, xs(2), :, :, colx], m1x.at[hh, yy], p1_send.at[0], m1x_recv.at[hh, yy], dev(xx=xs(go))
        ).start()
        remote(
            s1.at[hh, yy, xs(back), :, :, colx], r1x.at[0, hh, yy], p1_send.at[1], p1x_recv.at[0], dev(xx=xs(back))
        ).start()

        @pl.when(d == 2)
        def _():
            remote(
                s1.at[hh, yy, :, :, :, coly], m1y.at[hh], p1_send.at[3], m1y_recv.at[hh], dev(yy=ys(go))
            ).start()

        @pl.when(d == back)
        def _():
            remote(
                s1.at[hh, yy, :, :, :, coly], r1y.at[0, hh], p1_send.at[4], p1y_recv.at[0], dev(yy=ys(back))
            ).start()

        @pl.loop(0, NL)
        def _(ll):
            k = lax.rem(hh * NL + ll + NZ - h * NL - l, NZ)
            up = k < 4
            odd = lax.rem(k, 2) == 1
            slot = jnp.where(odd, jnp.where((k == 1) | (k == 7), 0, 2) + jnp.where(up, 0, 1), 4)
            hop = jnp.where(odd, jnp.where(up, 1, NZ - 1), jnp.where(yy < NY // 2, 2, NZ - 2))

            @pl.when(odd | (k == 4))
            def _():
                remote(
                    s1.at[hh, yy, :, ll, :, colz], r1z.at[slot, yy], p1_send.at[6], p1z_recv.at[slot], zdev(hop)
                ).start()

    @pl.loop(0, steps)
    def _(it):
        _, _, hh, yy = place(it)
        tok_copy(it).wait()
        part = lax.dot_general(tok[it], og[...], (((0,), (0,)), ((), ())), preferred_element_type=F32)
        part = part.reshape(NX, NL, NC, rows, kv)
        even, odd = part[:, :, 0], part[:, :, 1]
        own[hh, yy] = jnp.where(c == 0, even, odd)
        sib_out[hh, yy] = jnp.where(c == 0, odd, even).astype(BF16)
        remote(sib_out.at[hh, yy], sib_in.at[hh, yy], sib_send.at[0], sib_recv.at[it], sib).start()

        @pl.when(it > 0)
        def _():
            exchange_first(it - 1)

    exchange_first(jnp.int32(steps - 1))

    wait_recv(cnt_in.at[0], cnt_recv.at[0])
    cnt[1] = cnt[0] + cnt_in[0]
    for k in xd:
        remote(cnt.at[1], cnt_in.at[k], cnt_send.at[1], cnt_recv.at[k], dev(xx=xs(k))).start()

    @pl.loop(0, steps)
    def _(it):
        _, _, hh, yy = place(it)
        go = 1 + 2 * hh
        wait_recv(m1x.at[hh, yy], m1x_recv.at[hh, yy])
        f1x[hh, yy] = (s1[hh, yy, xs(go), :, :, colx].astype(F32) + m1x[hh, yy].astype(F32)).astype(BF16)
        remote(f1x.at[hh, yy], r1x.at[1, hh, yy], p1_send.at[2], p1x_recv.at[1], dev(xx=xs(go))).start()

    @pl.loop(0, NH)
    def _(hh):
        go = 1 + 2 * hh
        wait_recv(m1y.at[hh], m1y_recv.at[hh])

        @pl.loop(0, NX)
        def _(xx):
            f1y[hh, xx] = (s1[hh, ys(go), xx, :, :, coly].astype(F32) + m1y[hh, xx].astype(F32)).astype(BF16)

        remote(f1y.at[hh], r1y.at[1, hh], p1_send.at[5], p1y_recv.at[1], dev(yy=ys(go))).start()

    for slot in (2, 3, 4):
        wait_recv(r1z.at[slot], p1z_recv.at[slot])
    for i, k in ((0, 2), (1, NZ - 2)):
        hh, ll = zat(k)
        for yy in range(NY):
            total = s1[hh, yy, :, ll, :, colz].astype(F32) + r1z[2 + i, yy].astype(F32)
            if (yy < NY // 2) == (i == 0):
                total += r1z[4, yy].astype(F32)
            f1z[i, yy] = total.astype(BF16)
        remote(f1z.at[i], r1z.at[5 + i], p1_send.at[7], p1z_recv.at[5 + i], zdev(k)).start()

    for k in range(2):
        wait_recv(r1x.at[k], p1x_recv.at[k])

    @pl.loop(0, NH * NY)
    def _(i):
        hh, yy = lax.div(i, NY), lax.rem(i, NY)
        total = s1[hh, yy, x, :, :, colx].astype(F32)
        for k in range(2):
            total += r1x[k, hh, yy].astype(F32)
        s2x[hh, yy] = total.astype(BF16)

    for k in yd:
        remote(s2x.at[:, ys(k)], r2x.at[k - 1], p2_send.at[0], p2x_recv.at[k - 1], dev(yy=ys(k))).start()

    for k in range(2):
        wait_recv(r1y.at[k], p1y_recv.at[k])

    @pl.loop(0, NH * NX)
    def _(i):
        hh, xx = lax.div(i, NX), lax.rem(i, NX)
        total = s1[hh, y, xx, :, :, coly].astype(F32)
        for k in range(2):
            total += r1y[k, hh, xx].astype(F32)
        s2y[hh, xx] = total.astype(BF16)

    for k in xd:
        remote(s2y.at[:, xs(k)], r2y.at[k - 1], p2_send.at[1], p2y_recv.at[k - 1], dev(xx=xs(k))).start()

    for k in (0, 1, 5, 6):
        wait_recv(r1z.at[k], p1z_recv.at[k])

    @pl.loop(0, NY)
    def _(yy):
        total = s1[h, yy, :, l, :, colz].astype(F32)
        for k in (0, 1, 5, 6):
            total += r1z[k, yy].astype(F32)
        s2z[yy] = total.astype(BF16)

    for k in xd:
        remote(s2z.at[:, xs(k)], r2z.at[k - 1], p2_send.at[2], p2z_recv.at[k - 1], dev(xx=xs(k))).start()

    for k in xd:
        wait_recv(cnt_in.at[k], cnt_recv.at[k])
    cnt[2] = cnt[1] + cnt_in[1] + cnt_in[2] + cnt_in[3]
    for k in yd:
        remote(cnt.at[2], cnt_in.at[NX - 1 + k], cnt_send.at[2], cnt_recv.at[NX - 1 + k], dev(yy=ys(k))).start()

    for k in yd:
        wait_recv(r2x.at[k - 1], p2x_recv.at[k - 1])
    total = s2x[:, y].astype(F32)
    for k in yd:
        total += r2x[k - 1].astype(F32)
    s3a[:, :, :, colx] = total.astype(BF16)
    for k in xd:
        wait_recv(r2y.at[k - 1], p2y_recv.at[k - 1])
    total = s2y[:, x].astype(F32)
    for k in xd:
        total += r2y[k - 1].astype(F32)
    s3a[:, :, :, coly] = total.astype(BF16)
    for e, f in zd:
        slot = e * NL + f - 1
        remote(
            s3a.at[hs(e), ls(f)], r3a.at[slot], p3_send.at[0], p3a_recv.at[slot], dev(hh=hs(e), ll=ls(f))
        ).start()
    for k in xd:
        wait_recv(r2z.at[k - 1], p2z_recv.at[k - 1])
    total = s2z[:, x].astype(F32)
    for k in xd:
        total += r2z[k - 1].astype(F32)
    s3z[...] = total.astype(BF16)
    for k in yd:
        remote(s3z.at[ys(k)], r3z.at[k - 1], p3_send.at[1], p3z_recv.at[k - 1], dev(yy=ys(k))).start()

    base = NX + NY - 1
    for k in yd:
        wait_recv(cnt_in.at[NX - 1 + k], cnt_recv.at[NX - 1 + k])
    cnt[3] = cnt[2] + cnt_in[NX] + cnt_in[NX + 1] + cnt_in[NX + 2]
    for e, f in zd:
        slot = base + e * NL + f - 1
        remote(cnt.at[3], cnt_in.at[slot], cnt_send.at[3], cnt_recv.at[slot], dev(hh=hs(e), ll=ls(f))).start()

    for k in range(1, NZ):
        wait_recv(r3a.at[k - 1], p3a_recv.at[k - 1])
    sum_a = s3a[h, l].astype(F32)
    for k in range(1, NZ):
        sum_a += r3a[k - 1].astype(F32)
    for k in yd:
        wait_recv(r3z.at[k - 1], p3z_recv.at[k - 1])
    sum_z = s3z[y].astype(F32)
    for k in yd:
        sum_z += r3z[k - 1].astype(F32)
    for k in range(1, NZ):
        wait_recv(cnt_in.at[base + k - 1], cnt_recv.at[base + k - 1])
    count = cnt[3]
    for k in range(1, NZ):
        count += cnt_in[base + k - 1]
    count = count[0:1, 0:1]

    def adam(cols, summed):
        grad = summed / count
        new_first = 0.9 * first[:, cols] + 0.1 * grad
        new_second = 0.95 * second[:, cols] + 0.05 * grad * grad
        update = new_first / (1.0 - 0.9**STEP) / (jnp.sqrt(new_second / (1.0 - 0.95**STEP)) + 1e-08)
        new_master = master[:, cols] - 0.001 * (update + 0.1 * master[:, cols])
        o_first[:, cols] = new_first
        o_second[:, cols] = new_second
        o_master[:, cols] = new_master
        w[h, y, x, l, c, :, cols] = new_master.astype(BF16)

    adam(colxy, sum_a)
    adam(colz, sum_z)

    def gather(ref, send, recv, to):
        remote(ref, ref, send, recv, to).start()

    for e, f in zd:
        gather(w.at[h, y, x, l, c, :, colxy], a3_send.at[0], a3a_recv.at[e * NL + f - 1], dev(hh=hs(e), ll=ls(f)))
    for k in yd:
        gather(w.at[h, y, x, l, c, :, colz], a3_send.at[1], a3z_recv.at[k - 1], dev(yy=ys(k)))
    for k in range(1, NZ):
        wait_recv(r3a.at[k - 1], a3a_recv.at[k - 1])
    for k in yd:
        gather(w.at[:, y, x, :, c, :, colx], a2_send.at[0], a2x_recv.at[k - 1], dev(yy=ys(k)))
    for k in xd:
        gather(w.at[:, y, x, :, c, :, coly], a2_send.at[1], a2y_recv.at[k - 1], dev(xx=xs(k)))
    for k in yd:
        wait_recv(r3z.at[k - 1], a3z_recv.at[k - 1])
    for k in xd:
        gather(w.at[h, :, x, l, c, :, colz], a2_send.at[2], a2z_recv.at[k - 1], dev(xx=xs(k)))

    def xpart(k, hh):
        return w.at[hh, :, xs(k), :, c, :, colx]

    def ypart(k, hh):
        return w.at[hh, ys(k), :, :, c, :, coly]

    def zpart(k):
        hh, ll = zat(k)
        return w.at[hh, :, :, ll, c, :, colz]

    def zhalf(k, i):
        hh, ll = zat(k)
        return w.at[hh, pl.ds(i * (NY // 2), NY // 2), :, ll, c, :, colz]

    for k in yd:
        wait_recv(r2x.at[k - 1], a2x_recv.at[k - 1])
    for i in range(2):
        gather(xpart(0, i), a1_send.at[0], a1x_recv.at[i, 0], dev(xx=xs(1 + 2 * i)))
    for i in range(2):
        gather(xpart(0, i), a1_send.at[0], a1x_recv.at[i, 1], dev(xx=xs(3 - 2 * i)))
    for k in xd:
        wait_recv(r2y.at[k - 1], a2y_recv.at[k - 1])
    for i in range(2):
        gather(ypart(0, i), a1_send.at[2], a1y_recv.at[i, 0], dev(yy=ys(1 + 2 * i)))
    for i in range(2):
        gather(ypart(0, i), a1_send.at[2], a1y_recv.at[i, 1], dev(yy=ys(3 - 2 * i)))
    for k in xd:
        wait_recv(r2z.at[k - 1], a2z_recv.at[k - 1])
    for slot, k in enumerate((2, -2, 1, -1)):
        gather(zpart(0), a1_send.at[4], a1z_recv.at[slot], zdev(k))
    for i in range(2):
        gather(xpart(0, i), f_send.at[0], fx_recv.at[0], sib)
        gather(ypart(0, i), f_send.at[1], fy_recv.at[0], sib)
    gather(zpart(0), f_send.at[2], fz_recv.at[0], sib)

    for i in range(2):
        wait_recv(m1x.at[0], a1x_recv.at[i, 0])
        gather(xpart(3 - 2 * i, i), a1_send.at[1], a1x_recv.at[i, 2], dev(xx=xs(1 + 2 * i)))
        wait_recv(m1y.at[0], a1y_recv.at[i, 0])
        gather(ypart(3 - 2 * i, i), a1_send.at[3], a1y_recv.at[i, 2], dev(yy=ys(1 + 2 * i)))
    for i, k in enumerate((-2, 2)):
        wait_recv(r1z.at[0], a1z_recv.at[i])
        gather(zhalf(k, i), a1_send.at[5], a1z_recv.at[4 + i], zdev(-k))
        gather(zpart(k), a1_send.at[5], a1z_recv.at[6 + i], zdev(-k // 2))
    for i in range(2):
        gather(xpart(3 - 2 * i, i), f_send.at[0], fx_recv.at[3 - 2 * i], sib)
        gather(ypart(3 - 2 * i, i), f_send.at[1], fy_recv.at[3 - 2 * i], sib)
    for k in (-2, 2):
        gather(zpart(k), f_send.at[2], fz_recv.at[0], sib)

    def project_x(k):
        for hh in range(NH):
            lhs = jnp.concatenate([nxt[(hh * NY + yy) * NX + xs(k)] for yy in range(NY)], axis=1)
            rhs = w[hh, :, xs(k), :, :, :, colx].reshape(NY * NL * NC * rows, ca)
            acc[:, colx] += jnp.dot(lhs, rhs, preferred_element_type=F32)

    def project_y(k):
        for hh in range(NH):
            lhs = jnp.concatenate([nxt[(hh * NY + ys(k)) * NX + xx] for xx in range(NX)], axis=1)
            rhs = w[hh, ys(k), :, :, :, :, coly].reshape(NX * NL * NC * rows, cb - ca)
            acc[:, coly] += jnp.dot(lhs, rhs, preferred_element_type=F32)

    acc[...] = jnp.zeros_like(acc)

    @pl.loop(0, NH * NY * NX)
    def _(i):
        nxt_copy(i).wait()

    wait_recv(r1x.at[0], fx_recv.at[0])
    project_x(0)
    for i in range(2):
        wait_recv(m1x.at[0], a1x_recv.at[i, 1])
        gather(xpart(1 + 2 * i, i), f_send.at[0], fx_recv.at[1 + 2 * i], sib)
        wait_recv(m1y.at[0], a1y_recv.at[i, 1])
        gather(ypart(1 + 2 * i, i), f_send.at[1], fy_recv.at[1 + 2 * i], sib)
    wait_recv(r1y.at[0], fy_recv.at[0])
    project_y(0)
    for i, k in enumerate((-1, 1)):
        wait_recv(r1z.at[0], a1z_recv.at[2 + i])
        gather(zpart(k), f_send.at[2], fz_recv.at[0], sib)
    for k in (1, 3):
        wait_recv(r1x.at[0], fx_recv.at[k])
        project_x(k)
        wait_recv(r1y.at[0], fy_recv.at[k])
        project_y(k)
    for i in range(2):
        wait_recv(m1x.at[0], a1x_recv.at[i, 2])
        gather(xpart(2, i), f_send.at[0], fx_recv.at[2], sib)
        wait_recv(m1y.at[0], a1y_recv.at[i, 2])
        gather(ypart(2, i), f_send.at[1], fy_recv.at[2], sib)
    for i, k in enumerate((-3, 3)):
        wait_recv(r1z.at[0], a1z_recv.at[6 + i])
        gather(zpart(k), f_send.at[2], fz_recv.at[0], sib)
    for i in range(2):
        wait_recv(r1z.at[0, pl.ds(0, NY // 2)], a1z_recv.at[4 + i])
        gather(zhalf(4, i), f_send.at[2], fz_recv.at[0], sib)
    sec_copy = pltpu.make_async_copy(w.at[:, :, :, l, c], o_sec, out_sem.at[0])
    sec_copy.start()
    wait_recv(r1x.at[0], fx_recv.at[2])
    project_x(2)
    o_proj[:, colx] = acc[:, colx].astype(BF16)
    wait_recv(r1y.at[0], fy_recv.at[2])
    project_y(2)
    o_proj[:, coly] = acc[:, coly].astype(BF16)
    wait_recv(w.at[:, :, :, :, 1 - c, :, colz], fz_recv.at[0])

    @pl.loop(0, steps)
    def _(i):
        hh, yy = lax.div(i, NY), lax.rem(i, NY)
        lhs = jnp.concatenate([nxt[i * NX + xx] for xx in range(NX)], axis=1)
        acc[:, colz] += jnp.dot(lhs, w[hh, yy, :, :, :, :, colz].reshape(width, kv - cb), preferred_element_type=F32)

    o_proj[:, colz] = acc[:, colz].astype(BF16)
    sec_copy.wait()

    wait_send(sib_out, sib_send.at[0])
    wait_send(cnt.at[0], cnt_send.at[0])
    wait_send(cnt_in.at[pl.ds(0, NX - 1)], cnt_send.at[1])
    wait_send(cnt_in.at[pl.ds(0, NY - 1)], cnt_send.at[2])
    wait_send(cnt_in.at[pl.ds(0, NZ - 1)], cnt_send.at[3])
    for i, ref in enumerate((m1x, r1x.at[0], r1x.at[1], m1y, r1y.at[0], r1y.at[1], r1z.at[pl.ds(0, 5)], f1z)):
        wait_send(ref, p1_send.at[i])
    for i, ref in enumerate((r1x, r1x.at[0], r1y, r1y.at[0], r1z.at[pl.ds(0, 4)], r1z.at[pl.ds(0, 3)])):
        wait_send(ref, a1_send.at[i])
    for i, ref in enumerate((r2x, r2y, r2z)):
        wait_send(ref, p2_send.at[i])
        wait_send(ref, a2_send.at[i])
    for i, ref in enumerate((r3a, r3z)):
        wait_send(ref, p3_send.at[i])
        wait_send(ref, a3_send.at[i])
    for i, cols in enumerate((colx, coly, colz)):
        wait_send(w.at[:, :, :, :, c, :, cols], f_send.at[i])


def copy_out(*refs):
    sem = refs[-1]
    copies = [pltpu.make_async_copy(refs[i], refs[5 + i], sem.at[i]) for i in range(5)]
    for copy in copies:
        copy.start()
    for copy in copies:
        copy.wait()


def body(tokens, out_grad, next_tokens, overflow, master, first_moment, second_moment):
    toks, din = tokens.shape
    rows, kv = master.shape
    ca, cb = 3 * kv // 8, 6 * kv // 8
    cx, cy, cz = ca, cb - ca, kv - cb
    width = NX * NL * NC * rows
    vmem, anym = pl.BlockSpec(memory_space=pltpu.VMEM), pl.BlockSpec(memory_space=pl.ANY)
    dma = pltpu.SemaphoreType.DMA
    shapes = (
        jax.ShapeDtypeStruct((rows, kv), F32),
        jax.ShapeDtypeStruct((rows, kv), F32),
        jax.ShapeDtypeStruct((rows, kv), F32),
        jax.ShapeDtypeStruct((NH, NY, NX, rows, kv), BF16),
        jax.ShapeDtypeStruct((toks, kv), BF16),
    )
    scratch = [
        pltpu.VMEM((NH * NY, toks, width), BF16),
        pltpu.VMEM((toks, kv), BF16),
        pltpu.VMEM((NH * NY * NX, toks, NL * NC * rows), BF16),
        pltpu.VMEM((NH, NY, NX, NL, rows, kv), F32),
        pltpu.VMEM((NH, NY, NX, NL, rows, kv), BF16),
        pltpu.VMEM((NH, NY, NX, NL, rows, kv), BF16),
        pltpu.VMEM((NH, NY, NX, NL, rows, kv), BF16),
        pltpu.VMEM((NH, NY, NL, rows, cx), BF16),
        pltpu.VMEM((NH, NX, NL, rows, cy), BF16),
        pltpu.VMEM((NH, NY, NL, rows, cx), BF16),
        pltpu.VMEM((NH, NX, NL, rows, cy), BF16),
        pltpu.VMEM((2, NY, NX, rows, cz), BF16),
        pltpu.VMEM((2, NH, NY, NL, rows, cx), BF16),
        pltpu.VMEM((2, NH, NX, NL, rows, cy), BF16),
        pltpu.VMEM((7, NY, NX, rows, cz), BF16),
        pltpu.VMEM((NH, NY, NL, rows, cx), BF16),
        pltpu.VMEM((NH, NX, NL, rows, cy), BF16),
        pltpu.VMEM((NY, NX, rows, cz), BF16),
        pltpu.VMEM((NY - 1, NH, NL, rows, cx), BF16),
        pltpu.VMEM((NX - 1, NH, NL, rows, cy), BF16),
        pltpu.VMEM((NX - 1, NY, rows, cz), BF16),
        pltpu.VMEM((NH, NL, rows, cx + cy), BF16),
        pltpu.VMEM((NY, rows, cz), BF16),
        pltpu.VMEM((NZ - 1, rows, cx + cy), BF16),
        pltpu.VMEM((NY - 1, rows, cz), BF16),
        pltpu.VMEM((4, 8, 128), F32),
        pltpu.VMEM((1 + NX - 1 + NY - 1 + NZ - 1, 8, 128), F32),
        pltpu.VMEM((NH, NY, NX, NL, NC, rows, kv), BF16),
        pltpu.VMEM((toks, kv), F32),
    ]
    sems = (
        [(1,), (NH * NY,), (NH * NY * NX,), (1,), (1,), (NH * NY,), (4,), (NX + NY + NZ - 2,)]
        + [(8,), (NH, NY), (NH,), (2,), (2,), (7,)]
        + [(3,), (NY - 1,), (NX - 1,), (NX - 1,)]
        + [(2,), (NZ - 1,), (NY - 1,)]
        + [(2,), (NZ - 1,), (NY - 1,)]
        + [(3,), (NY - 1,), (NX - 1,), (NX - 1,)]
        + [(6,), (2, 3), (2, 3), (8,)]
        + [(3,), (NX,), (NY,), (1,)]
    )
    results = pl.pallas_call(
        kernel,
        out_shape=shapes,
        in_specs=[pl.BlockSpec(memory_space=pltpu.SMEM), anym, anym, anym, vmem, vmem, vmem],
        out_specs=(vmem, vmem, vmem, anym, vmem),
        scratch_shapes=scratch + [dma(n) for n in sems],
        compiler_params=pltpu.CompilerParams(
            collective_id=0, has_side_effects=True, vmem_limit_bytes=58 * 2**20
        ),
        cost_estimate=pl.CostEstimate(flops=4 * toks * din * kv, bytes_accessed=12 * 2**20, transcendentals=rows * kv),
    )(overflow, tokens, out_grad, next_tokens, master, first_moment, second_moment)
    new_master, new_first, new_second, sec, proj = pl.pallas_call(
        copy_out,
        out_shape=shapes,
        in_specs=[anym] * 5,
        out_specs=[anym] * 5,
        scratch_shapes=[dma((5,))],
    )(*results)
    return (new_master, new_first, new_second, sec.reshape(NH * NY * NX, rows, kv), proj)


def solution(mesh):
    return jax.shard_map(
        body,
        mesh=mesh,
        in_specs=(
            P(("node", "local"), None),
            P(("node", "local"), None),
            P(("node", "local"), None),
            P(("node", "local")),
            P(("node", "local"), None),
            P(("node", "local"), None),
            P(("node", "local"), None),
        ),
        out_specs=(
            P(("node", "local"), None),
            P(("node", "local"), None),
            P(("node", "local"), None),
            P(None, "local", None),
            P(("node", "local"), None),
        ),
        check_vma=False,
    )
```

```python
import functools

import jax
import jax.numpy as jnp
from jax import lax
from jax.experimental import pallas as pl
from jax.experimental.pallas import tpu as pltpu
from jax.sharding import PartitionSpec as P

STEP = 10
MESH = pl.DeviceIdType.MESH
NH, NY, NX, NL, NC = 2, 4, 4, 4, 2
NZ = NH * NL
PARTS = (1, 1, 1, 2, 4)
F32, BF16 = jnp.float32, jnp.bfloat16


def kernel(
    ov, tok_hbm, og_hbm, nxt_hbm, master, first, second,
    o_master, o_first, o_second, o_sec, o_proj,
    tok, og, nxt, own, sib_out, sib_in, s1,
    m1x, m1y, f1x, f1y, f1z, r1x, r1y, r1z, s2x, s2y, s2z, r2x, r2y, r2z, s3a, s3z, r3a, r3z,
    cnt, cnt_in, w, acc,
    in_sem, tok_sem, nxt_sem, out_sem, sib_send, sib_recv, cnt_send, cnt_recv,
    p1_send, m1x_recv, m1y_recv, p1x_recv, p1y_recv, p1z_recv,
    p2_send, p2x_recv, p2y_recv, p2z_recv, p3_send, p3a_recv, p3z_recv,
    a3_send, a3a_recv, a3z_recv, a2_send, a2x_recv, a2y_recv, a2z_recv,
    a1_send, a1x_recv, a1y_recv, a1z_recv, f_send, fx_recv, fy_recv, fz_recv,
):
    rows, kv = master.shape
    ca, cb = r1x.shape[-1], r1x.shape[-1] + r1y.shape[-1]
    colx, coly, colz, colxy = pl.ds(0, ca), pl.ds(ca, cb - ca), pl.ds(cb, kv - cb), pl.ds(0, cb)
    node, loc = lax.axis_index("node"), lax.axis_index("local")
    x, y, h = lax.rem(node, NX), lax.rem(lax.div(node, NX), NY), lax.div(node, NX * NY)
    c, l = lax.rem(loc, NC), lax.div(loc, NC)

    def dev(hh=h, yy=y, xx=x, ll=l, cc=c):
        return ((hh * NY + yy) * NX + xx, ll * NC + cc)

    def xs(d):
        return lax.rem(x + d, NX)

    def ys(d):
        return lax.rem(y + d, NY)

    def hs(e):
        return lax.rem(h + e, NH)

    def ls(f):
        return lax.rem(l + f, NL)

    def zdev(k):
        zz = lax.rem(h * NL + l + k + NZ, NZ)
        return dev(hh=lax.div(zz, NL), ll=lax.rem(zz, NL))

    def zat(k):
        zz = lax.rem(h * NL + l + k + NZ, NZ)
        return lax.div(zz, NL), lax.rem(zz, NL)

    xd, yd = range(1, NX), range(1, NY)
    zd = [(e, f) for e in range(NH) for f in range(NL)][1:]
    sib = dev(cc=1 - c)

    def remote(src, dst, send, recv, to):
        return pltpu.make_async_remote_copy(
            src_ref=src, dst_ref=dst, send_sem=send, recv_sem=recv, device_id=to, device_id_type=MESH
        )

    def wait_recv(ref, sem):
        remote(ref, ref, sem, sem, sib).wait_recv()

    def wait_send(ref, sem):
        remote(ref, ref, sem, sem, sib).wait_send()

    pending = []

    def drain():
        for ref, sem in pending:
            wait_send(ref, sem)

    og_copy = pltpu.make_async_copy(og_hbm, og, in_sem.at[0])

    def nxt_copy(i):
        cols = pl.ds(pl.multiple_of(i * NL * NC * rows, NL * NC * rows), NL * NC * rows)
        return pltpu.make_async_copy(nxt_hbm.at[:, cols], nxt.at[i], nxt_sem.at[i])

    og_copy.start()
    width = NX * NL * NC * rows
    steps = NH * NY

    def place(it):
        e, d = lax.rem(it, NH), lax.rem(2 + NY - lax.div(it, NH), NY)
        return e, d, hs(e), ys(d)

    def tok_copy(it):
        _, _, hh, yy = place(it)
        cols = pl.ds(pl.multiple_of((hh * NY + yy) * width, width), width)
        return pltpu.make_async_copy(tok_hbm.at[:, cols], tok.at[it], tok_sem.at[it])

    @pl.loop(0, steps)
    def _(it):
        tok_copy(it).start()

    @pl.loop(0, NH * NY * NX)
    def _(i):
        nxt_copy(i).start()

    peers = [sib]
    peers += [dev(xx=xs(d)) for d in xd] + [dev(yy=ys(d)) for d in yd]
    peers += [dev(hh=hs(e), ll=ls(f)) for e, f in zd]
    barrier = pltpu.get_barrier_semaphore()
    for to in peers:
        pl.semaphore_signal(barrier, inc=1, device_id=to, device_id_type=MESH)
    kept = (1 - ov[0]).astype(F32)
    cnt[0] = jnp.full(cnt.shape[1:], kept, F32)
    og_copy.wait()
    og[...] = og[...] * kept.astype(BF16)
    pl.semaphore_wait(barrier, len(peers))
    remote(cnt.at[0], cnt_in.at[0], cnt_send.at[0], cnt_recv.at[0], sib).start()

    def exchange_first(it):
        e, d, hh, yy = place(it)
        wait_recv(sib_in.at[hh, yy], sib_recv.at[it])
        s1[hh, yy] = (own[hh, yy] + sib_in[hh, yy].astype(F32)).astype(BF16)
        go, back = 1 + 2 * hh, NX - 1 - 2 * hh
        remote(
            s1.at[hh, yy, xs(2), :, :, colx], m1x.at[hh, yy], p1_send.at[0], m1x_recv.at[hh, yy], dev(xx=xs(go))
        ).start()
        remote(
            s1.at[hh, yy, xs(back), :, :, colx], r1x.at[0, hh, yy], p1_send.at[1], p1x_recv.at[0], dev(xx=xs(back))
        ).start()

        @pl.when(d == 2)
        def _():
            remote(
                s1.at[hh, yy, :, :, :, coly], m1y.at[hh], p1_send.at[3], m1y_recv.at[hh], dev(yy=ys(go))
            ).start()

        @pl.when(d == back)
        def _():
            remote(
                s1.at[hh, yy, :, :, :, coly], r1y.at[0, hh], p1_send.at[4], p1y_recv.at[0], dev(yy=ys(back))
            ).start()

        @pl.loop(0, NL)
        def _(ll):
            k = lax.rem(hh * NL + ll + NZ - h * NL - l, NZ)
            up = k < 4
            odd = lax.rem(k, 2) == 1
            slot = jnp.where(odd, jnp.where((k == 1) | (k == 7), 0, 2) + jnp.where(up, 0, 1), 4)
            hop = jnp.where(odd, jnp.where(up, 1, NZ - 1), jnp.where(yy < NY // 2, 2, NZ - 2))

            @pl.when(odd | (k == 4))
            def _():
                remote(
                    s1.at[hh, yy, :, ll, :, colz], r1z.at[slot, yy], p1_send.at[6], p1z_recv.at[slot], zdev(hop)
                ).start()

    @pl.loop(0, steps)
    def _(it):
        _, _, hh, yy = place(it)
        tok_copy(it).wait()
        part = lax.dot_general(tok[it], og[...], (((0,), (0,)), ((), ())), preferred_element_type=F32)
        part = part.reshape(NX, NL, NC, rows, kv)
        even, odd = part[:, :, 0], part[:, :, 1]
        own[hh, yy] = jnp.where(c == 0, even, odd)
        sib_out[hh, yy] = jnp.where(c == 0, odd, even).astype(BF16)
        remote(sib_out.at[hh, yy], sib_in.at[hh, yy], sib_send.at[0], sib_recv.at[it], sib).start()

        @pl.when(it > 0)
        def _():
            exchange_first(it - 1)

    exchange_first(jnp.int32(steps - 1))

    wait_recv(cnt_in.at[0], cnt_recv.at[0])
    cnt[1] = cnt[0] + cnt_in[0]
    for k in xd:
        remote(cnt.at[1], cnt_in.at[k], cnt_send.at[1], cnt_recv.at[k], dev(xx=xs(k))).start()

    pending += [(sib_out, sib_send.at[0]), (cnt.at[0], cnt_send.at[0]), (cnt_in.at[pl.ds(0, NX - 1)], cnt_send.at[1])]
    pending += [(m1x, p1_send.at[0]), (r1x.at[0], p1_send.at[1]), (m1y, p1_send.at[3]), (r1y.at[0], p1_send.at[4])]
    pending += [(r1z.at[pl.ds(0, 5)], p1_send.at[6])]

    @pl.loop(0, steps)
    def _(it):
        _, _, hh, yy = place(it)
        go = 1 + 2 * hh
        wait_recv(m1x.at[hh, yy], m1x_recv.at[hh, yy])
        f1x[hh, yy] = (s1[hh, yy, xs(go), :, :, colx].astype(F32) + m1x[hh, yy].astype(F32)).astype(BF16)
        remote(f1x.at[hh, yy], r1x.at[1, hh, yy], p1_send.at[2], p1x_recv.at[1], dev(xx=xs(go))).start()

    @pl.loop(0, NH)
    def _(hh):
        go = 1 + 2 * hh
        wait_recv(m1y.at[hh], m1y_recv.at[hh])

        @pl.loop(0, NX)
        def _(xx):
            f1y[hh, xx] = (s1[hh, ys(go), xx, :, :, coly].astype(F32) + m1y[hh, xx].astype(F32)).astype(BF16)

        remote(f1y.at[hh], r1y.at[1, hh], p1_send.at[5], p1y_recv.at[1], dev(yy=ys(go))).start()

    for slot in (2, 3, 4):
        wait_recv(r1z.at[slot], p1z_recv.at[slot])
    for i, k in ((0, 2), (1, NZ - 2)):
        hh, ll = zat(k)
        for yy in range(NY):
            total = s1[hh, yy, :, ll, :, colz].astype(F32) + r1z[2 + i, yy].astype(F32)
            if (yy < NY // 2) == (i == 0):
                total += r1z[4, yy].astype(F32)
            f1z[i, yy] = total.astype(BF16)
        remote(f1z.at[i], r1z.at[5 + i], p1_send.at[7], p1z_recv.at[5 + i], zdev(k)).start()

    pending += [(f1x, p1_send.at[2]), (f1y, p1_send.at[5]), (f1z, p1_send.at[7])]

    for k in range(2):
        wait_recv(r1x.at[k], p1x_recv.at[k])

    @pl.loop(0, NH * NY)
    def _(i):
        hh, yy = lax.div(i, NY), lax.rem(i, NY)
        total = s1[hh, yy, x, :, :, colx].astype(F32)
        for k in range(2):
            total += r1x[k, hh, yy].astype(F32)
        s2x[hh, yy] = total.astype(BF16)

    for k in yd:
        remote(s2x.at[:, ys(k)], r2x.at[k - 1], p2_send.at[0], p2x_recv.at[k - 1], dev(yy=ys(k))).start()

    for k in range(2):
        wait_recv(r1y.at[k], p1y_recv.at[k])

    @pl.loop(0, NH * NX)
    def _(i):
        hh, xx = lax.div(i, NX), lax.rem(i, NX)
        total = s1[hh, y, xx, :, :, coly].astype(F32)
        for k in range(2):
            total += r1y[k, hh, xx].astype(F32)
        s2y[hh, xx] = total.astype(BF16)

    for k in xd:
        remote(s2y.at[:, xs(k)], r2y.at[k - 1], p2_send.at[1], p2y_recv.at[k - 1], dev(xx=xs(k))).start()

    for k in (0, 1, 5, 6):
        wait_recv(r1z.at[k], p1z_recv.at[k])

    @pl.loop(0, NY)
    def _(yy):
        total = s1[h, yy, :, l, :, colz].astype(F32)
        for k in (0, 1, 5, 6):
            total += r1z[k, yy].astype(F32)
        s2z[yy] = total.astype(BF16)

    for k in xd:
        remote(s2z.at[:, xs(k)], r2z.at[k - 1], p2_send.at[2], p2z_recv.at[k - 1], dev(xx=xs(k))).start()

    for k in xd:
        wait_recv(cnt_in.at[k], cnt_recv.at[k])
    cnt[2] = cnt[1] + cnt_in[1] + cnt_in[2] + cnt_in[3]
    for k in yd:
        remote(cnt.at[2], cnt_in.at[NX - 1 + k], cnt_send.at[2], cnt_recv.at[NX - 1 + k], dev(yy=ys(k))).start()

    pending += [(r2x, p2_send.at[0]), (r2y, p2_send.at[1]), (r2z, p2_send.at[2])]
    pending += [(cnt_in.at[pl.ds(0, NY - 1)], cnt_send.at[2])]

    for k in yd:
        wait_recv(r2x.at[k - 1], p2x_recv.at[k - 1])
    total = s2x[:, y].astype(F32)
    for k in yd:
        total += r2x[k - 1].astype(F32)
    s3a[:, :, :, colx] = total.astype(BF16)
    for k in xd:
        wait_recv(r2y.at[k - 1], p2y_recv.at[k - 1])
    total = s2y[:, x].astype(F32)
    for k in xd:
        total += r2y[k - 1].astype(F32)
    s3a[:, :, :, coly] = total.astype(BF16)
    for e, f in zd:
        slot = e * NL + f - 1
        remote(
            s3a.at[hs(e), ls(f)], r3a.at[slot], p3_send.at[0], p3a_recv.at[slot], dev(hh=hs(e), ll=ls(f))
        ).start()
    for k in xd:
        wait_recv(r2z.at[k - 1], p2z_recv.at[k - 1])
    total = s2z[:, x].astype(F32)
    for k in xd:
        total += r2z[k - 1].astype(F32)
    s3z[...] = total.astype(BF16)
    for k in yd:
        remote(s3z.at[ys(k)], r3z.at[k - 1], p3_send.at[1], p3z_recv.at[k - 1], dev(yy=ys(k))).start()

    base = NX + NY - 1
    for k in yd:
        wait_recv(cnt_in.at[NX - 1 + k], cnt_recv.at[NX - 1 + k])
    cnt[3] = cnt[2] + cnt_in[NX] + cnt_in[NX + 1] + cnt_in[NX + 2]
    for e, f in zd:
        slot = base + e * NL + f - 1
        remote(cnt.at[3], cnt_in.at[slot], cnt_send.at[3], cnt_recv.at[slot], dev(hh=hs(e), ll=ls(f))).start()

    for k in range(1, NZ):
        wait_recv(r3a.at[k - 1], p3a_recv.at[k - 1])
    sum_a = s3a[h, l].astype(F32)
    for k in range(1, NZ):
        sum_a += r3a[k - 1].astype(F32)
    for k in yd:
        wait_recv(r3z.at[k - 1], p3z_recv.at[k - 1])
    sum_z = s3z[y].astype(F32)
    for k in yd:
        sum_z += r3z[k - 1].astype(F32)
    for k in range(1, NZ):
        wait_recv(cnt_in.at[base + k - 1], cnt_recv.at[base + k - 1])
    count = cnt[3]
    for k in range(1, NZ):
        count += cnt_in[base + k - 1]
    count = count[0:1, 0:1]

    pending += [(r3a, p3_send.at[0]), (r3z, p3_send.at[1]), (cnt_in.at[pl.ds(0, NZ - 1)], cnt_send.at[3])]

    def adam(cols, summed):
        grad = summed / count
        new_first = 0.9 * first[:, cols] + 0.1 * grad
        new_second = 0.95 * second[:, cols] + 0.05 * grad * grad
        update = new_first / (1.0 - 0.9**STEP) / (jnp.sqrt(new_second / (1.0 - 0.95**STEP)) + 1e-08)
        new_master = master[:, cols] - 0.001 * (update + 0.1 * master[:, cols])
        o_first[:, cols] = new_first
        o_second[:, cols] = new_second
        o_master[:, cols] = new_master
        w[h, y, x, l, c, :, cols] = new_master.astype(BF16)

    adam(colxy, sum_a)
    adam(colz, sum_z)

    def gather(ref, send, recv, to):
        remote(ref, ref, send, recv, to).start()

    for e, f in zd:
        gather(w.at[h, y, x, l, c, :, colxy], a3_send.at[0], a3a_recv.at[e * NL + f - 1], dev(hh=hs(e), ll=ls(f)))
    for k in yd:
        gather(w.at[h, y, x, l, c, :, colz], a3_send.at[1], a3z_recv.at[k - 1], dev(yy=ys(k)))
    for k in range(1, NZ):
        wait_recv(r3a.at[k - 1], a3a_recv.at[k - 1])
    for k in yd:
        gather(w.at[:, y, x, :, c, :, colx], a2_send.at[0], a2x_recv.at[k - 1], dev(yy=ys(k)))
    for k in xd:
        gather(w.at[:, y, x, :, c, :, coly], a2_send.at[1], a2y_recv.at[k - 1], dev(xx=xs(k)))
    for k in yd:
        wait_recv(r3z.at[k - 1], a3z_recv.at[k - 1])
    for k in xd:
        gather(w.at[h, :, x, l, c, :, colz], a2_send.at[2], a2z_recv.at[k - 1], dev(xx=xs(k)))

    def xpart(k, hh):
        return w.at[hh, :, xs(k), :, c, :, colx]

    def ypart(k, hh):
        return w.at[hh, ys(k), :, :, c, :, coly]

    def zpart(k):
        hh, ll = zat(k)
        return w.at[hh, :, :, ll, c, :, colz]

    def zhalf(k, i):
        hh, ll = zat(k)
        return w.at[hh, pl.ds(i * (NY // 2), NY // 2), :, ll, c, :, colz]

    pending += [(r3a, a3_send.at[0]), (r3z, a3_send.at[1])]
    pending += [(r2x, a2_send.at[0]), (r2y, a2_send.at[1]), (r2z, a2_send.at[2])]

    for k in yd:
        wait_recv(r2x.at[k - 1], a2x_recv.at[k - 1])
    for i in range(2):
        gather(xpart(0, i), a1_send.at[0], a1x_recv.at[i, 0], dev(xx=xs(1 + 2 * i)))
    for i in range(2):
        gather(xpart(0, i), a1_send.at[0], a1x_recv.at[i, 1], dev(xx=xs(3 - 2 * i)))
    for k in xd:
        wait_recv(r2y.at[k - 1], a2y_recv.at[k - 1])
    for i in range(2):
        gather(ypart(0, i), a1_send.at[2], a1y_recv.at[i, 0], dev(yy=ys(1 + 2 * i)))
    for i in range(2):
        gather(ypart(0, i), a1_send.at[2], a1y_recv.at[i, 1], dev(yy=ys(3 - 2 * i)))
    for k in xd:
        wait_recv(r2z.at[k - 1], a2z_recv.at[k - 1])
    for slot, k in enumerate((2, -2, 1, -1)):
        gather(zpart(0), a1_send.at[4], a1z_recv.at[slot], zdev(k))
    for i in range(2):
        gather(xpart(0, i), f_send.at[0], fx_recv.at[0], sib)
        gather(ypart(0, i), f_send.at[1], fy_recv.at[0], sib)
    gather(zpart(0), f_send.at[2], fz_recv.at[0], sib)

    for i in range(2):
        wait_recv(m1x.at[0], a1x_recv.at[i, 0])
        gather(xpart(3 - 2 * i, i), a1_send.at[1], a1x_recv.at[i, 2], dev(xx=xs(1 + 2 * i)))
        wait_recv(m1y.at[0], a1y_recv.at[i, 0])
        gather(ypart(3 - 2 * i, i), a1_send.at[3], a1y_recv.at[i, 2], dev(yy=ys(1 + 2 * i)))
    for i, k in enumerate((-2, 2)):
        wait_recv(r1z.at[0], a1z_recv.at[i])
        gather(zhalf(k, i), a1_send.at[5], a1z_recv.at[4 + i], zdev(-k))
        gather(zpart(k), a1_send.at[5], a1z_recv.at[6 + i], zdev(-k // 2))
    for i in range(2):
        gather(xpart(3 - 2 * i, i), f_send.at[0], fx_recv.at[3 - 2 * i], sib)
        gather(ypart(3 - 2 * i, i), f_send.at[1], fy_recv.at[3 - 2 * i], sib)
    for k in (-2, 2):
        gather(zpart(k), f_send.at[2], fz_recv.at[0], sib)

    pending += [(r1x, a1_send.at[0]), (r1x.at[0], a1_send.at[1]), (r1y, a1_send.at[2]), (r1y.at[0], a1_send.at[3])]
    pending += [(r1z.at[pl.ds(0, 4)], a1_send.at[4]), (r1z.at[pl.ds(0, 3)], a1_send.at[5])]
    pending += [(w.at[:, :, :, :, c, :, cols], f_send.at[i]) for i, cols in enumerate((colx, coly, colz))]

    def project_x(k):
        for hh in range(NH):
            lhs = jnp.concatenate([nxt[(hh * NY + yy) * NX + xs(k)] for yy in range(NY)], axis=1)
            rhs = w[hh, :, xs(k), :, :, :, colx].reshape(NY * NL * NC * rows, ca)
            acc[:, colx] += jnp.dot(lhs, rhs, preferred_element_type=F32)

    def project_y(k):
        for hh in range(NH):
            lhs = jnp.concatenate([nxt[(hh * NY + ys(k)) * NX + xx] for xx in range(NX)], axis=1)
            rhs = w[hh, ys(k), :, :, :, :, coly].reshape(NX * NL * NC * rows, cb - ca)
            acc[:, coly] += jnp.dot(lhs, rhs, preferred_element_type=F32)

    acc[...] = jnp.zeros_like(acc)

    @pl.loop(0, NH * NY * NX)
    def _(i):
        nxt_copy(i).wait()

    wait_recv(r1x.at[0], fx_recv.at[0])
    project_x(0)
    for i in range(2):
        wait_recv(m1x.at[0], a1x_recv.at[i, 1])
        gather(xpart(1 + 2 * i, i), f_send.at[0], fx_recv.at[1 + 2 * i], sib)
        wait_recv(m1y.at[0], a1y_recv.at[i, 1])
        gather(ypart(1 + 2 * i, i), f_send.at[1], fy_recv.at[1 + 2 * i], sib)
    wait_recv(r1y.at[0], fy_recv.at[0])
    project_y(0)
    for i, k in enumerate((-1, 1)):
        wait_recv(r1z.at[0], a1z_recv.at[2 + i])
        gather(zpart(k), f_send.at[2], fz_recv.at[0], sib)
    for k in (1, 3):
        wait_recv(r1x.at[0], fx_recv.at[k])
        project_x(k)
        wait_recv(r1y.at[0], fy_recv.at[k])
        project_y(k)
    for i in range(2):
        wait_recv(m1x.at[0], a1x_recv.at[i, 2])
        gather(xpart(2, i), f_send.at[0], fx_recv.at[2], sib)
        wait_recv(m1y.at[0], a1y_recv.at[i, 2])
        gather(ypart(2, i), f_send.at[1], fy_recv.at[2], sib)
    for i, k in enumerate((-3, 3)):
        wait_recv(r1z.at[0], a1z_recv.at[6 + i])
        gather(zpart(k), f_send.at[2], fz_recv.at[0], sib)
    for i in range(2):
        wait_recv(r1z.at[0, pl.ds(0, NY // 2)], a1z_recv.at[4 + i])
        gather(zhalf(4, i), f_send.at[2], fz_recv.at[0], sib)
    sec_copy = pltpu.make_async_copy(w.at[:, :, :, l, c], o_sec, out_sem.at[0])
    sec_copy.start()
    wait_recv(r1x.at[0], fx_recv.at[2])
    project_x(2)
    o_proj[:, colx] = acc[:, colx].astype(BF16)
    wait_recv(r1y.at[0], fy_recv.at[2])
    project_y(2)
    o_proj[:, coly] = acc[:, coly].astype(BF16)
    wait_recv(w.at[:, :, :, :, 1 - c, :, colz], fz_recv.at[0])

    @pl.loop(0, steps)
    def _(i):
        hh, yy = lax.div(i, NY), lax.rem(i, NY)
        lhs = jnp.concatenate([nxt[i * NX + xx] for xx in range(NX)], axis=1)
        acc[:, colz] += jnp.dot(lhs, w[hh, yy, :, :, :, :, colz].reshape(width, kv - cb), preferred_element_type=F32)

    o_proj[:, colz] = acc[:, colz].astype(BF16)
    sec_copy.wait()

    drain()


def copy_out(*refs):
    src, dst, held, sem_in, sem_out = refs[:5], refs[5:10], refs[10:15], refs[15], refs[16]
    parts = []
    for i in range(5):
        rows = src[i].shape[0]
        n = PARTS[i]
        parts += [(i, pl.ds(j * rows // n, rows // n)) for j in range(n)]
    reads = [pltpu.make_async_copy(src[i].at[r], held[i].at[r], sem_in.at[j]) for j, (i, r) in enumerate(parts)]
    writes = [pltpu.make_async_copy(held[i].at[r], dst[i].at[r], sem_out.at[j]) for j, (i, r) in enumerate(parts)]
    for copy in reads:
        copy.start()
    for read, write in zip(reads, writes):
        read.wait()
        write.start()
    for copy in writes:
        copy.wait()


def body(tokens, out_grad, next_tokens, overflow, master, first_moment, second_moment):
    toks, din = tokens.shape
    rows, kv = master.shape
    ca, cb = 3 * kv // 8, 6 * kv // 8
    cx, cy, cz = ca, cb - ca, kv - cb
    width = NX * NL * NC * rows
    vmem, anym = pl.BlockSpec(memory_space=pltpu.VMEM), pl.BlockSpec(memory_space=pl.ANY)
    dma = pltpu.SemaphoreType.DMA
    shapes = (
        jax.ShapeDtypeStruct((rows, kv), F32),
        jax.ShapeDtypeStruct((rows, kv), F32),
        jax.ShapeDtypeStruct((rows, kv), F32),
        jax.ShapeDtypeStruct((NH, NY, NX, rows, kv), BF16),
        jax.ShapeDtypeStruct((toks, kv), BF16),
    )
    scratch = [
        pltpu.VMEM((NH * NY, toks, width), BF16),
        pltpu.VMEM((toks, kv), BF16),
        pltpu.VMEM((NH * NY * NX, toks, NL * NC * rows), BF16),
        pltpu.VMEM((NH, NY, NX, NL, rows, kv), F32),
        pltpu.VMEM((NH, NY, NX, NL, rows, kv), BF16),
        pltpu.VMEM((NH, NY, NX, NL, rows, kv), BF16),
        pltpu.VMEM((NH, NY, NX, NL, rows, kv), BF16),
        pltpu.VMEM((NH, NY, NL, rows, cx), BF16),
        pltpu.VMEM((NH, NX, NL, rows, cy), BF16),
        pltpu.VMEM((NH, NY, NL, rows, cx), BF16),
        pltpu.VMEM((NH, NX, NL, rows, cy), BF16),
        pltpu.VMEM((2, NY, NX, rows, cz), BF16),
        pltpu.VMEM((2, NH, NY, NL, rows, cx), BF16),
        pltpu.VMEM((2, NH, NX, NL, rows, cy), BF16),
        pltpu.VMEM((7, NY, NX, rows, cz), BF16),
        pltpu.VMEM((NH, NY, NL, rows, cx), BF16),
        pltpu.VMEM((NH, NX, NL, rows, cy), BF16),
        pltpu.VMEM((NY, NX, rows, cz), BF16),
        pltpu.VMEM((NY - 1, NH, NL, rows, cx), BF16),
        pltpu.VMEM((NX - 1, NH, NL, rows, cy), BF16),
        pltpu.VMEM((NX - 1, NY, rows, cz), BF16),
        pltpu.VMEM((NH, NL, rows, cx + cy), BF16),
        pltpu.VMEM((NY, rows, cz), BF16),
        pltpu.VMEM((NZ - 1, rows, cx + cy), BF16),
        pltpu.VMEM((NY - 1, rows, cz), BF16),
        pltpu.VMEM((4, 8, 128), F32),
        pltpu.VMEM((1 + NX - 1 + NY - 1 + NZ - 1, 8, 128), F32),
        pltpu.VMEM((NH, NY, NX, NL, NC, rows, kv), BF16),
        pltpu.VMEM((toks, kv), F32),
    ]
    sems = (
        [(1,), (NH * NY,), (NH * NY * NX,), (1,), (1,), (NH * NY,), (4,), (NX + NY + NZ - 2,)]
        + [(8,), (NH, NY), (NH,), (2,), (2,), (7,)]
        + [(3,), (NY - 1,), (NX - 1,), (NX - 1,)]
        + [(2,), (NZ - 1,), (NY - 1,)]
        + [(2,), (NZ - 1,), (NY - 1,)]
        + [(3,), (NY - 1,), (NX - 1,), (NX - 1,)]
        + [(6,), (2, 3), (2, 3), (8,)]
        + [(3,), (NX,), (NY,), (1,)]
    )
    results = pl.pallas_call(
        kernel,
        out_shape=shapes,
        in_specs=[pl.BlockSpec(memory_space=pltpu.SMEM), anym, anym, anym, vmem, vmem, vmem],
        out_specs=(vmem, vmem, vmem, anym, vmem),
        scratch_shapes=scratch + [dma(n) for n in sems],
        compiler_params=pltpu.CompilerParams(
            collective_id=0, has_side_effects=True, vmem_limit_bytes=58 * 2**20
        ),
        cost_estimate=pl.CostEstimate(flops=4 * toks * din * kv, bytes_accessed=12 * 2**20, transcendentals=rows * kv),
    )(overflow, tokens, out_grad, next_tokens, master, first_moment, second_moment)
    new_master, new_first, new_second, sec, proj = pl.pallas_call(
        copy_out,
        out_shape=shapes,
        in_specs=[anym] * 5,
        out_specs=[anym] * 5,
        scratch_shapes=[pltpu.VMEM(shape.shape, shape.dtype) for shape in shapes] + [dma((sum(PARTS),))] * 2,
        compiler_params=pltpu.CompilerParams(vmem_limit_bytes=58 * 2**20),
    )(*results)
    return (new_master, new_first, new_second, sec.reshape(NH * NY * NX, rows, kv), proj)


def solution(mesh):
    return jax.shard_map(
        body,
        mesh=mesh,
        in_specs=(
            P(("node", "local"), None),
            P(("node", "local"), None),
            P(("node", "local"), None),
            P(("node", "local")),
            P(("node", "local"), None),
            P(("node", "local"), None),
            P(("node", "local"), None),
        ),
        out_specs=(
            P(("node", "local"), None),
            P(("node", "local"), None),
            P(("node", "local"), None),
            P(None, "local", None),
            P(("node", "local"), None),
        ),
        check_vma=False,
    )
```

```python
import functools

import jax
import jax.numpy as jnp
from jax import lax
from jax.experimental import pallas as pl
from jax.experimental.pallas import tpu as pltpu
from jax.sharding import PartitionSpec as P

STEP = 10
MESH = pl.DeviceIdType.MESH
NH, NY, NX, NL, NC = 2, 4, 4, 4, 2
NZ = NH * NL
LAG = 2
PARTS = (1, 1, 1, 2, 2)
F32, BF16 = jnp.float32, jnp.bfloat16


def kernel(
    ov_hbm, tok_hbm, og_hbm, nxt_hbm, master_hbm, first_hbm, second_hbm,
    o_master, o_first, o_second, o_sec, o_proj,
    ov, master, first, second, tok, og, nxt, own, sib_out, sib_in, s1,
    m1x, m1y, f1x, f1y, f1z, r1x, r1y, r1z, s2x, s2y, s2z, r2x, r2y, r2z, s3a, s3z, r3a, r3z,
    cnt, cnt_in, w, acc,
    in_sem, tok_sem, nxt_sem, out_sem, sib_send, sib_recv, cnt_send, cnt_recv,
    p1_send, m1x_recv, m1y_recv, p1x_recv, p1y_recv, p1z_recv,
    p2_send, p2x_recv, p2y_recv, p2z_recv, p3_send, p3a_recv, p3z_recv,
    a3_send, a3a_recv, a3z_recv, a2_send, a2x_recv, a2y_recv, a2z_recv,
    a1_send, a1x_recv, a1y_recv, a1z_recv, f_send, fx_recv, fy_recv, fz_recv,
):
    rows, kv = master.shape
    ca, cb = r1x.shape[-1], r1x.shape[-1] + r1y.shape[-1]
    colx, coly, colz, colxy = pl.ds(0, ca), pl.ds(ca, cb - ca), pl.ds(cb, kv - cb), pl.ds(0, cb)
    node, loc = lax.axis_index("node"), lax.axis_index("local")
    x, y, h = lax.rem(node, NX), lax.rem(lax.div(node, NX), NY), lax.div(node, NX * NY)
    c, l = lax.rem(loc, NC), lax.div(loc, NC)

    def dev(hh=h, yy=y, xx=x, ll=l, cc=c):
        return ((hh * NY + yy) * NX + xx, ll * NC + cc)

    def xs(d):
        return lax.rem(x + d, NX)

    def ys(d):
        return lax.rem(y + d, NY)

    def hs(e):
        return lax.rem(h + e, NH)

    def ls(f):
        return lax.rem(l + f, NL)

    def zdev(k):
        zz = lax.rem(h * NL + l + k + NZ, NZ)
        return dev(hh=lax.div(zz, NL), ll=lax.rem(zz, NL))

    def zat(k):
        zz = lax.rem(h * NL + l + k + NZ, NZ)
        return lax.div(zz, NL), lax.rem(zz, NL)

    xd, yd = range(1, NX), range(1, NY)
    zd = [(e, f) for e in range(NH) for f in range(NL)][1:]
    sib = dev(cc=1 - c)

    def remote(src, dst, send, recv, to):
        return pltpu.make_async_remote_copy(
            src_ref=src, dst_ref=dst, send_sem=send, recv_sem=recv, device_id=to, device_id_type=MESH
        )

    def wait_recv(ref, sem):
        remote(ref, ref, sem, sem, sib).wait_recv()

    def wait_send(ref, sem):
        remote(ref, ref, sem, sem, sib).wait_send()

    pending = []

    def drain():
        for ref, sem in pending:
            wait_send(ref, sem)

    peers = [sib]
    peers += [dev(xx=xs(d)) for d in xd] + [dev(yy=ys(d)) for d in yd]
    peers += [dev(hh=hs(e), ll=ls(f)) for e, f in zd]
    barrier = pltpu.get_barrier_semaphore()
    for to in peers:
        pl.semaphore_signal(barrier, inc=1, device_id=to, device_id_type=MESH)

    og_copy = pltpu.make_async_copy(og_hbm, og, in_sem.at[0])

    def nxt_copy(i):
        cols = pl.ds(pl.multiple_of(i * NL * NC * rows, NL * NC * rows), NL * NC * rows)
        return pltpu.make_async_copy(nxt_hbm.at[:, cols], nxt.at[i], nxt_sem.at[i])

    ov_copy = pltpu.make_async_copy(ov_hbm, ov, in_sem.at[1])
    adam_copies = [
        pltpu.make_async_copy(src, dst, in_sem.at[2 + i])
        for i, (src, dst) in enumerate(((master_hbm, master), (first_hbm, first), (second_hbm, second)))
    ]
    og_copy.start()
    ov_copy.start()
    width = NX * NL * NC * rows
    steps = NH * NY

    def place(it):
        e, d = lax.rem(it, NH), lax.rem(2 + NY - lax.div(it, NH), NY)
        return e, d, hs(e), ys(d)

    def tok_copy(it):
        _, _, hh, yy = place(it)
        cols = pl.ds(pl.multiple_of((hh * NY + yy) * width, width), width)
        return pltpu.make_async_copy(tok_hbm.at[:, cols], tok.at[it], tok_sem.at[it])

    @pl.loop(0, steps)
    def _(it):
        tok_copy(it).start()

    for copy in adam_copies:
        copy.start()
    og_copy.wait()
    ov_copy.wait()
    kept = (1 - ov[0]).astype(F32)
    og[...] = og[...] * kept.astype(BF16)
    cnt[0] = jnp.full(cnt.shape[1:], kept, F32)

    def partial_sum(it):
        _, _, hh, yy = place(it)
        tok_copy(it).wait()
        part = lax.dot_general(tok[it], og[...], (((0,), (0,)), ((), ())), preferred_element_type=F32)
        part = part.reshape(NX, NL, NC, rows, kv)
        even, odd = part[:, :, 0], part[:, :, 1]
        own[hh, yy] = jnp.where(c == 0, even, odd)
        sib_out[hh, yy] = jnp.where(c == 0, odd, even).astype(BF16)

    def send_partial(it):
        _, _, hh, yy = place(it)
        remote(sib_out.at[hh, yy], sib_in.at[hh, yy], sib_send.at[0], sib_recv.at[it], sib).start()

    pl.loop(0, LAG)(partial_sum)
    pl.semaphore_wait(barrier, len(peers))
    remote(cnt.at[0], cnt_in.at[0], cnt_send.at[0], cnt_recv.at[0], sib).start()
    pl.loop(0, LAG)(send_partial)

    def exchange_first(it):
        e, d, hh, yy = place(it)
        wait_recv(sib_in.at[hh, yy], sib_recv.at[it])
        s1[hh, yy] = (own[hh, yy] + sib_in[hh, yy].astype(F32)).astype(BF16)
        go, back = 1 + 2 * hh, NX - 1 - 2 * hh
        remote(
            s1.at[hh, yy, xs(2), :, :, colx], m1x.at[hh, yy], p1_send.at[0], m1x_recv.at[hh, yy], dev(xx=xs(go))
        ).start()
        remote(
            s1.at[hh, yy, xs(back), :, :, colx], r1x.at[0, hh, yy], p1_send.at[1], p1x_recv.at[0], dev(xx=xs(back))
        ).start()

        @pl.when(d == 2)
        def _():
            remote(
                s1.at[hh, yy, :, :, :, coly], m1y.at[hh], p1_send.at[3], m1y_recv.at[hh], dev(yy=ys(go))
            ).start()

        @pl.when(d == back)
        def _():
            remote(
                s1.at[hh, yy, :, :, :, coly], r1y.at[0, hh], p1_send.at[4], p1y_recv.at[0], dev(yy=ys(back))
            ).start()

        @pl.loop(0, NL, unroll=True)
        def _(ll):
            k = lax.rem(hh * NL + ll + NZ - h * NL - l, NZ)
            up = k < 4
            odd = lax.rem(k, 2) == 1
            slot = jnp.where(odd, jnp.where((k == 1) | (k == 7), 0, 2) + jnp.where(up, 0, 1), 4)
            hop = jnp.where(odd, jnp.where(up, 1, NZ - 1), jnp.where(yy < NY // 2, 2, NZ - 2))

            @pl.when(odd | (k == 4))
            def _():
                remote(
                    s1.at[hh, yy, :, ll, :, colz], r1z.at[slot, yy], p1_send.at[6], p1z_recv.at[slot], zdev(hop)
                ).start()

    @pl.loop(LAG, steps)
    def _(it):
        partial_sum(it)
        send_partial(it)
        exchange_first(it - LAG)

    pl.loop(steps - LAG, steps)(exchange_first)

    wait_recv(cnt_in.at[0], cnt_recv.at[0])
    cnt[1] = cnt[0] + cnt_in[0]
    for k in xd:
        remote(cnt.at[1], cnt_in.at[k], cnt_send.at[1], cnt_recv.at[k], dev(xx=xs(k))).start()

    pending += [(sib_out, sib_send.at[0]), (cnt.at[0], cnt_send.at[0]), (cnt_in.at[pl.ds(0, NX - 1)], cnt_send.at[1])]
    pending += [(m1x, p1_send.at[0]), (r1x.at[0], p1_send.at[1]), (m1y, p1_send.at[3]), (r1y.at[0], p1_send.at[4])]
    pending += [(r1z.at[pl.ds(0, 5)], p1_send.at[6])]

    for slot in (2, 3, 4):
        wait_recv(r1z.at[slot], p1z_recv.at[slot])
    for i, k in ((0, 2), (1, NZ - 2)):
        hh, ll = zat(k)
        for yy in range(NY):
            total = s1[hh, yy, :, ll, :, colz].astype(F32) + r1z[2 + i, yy].astype(F32)
            if (yy < NY // 2) == (i == 0):
                total += r1z[4, yy].astype(F32)
            f1z[i, yy] = total.astype(BF16)
        remote(f1z.at[i], r1z.at[5 + i], p1_send.at[7], p1z_recv.at[5 + i], zdev(k)).start()

    @pl.loop(0, steps)
    def _(it):
        _, _, hh, yy = place(it)
        go = 1 + 2 * hh
        wait_recv(m1x.at[hh, yy], m1x_recv.at[hh, yy])
        f1x[hh, yy] = (s1[hh, yy, xs(go), :, :, colx].astype(F32) + m1x[hh, yy].astype(F32)).astype(BF16)
        remote(f1x.at[hh, yy], r1x.at[1, hh, yy], p1_send.at[2], p1x_recv.at[1], dev(xx=xs(go))).start()

    @pl.loop(0, NH)
    def _(hh):
        go = 1 + 2 * hh
        wait_recv(m1y.at[hh], m1y_recv.at[hh])

        @pl.loop(0, NX)
        def _(xx):
            f1y[hh, xx] = (s1[hh, ys(go), xx, :, :, coly].astype(F32) + m1y[hh, xx].astype(F32)).astype(BF16)

        remote(f1y.at[hh], r1y.at[1, hh], p1_send.at[5], p1y_recv.at[1], dev(yy=ys(go))).start()

    pending += [(f1x, p1_send.at[2]), (f1y, p1_send.at[5]), (f1z, p1_send.at[7])]

    @pl.loop(0, NH * NY * NX)
    def _(i):
        nxt_copy(i).start()

    for k in range(2):
        wait_recv(r1x.at[k], p1x_recv.at[k])

    @pl.loop(0, NH * NY)
    def _(i):
        hh, yy = lax.div(i, NY), lax.rem(i, NY)
        total = s1[hh, yy, x, :, :, colx].astype(F32)
        for k in range(2):
            total += r1x[k, hh, yy].astype(F32)
        s2x[hh, yy] = total.astype(BF16)

    for k in yd:
        remote(s2x.at[:, ys(k)], r2x.at[k - 1], p2_send.at[0], p2x_recv.at[k - 1], dev(yy=ys(k))).start()

    for k in range(2):
        wait_recv(r1y.at[k], p1y_recv.at[k])

    @pl.loop(0, NH * NX)
    def _(i):
        hh, xx = lax.div(i, NX), lax.rem(i, NX)
        total = s1[hh, y, xx, :, :, coly].astype(F32)
        for k in range(2):
            total += r1y[k, hh, xx].astype(F32)
        s2y[hh, xx] = total.astype(BF16)

    for k in xd:
        remote(s2y.at[:, xs(k)], r2y.at[k - 1], p2_send.at[1], p2y_recv.at[k - 1], dev(xx=xs(k))).start()

    for k in (0, 1, 5, 6):
        wait_recv(r1z.at[k], p1z_recv.at[k])

    @pl.loop(0, NY)
    def _(yy):
        total = s1[h, yy, :, l, :, colz].astype(F32)
        for k in (0, 1, 5, 6):
            total += r1z[k, yy].astype(F32)
        s2z[yy] = total.astype(BF16)

    for k in xd:
        remote(s2z.at[:, xs(k)], r2z.at[k - 1], p2_send.at[2], p2z_recv.at[k - 1], dev(xx=xs(k))).start()

    for k in xd:
        wait_recv(cnt_in.at[k], cnt_recv.at[k])
    cnt[2] = cnt[1] + cnt_in[1] + cnt_in[2] + cnt_in[3]
    for k in yd:
        remote(cnt.at[2], cnt_in.at[NX - 1 + k], cnt_send.at[2], cnt_recv.at[NX - 1 + k], dev(yy=ys(k))).start()

    pending += [(r2x, p2_send.at[0]), (r2y, p2_send.at[1]), (r2z, p2_send.at[2])]
    pending += [(cnt_in.at[pl.ds(0, NY - 1)], cnt_send.at[2])]

    for k in yd:
        wait_recv(r2x.at[k - 1], p2x_recv.at[k - 1])
    total = s2x[:, y].astype(F32)
    for k in yd:
        total += r2x[k - 1].astype(F32)
    s3a[:, :, :, colx] = total.astype(BF16)
    for k in xd:
        wait_recv(r2y.at[k - 1], p2y_recv.at[k - 1])
    total = s2y[:, x].astype(F32)
    for k in xd:
        total += r2y[k - 1].astype(F32)
    s3a[:, :, :, coly] = total.astype(BF16)
    for e, f in zd:
        slot = e * NL + f - 1
        remote(
            s3a.at[hs(e), ls(f)], r3a.at[slot], p3_send.at[0], p3a_recv.at[slot], dev(hh=hs(e), ll=ls(f))
        ).start()
    for k in xd:
        wait_recv(r2z.at[k - 1], p2z_recv.at[k - 1])
    total = s2z[:, x].astype(F32)
    for k in xd:
        total += r2z[k - 1].astype(F32)
    s3z[...] = total.astype(BF16)
    for k in yd:
        remote(s3z.at[ys(k)], r3z.at[k - 1], p3_send.at[1], p3z_recv.at[k - 1], dev(yy=ys(k))).start()

    base = NX + NY - 1
    for k in yd:
        wait_recv(cnt_in.at[NX - 1 + k], cnt_recv.at[NX - 1 + k])
    cnt[3] = cnt[2] + cnt_in[NX] + cnt_in[NX + 1] + cnt_in[NX + 2]
    for e, f in zd:
        slot = base + e * NL + f - 1
        remote(cnt.at[3], cnt_in.at[slot], cnt_send.at[3], cnt_recv.at[slot], dev(hh=hs(e), ll=ls(f))).start()

    for k in range(1, NZ):
        wait_recv(r3a.at[k - 1], p3a_recv.at[k - 1])
    sum_a = s3a[h, l].astype(F32)
    for k in range(1, NZ):
        sum_a += r3a[k - 1].astype(F32)
    for k in yd:
        wait_recv(r3z.at[k - 1], p3z_recv.at[k - 1])
    sum_z = s3z[y].astype(F32)
    for k in yd:
        sum_z += r3z[k - 1].astype(F32)
    for k in range(1, NZ):
        wait_recv(cnt_in.at[base + k - 1], cnt_recv.at[base + k - 1])
    count = cnt[3]
    for k in range(1, NZ):
        count += cnt_in[base + k - 1]
    count = count[0:1, 0:1]

    pending += [(r3a, p3_send.at[0]), (r3z, p3_send.at[1]), (cnt_in.at[pl.ds(0, NZ - 1)], cnt_send.at[3])]

    for copy in adam_copies:
        copy.wait()

    def adam(cols, summed):
        grad = summed / count
        new_first = 0.9 * first[:, cols] + 0.1 * grad
        new_second = 0.95 * second[:, cols] + 0.05 * grad * grad
        update = new_first / (1.0 - 0.9**STEP) / (jnp.sqrt(new_second / (1.0 - 0.95**STEP)) + 1e-08)
        new_master = master[:, cols] - 0.001 * (update + 0.1 * master[:, cols])
        o_first[:, cols] = new_first
        o_second[:, cols] = new_second
        o_master[:, cols] = new_master
        w[h, y, x, l, c, :, cols] = new_master.astype(BF16)

    adam(colxy, sum_a)
    adam(colz, sum_z)

    def gather(ref, send, recv, to):
        remote(ref, ref, send, recv, to).start()

    for e, f in zd:
        gather(w.at[h, y, x, l, c, :, colxy], a3_send.at[0], a3a_recv.at[e * NL + f - 1], dev(hh=hs(e), ll=ls(f)))
    for k in yd:
        gather(w.at[h, y, x, l, c, :, colz], a3_send.at[1], a3z_recv.at[k - 1], dev(yy=ys(k)))
    for k in range(1, NZ):
        wait_recv(r3a.at[k - 1], a3a_recv.at[k - 1])
    for k in yd:
        gather(w.at[:, y, x, :, c, :, colx], a2_send.at[0], a2x_recv.at[k - 1], dev(yy=ys(k)))
    for k in xd:
        gather(w.at[:, y, x, :, c, :, coly], a2_send.at[1], a2y_recv.at[k - 1], dev(xx=xs(k)))
    for k in yd:
        wait_recv(r3z.at[k - 1], a3z_recv.at[k - 1])
    for k in xd:
        gather(w.at[h, :, x, l, c, :, colz], a2_send.at[2], a2z_recv.at[k - 1], dev(xx=xs(k)))

    def xpart(k, hh):
        return w.at[hh, :, xs(k), :, c, :, colx]

    def ypart(k, hh):
        return w.at[hh, ys(k), :, :, c, :, coly]

    def zpart(k):
        hh, ll = zat(k)
        return w.at[hh, :, :, ll, c, :, colz]

    def zhalf(k, i):
        hh, ll = zat(k)
        return w.at[hh, pl.ds(i * (NY // 2), NY // 2), :, ll, c, :, colz]

    pending += [(r3a, a3_send.at[0]), (r3z, a3_send.at[1])]
    pending += [(r2x, a2_send.at[0]), (r2y, a2_send.at[1]), (r2z, a2_send.at[2])]

    def send_x(part, turn):
        for i in range(2):
            to = 1 + 2 * i if turn == 0 else 3 - 2 * i
            gather(w.at[i, part, x, :, c, :, colx], a1_send.at[0], a1x_recv.at[i, turn], dev(xx=xs(to)))

    def send_y(part, turn):
        for i in range(2):
            to = 1 + 2 * i if turn == 0 else 3 - 2 * i
            gather(w.at[i, y, part, :, c, :, coly], a1_send.at[2], a1y_recv.at[i, turn], dev(yy=ys(to)))

    def send_z(part, turn):
        for i in range(2):
            to = (2 - turn) * (1 - 2 * i)
            gather(w.at[h, :, part, l, c, :, colz], a1_send.at[4], a1z_recv.at[2 * turn + i], zdev(to))

    for turn in range(2):
        send_x(y, turn)
        send_y(x, turn)
        send_z(x, turn)
    for k in (1, 3, 2):
        wait_recv(r2x.at[k - 1], a2x_recv.at[k - 1])
        send_x(ys(NY - k), 0)
        wait_recv(r2y.at[k - 1], a2y_recv.at[k - 1])
        send_y(xs(NX - k), 0)
        wait_recv(r2z.at[k - 1], a2z_recv.at[k - 1])
        send_z(xs(NX - k), 0)
    for k in (1, 3, 2):
        send_x(ys(NY - k), 1)
        send_y(xs(NX - k), 1)
        send_z(xs(NX - k), 1)
    for i in range(2):
        gather(xpart(0, i), f_send.at[0], fx_recv.at[0], sib)
        gather(ypart(0, i), f_send.at[1], fy_recv.at[0], sib)
    gather(zpart(0), f_send.at[2], fz_recv.at[0], sib)

    for i in range(2):
        wait_recv(m1x.at[0], a1x_recv.at[i, 0])
        gather(xpart(3 - 2 * i, i), a1_send.at[1], a1x_recv.at[i, 2], dev(xx=xs(1 + 2 * i)))
        wait_recv(m1y.at[0], a1y_recv.at[i, 0])
        gather(ypart(3 - 2 * i, i), a1_send.at[3], a1y_recv.at[i, 2], dev(yy=ys(1 + 2 * i)))
    for i, k in enumerate((-2, 2)):
        wait_recv(r1z.at[0], a1z_recv.at[i])
        gather(zhalf(k, i), a1_send.at[5], a1z_recv.at[4 + i], zdev(-k))
        gather(zpart(k), a1_send.at[5], a1z_recv.at[6 + i], zdev(-k // 2))
    for i in range(2):
        gather(xpart(3 - 2 * i, i), f_send.at[0], fx_recv.at[3 - 2 * i], sib)
        gather(ypart(3 - 2 * i, i), f_send.at[1], fy_recv.at[3 - 2 * i], sib)
    for k in (-2, 2):
        gather(zpart(k), f_send.at[2], fz_recv.at[0], sib)

    pending += [(r1x, a1_send.at[0]), (r1x.at[0], a1_send.at[1]), (r1y, a1_send.at[2]), (r1y.at[0], a1_send.at[3])]
    pending += [(r1z.at[pl.ds(0, 4)], a1_send.at[4]), (r1z.at[pl.ds(0, 3)], a1_send.at[5])]
    pending += [(w.at[:, :, :, :, c, :, cols], f_send.at[i]) for i, cols in enumerate((colx, coly, colz))]

    def project_x(k):
        for hh in range(NH):
            lhs = jnp.concatenate([nxt[(hh * NY + yy) * NX + xs(k)] for yy in range(NY)], axis=1)
            rhs = w[hh, :, xs(k), :, :, :, colx].reshape(NY * NL * NC * rows, ca)
            acc[:, colx] += jnp.dot(lhs, rhs, preferred_element_type=F32)

    def project_y(k):
        for hh in range(NH):
            lhs = jnp.concatenate([nxt[(hh * NY + ys(k)) * NX + xx] for xx in range(NX)], axis=1)
            rhs = w[hh, ys(k), :, :, :, :, coly].reshape(NX * NL * NC * rows, cb - ca)
            acc[:, coly] += jnp.dot(lhs, rhs, preferred_element_type=F32)

    acc[...] = jnp.zeros_like(acc)

    @pl.loop(0, NH * NY * NX)
    def _(i):
        nxt_copy(i).wait()

    wait_recv(r1x.at[0], fx_recv.at[0])
    project_x(0)
    for i in range(2):
        wait_recv(m1x.at[0], a1x_recv.at[i, 1])
        gather(xpart(1 + 2 * i, i), f_send.at[0], fx_recv.at[1 + 2 * i], sib)
        wait_recv(m1y.at[0], a1y_recv.at[i, 1])
        gather(ypart(1 + 2 * i, i), f_send.at[1], fy_recv.at[1 + 2 * i], sib)
    wait_recv(r1y.at[0], fy_recv.at[0])
    project_y(0)
    for i, k in enumerate((-1, 1)):
        wait_recv(r1z.at[0], a1z_recv.at[2 + i])
        gather(zpart(k), f_send.at[2], fz_recv.at[0], sib)
    for k in (1, 3):
        wait_recv(r1x.at[0], fx_recv.at[k])
        project_x(k)
        wait_recv(r1y.at[0], fy_recv.at[k])
        project_y(k)
    for i in range(2):
        wait_recv(m1x.at[0], a1x_recv.at[i, 2])
        gather(xpart(2, i), f_send.at[0], fx_recv.at[2], sib)
        wait_recv(m1y.at[0], a1y_recv.at[i, 2])
        gather(ypart(2, i), f_send.at[1], fy_recv.at[2], sib)
    for i, k in enumerate((-3, 3)):
        wait_recv(r1z.at[0], a1z_recv.at[6 + i])
        gather(zpart(k), f_send.at[2], fz_recv.at[0], sib)
    for i in range(2):
        wait_recv(r1z.at[0, pl.ds(0, NY // 2)], a1z_recv.at[4 + i])
        gather(zhalf(4, i), f_send.at[2], fz_recv.at[0], sib)
    sec_copy = pltpu.make_async_copy(w.at[:, :, :, l, c], o_sec, out_sem.at[0])
    sec_copy.start()
    wait_recv(r1x.at[0], fx_recv.at[2])
    project_x(2)
    o_proj[:, colx] = acc[:, colx].astype(BF16)
    wait_recv(r1y.at[0], fy_recv.at[2])
    project_y(2)
    o_proj[:, coly] = acc[:, coly].astype(BF16)
    wait_recv(w.at[:, :, :, :, 1 - c, :, colz], fz_recv.at[0])

    @pl.loop(0, NH)
    def _(hh):
        lhs = jnp.concatenate([nxt[hh * NY * NX + i] for i in range(NY * NX)], axis=1)
        rhs = w[hh, :, :, :, :, :, colz].reshape(NY * width, kv - cb)
        acc[:, colz] += jnp.dot(lhs, rhs, preferred_element_type=F32)

    o_proj[:, colz] = acc[:, colz].astype(BF16)
    sec_copy.wait()

    drain()


def copy_out(*refs):
    src, dst, sem = refs[:5], refs[5:10], refs[10]
    copies = []
    for i in range(5):
        n, rows = PARTS[i], src[i].shape[0]
        for j in range(n):
            part = pl.ds(j * rows // n, rows // n)
            copies.append(pltpu.make_async_copy(src[i].at[part], dst[i].at[part], sem.at[len(copies)]))
    for copy in copies:
        copy.start()
    for copy in copies:
        copy.wait()


def body(tokens, out_grad, next_tokens, overflow, master, first_moment, second_moment):
    toks, din = tokens.shape
    rows, kv = master.shape
    ca, cb = 3 * kv // 8, 6 * kv // 8
    cx, cy, cz = ca, cb - ca, kv - cb
    width = NX * NL * NC * rows
    vmem, anym = pl.BlockSpec(memory_space=pltpu.VMEM), pl.BlockSpec(memory_space=pl.ANY)
    dma = pltpu.SemaphoreType.DMA
    shapes = (
        jax.ShapeDtypeStruct((rows, kv), F32),
        jax.ShapeDtypeStruct((rows, kv), F32),
        jax.ShapeDtypeStruct((rows, kv), F32),
        jax.ShapeDtypeStruct((NH, NY, NX, rows, kv), BF16),
        jax.ShapeDtypeStruct((toks, kv), BF16),
    )
    scratch = [
        pltpu.SMEM((1,), jnp.int32),
        pltpu.VMEM((rows, kv), F32),
        pltpu.VMEM((rows, kv), F32),
        pltpu.VMEM((rows, kv), F32),
        pltpu.VMEM((NH * NY, toks, width), BF16),
        pltpu.VMEM((toks, kv), BF16),
        pltpu.VMEM((NH * NY * NX, toks, NL * NC * rows), BF16),
        pltpu.VMEM((NH, NY, NX, NL, rows, kv), F32),
        pltpu.VMEM((NH, NY, NX, NL, rows, kv), BF16),
        pltpu.VMEM((NH, NY, NX, NL, rows, kv), BF16),
        pltpu.VMEM((NH, NY, NX, NL, rows, kv), BF16),
        pltpu.VMEM((NH, NY, NL, rows, cx), BF16),
        pltpu.VMEM((NH, NX, NL, rows, cy), BF16),
        pltpu.VMEM((NH, NY, NL, rows, cx), BF16),
        pltpu.VMEM((NH, NX, NL, rows, cy), BF16),
        pltpu.VMEM((2, NY, NX, rows, cz), BF16),
        pltpu.VMEM((2, NH, NY, NL, rows, cx), BF16),
        pltpu.VMEM((2, NH, NX, NL, rows, cy), BF16),
        pltpu.VMEM((7, NY, NX, rows, cz), BF16),
        pltpu.VMEM((NH, NY, NL, rows, cx), BF16),
        pltpu.VMEM((NH, NX, NL, rows, cy), BF16),
        pltpu.VMEM((NY, NX, rows, cz), BF16),
        pltpu.VMEM((NY - 1, NH, NL, rows, cx), BF16),
        pltpu.VMEM((NX - 1, NH, NL, rows, cy), BF16),
        pltpu.VMEM((NX - 1, NY, rows, cz), BF16),
        pltpu.VMEM((NH, NL, rows, cx + cy), BF16),
        pltpu.VMEM((NY, rows, cz), BF16),
        pltpu.VMEM((NZ - 1, rows, cx + cy), BF16),
        pltpu.VMEM((NY - 1, rows, cz), BF16),
        pltpu.VMEM((4, 8, 128), F32),
        pltpu.VMEM((1 + NX - 1 + NY - 1 + NZ - 1, 8, 128), F32),
        pltpu.VMEM((NH, NY, NX, NL, NC, rows, kv), BF16),
        pltpu.VMEM((toks, kv), F32),
    ]
    sems = (
        [(5,), (NH * NY,), (NH * NY * NX,), (1,), (1,), (NH * NY,), (4,), (NX + NY + NZ - 2,)]
        + [(8,), (NH, NY), (NH,), (2,), (2,), (7,)]
        + [(3,), (NY - 1,), (NX - 1,), (NX - 1,)]
        + [(2,), (NZ - 1,), (NY - 1,)]
        + [(2,), (NZ - 1,), (NY - 1,)]
        + [(3,), (NY - 1,), (NX - 1,), (NX - 1,)]
        + [(6,), (2, 3), (2, 3), (8,)]
        + [(3,), (NX,), (NY,), (1,)]
    )
    results = pl.pallas_call(
        kernel,
        out_shape=[pltpu.VMEM(shape.shape, shape.dtype) for shape in shapes],
        in_specs=[anym] * 7,
        out_specs=[vmem] * 5,
        scratch_shapes=scratch + [dma(n) for n in sems],
        compiler_params=pltpu.CompilerParams(
            collective_id=0, has_side_effects=True, vmem_limit_bytes=56 * 2**20
        ),
        cost_estimate=pl.CostEstimate(flops=4 * toks * din * kv, bytes_accessed=12 * 2**20, transcendentals=rows * kv),
    )(overflow, tokens, out_grad, next_tokens, master, first_moment, second_moment)
    new_master, new_first, new_second, sec, proj = pl.pallas_call(
        copy_out,
        out_shape=shapes,
        in_specs=[vmem] * 5,
        out_specs=[anym] * 5,
        scratch_shapes=[dma((sum(PARTS),))],
        compiler_params=pltpu.CompilerParams(vmem_limit_bytes=8 * 2**20),
    )(*results)
    return (new_master, new_first, new_second, sec.reshape(NH * NY * NX, rows, kv), proj)


def solution(mesh):
    return jax.shard_map(
        body,
        mesh=mesh,
        in_specs=(
            P(("node", "local"), None),
            P(("node", "local"), None),
            P(("node", "local"), None),
            P(("node", "local")),
            P(("node", "local"), None),
            P(("node", "local"), None),
            P(("node", "local"), None),
        ),
        out_specs=(
            P(("node", "local"), None),
            P(("node", "local"), None),
            P(("node", "local"), None),
            P(None, "local", None),
            P(("node", "local"), None),
        ),
        check_vma=False,
    )
```

```python
import functools

import jax
import jax.numpy as jnp
from jax import lax
from jax.experimental import pallas as pl
from jax.experimental.pallas import tpu as pltpu
from jax.sharding import PartitionSpec as P

STEP = 10
MESH = pl.DeviceIdType.MESH
NH, NY, NX, NL, NC = 2, 4, 4, 4, 2
NZ = NH * NL
LAG = 2
PARTS = (1, 1, 1, 2, 2)
F32, BF16 = jnp.float32, jnp.bfloat16


def kernel(
    ov_hbm, tok_hbm, og_hbm, nxt_hbm, master_hbm, first_hbm, second_hbm,
    o_master, o_first, o_second, o_sec, o_proj,
    ov, master, first, second, tok, og, nxt, own, sib_out, sib_in, s1,
    m1x, m1y, f1x, f1y, f1z, r1x, r1y, r1z, s2x, s2y, s2z, r2x, r2y, r2z, s3a, s3z, r3a, r3z,
    cnt, cnt_in, w, acc,
    in_sem, tok_sem, nxt_sem, out_sem, sib_send, sib_recv, cnt_send, cnt_recv,
    p1_send, m1x_recv, m1y_recv, p1x_recv, p1y_recv, p1z_recv,
    p2_send, p2x_recv, p2y_recv, p2z_recv, p3_send, p3a_recv, p3z_recv,
    a3_send, a3a_recv, a3z_recv, a2_send, a2x_recv, a2y_recv, a2z_recv,
    a1_send, a1x_recv, a1y_recv, a1z_recv, f_send, fx_recv, fy_recv, fz_recv,
):
    rows, kv = master.shape
    ca, cb = r1x.shape[-1], r1x.shape[-1] + r1y.shape[-1]
    colx, coly, colz, colxy = pl.ds(0, ca), pl.ds(ca, cb - ca), pl.ds(cb, kv - cb), pl.ds(0, cb)
    node, loc = lax.axis_index("node"), lax.axis_index("local")
    x, y, h = lax.rem(node, NX), lax.rem(lax.div(node, NX), NY), lax.div(node, NX * NY)
    c, l = lax.rem(loc, NC), lax.div(loc, NC)

    def dev(hh=h, yy=y, xx=x, ll=l, cc=c):
        return ((hh * NY + yy) * NX + xx, ll * NC + cc)

    def xs(d):
        return lax.rem(x + d, NX)

    def ys(d):
        return lax.rem(y + d, NY)

    def hs(e):
        return lax.rem(h + e, NH)

    def ls(f):
        return lax.rem(l + f, NL)

    def zdev(k):
        zz = lax.rem(h * NL + l + k + NZ, NZ)
        return dev(hh=lax.div(zz, NL), ll=lax.rem(zz, NL))

    def zat(k):
        zz = lax.rem(h * NL + l + k + NZ, NZ)
        return lax.div(zz, NL), lax.rem(zz, NL)

    xd, yd = range(1, NX), range(1, NY)
    zd = [(e, f) for e in range(NH) for f in range(NL)][1:]
    sib = dev(cc=1 - c)

    def remote(src, dst, send, recv, to):
        return pltpu.make_async_remote_copy(
            src_ref=src, dst_ref=dst, send_sem=send, recv_sem=recv, device_id=to, device_id_type=MESH
        )

    def wait_recv(ref, sem):
        remote(ref, ref, sem, sem, sib).wait_recv()

    def wait_send(ref, sem):
        remote(ref, ref, sem, sem, sib).wait_send()

    pending = []

    def drain():
        for ref, sem in pending:
            wait_send(ref, sem)

    peers = [sib]
    peers += [dev(xx=xs(d)) for d in xd] + [dev(yy=ys(d)) for d in yd]
    peers += [dev(hh=hs(e), ll=ls(f)) for e, f in zd]
    barrier = pltpu.get_barrier_semaphore()
    for to in peers:
        pl.semaphore_signal(barrier, inc=1, device_id=to, device_id_type=MESH)

    og_copy = pltpu.make_async_copy(og_hbm, og, in_sem.at[0])

    def nxt_copy(i):
        cols = pl.ds(pl.multiple_of(i * NL * NC * rows, NL * NC * rows), NL * NC * rows)
        return pltpu.make_async_copy(nxt_hbm.at[:, cols], nxt.at[i], nxt_sem.at[i])

    ov_copy = pltpu.make_async_copy(ov_hbm, ov, in_sem.at[1])
    adam_copies = [
        pltpu.make_async_copy(src, dst, in_sem.at[2 + i])
        for i, (src, dst) in enumerate(((master_hbm, master), (first_hbm, first), (second_hbm, second)))
    ]
    ov_copy.start()
    og_copy.start()
    width = NX * NL * NC * rows
    steps = NH * NY

    def place(it):
        e, d = lax.rem(it, NH), lax.rem(2 + NY - lax.div(it, NH), NY)
        return e, d, hs(e), ys(d)

    def tok_copy(it):
        _, _, hh, yy = place(it)
        cols = pl.ds(pl.multiple_of((hh * NY + yy) * width, width), width)
        return pltpu.make_async_copy(tok_hbm.at[:, cols], tok.at[it], tok_sem.at[it])

    def start_tok(it):
        tok_copy(it).start()

    pl.loop(0, LAG)(start_tok)
    og_copy.wait()
    pl.loop(LAG, steps)(start_tok)
    ov_copy.wait()
    kept = (1 - ov[0]).astype(F32)
    og[...] = og[...] * kept.astype(BF16)
    cnt[0] = jnp.full(cnt.shape[1:], kept, F32)

    def partial_sum(it):
        _, _, hh, yy = place(it)
        tok_copy(it).wait()
        part = lax.dot_general(tok[it], og[...], (((0,), (0,)), ((), ())), preferred_element_type=F32)
        part = part.reshape(NX, NL, NC, rows, kv)
        even, odd = part[:, :, 0], part[:, :, 1]
        own[hh, yy] = jnp.where(c == 0, even, odd)
        sib_out[hh, yy] = jnp.where(c == 0, odd, even).astype(BF16)

    def send_partial(it):
        _, _, hh, yy = place(it)
        remote(sib_out.at[hh, yy], sib_in.at[hh, yy], sib_send.at[0], sib_recv.at[it], sib).start()

    pl.loop(0, LAG)(partial_sum)
    pl.semaphore_wait(barrier, len(peers))
    remote(cnt.at[0], cnt_in.at[0], cnt_send.at[0], cnt_recv.at[0], sib).start()
    pl.loop(0, LAG)(send_partial)

    def exchange_first(it):
        e, d, hh, yy = place(it)
        wait_recv(sib_in.at[hh, yy], sib_recv.at[it])
        s1[hh, yy] = (own[hh, yy] + sib_in[hh, yy].astype(F32)).astype(BF16)
        go, back = 1 + 2 * hh, NX - 1 - 2 * hh
        remote(
            s1.at[hh, yy, xs(2), :, :, colx], m1x.at[hh, yy], p1_send.at[0], m1x_recv.at[hh, yy], dev(xx=xs(go))
        ).start()
        remote(
            s1.at[hh, yy, xs(back), :, :, colx], r1x.at[0, hh, yy], p1_send.at[1], p1x_recv.at[0], dev(xx=xs(back))
        ).start()

        @pl.when(d == 2)
        def _():
            remote(
                s1.at[hh, yy, :, :, :, coly], m1y.at[hh], p1_send.at[3], m1y_recv.at[hh], dev(yy=ys(go))
            ).start()

        @pl.when(d == back)
        def _():
            remote(
                s1.at[hh, yy, :, :, :, coly], r1y.at[0, hh], p1_send.at[4], p1y_recv.at[0], dev(yy=ys(back))
            ).start()

        @pl.loop(0, NL, unroll=True)
        def _(ll):
            k = lax.rem(hh * NL + ll + NZ - h * NL - l, NZ)
            up = k < 4
            odd = lax.rem(k, 2) == 1
            slot = jnp.where(odd, jnp.where((k == 1) | (k == 7), 0, 2) + jnp.where(up, 0, 1), 4)
            hop = jnp.where(odd, jnp.where(up, 1, NZ - 1), jnp.where(yy < NY // 2, 2, NZ - 2))

            @pl.when(odd | (k == 4))
            def _():
                remote(
                    s1.at[hh, yy, :, ll, :, colz], r1z.at[slot, yy], p1_send.at[6], p1z_recv.at[slot], zdev(hop)
                ).start()

    @pl.loop(LAG, steps)
    def _(it):
        partial_sum(it)
        send_partial(it)
        exchange_first(it - LAG)

    pl.loop(steps - LAG, steps)(exchange_first)

    wait_recv(cnt_in.at[0], cnt_recv.at[0])
    cnt[1] = cnt[0] + cnt_in[0]
    for k in xd:
        remote(cnt.at[1], cnt_in.at[k], cnt_send.at[1], cnt_recv.at[k], dev(xx=xs(k))).start()

    pending += [(sib_out, sib_send.at[0]), (cnt.at[0], cnt_send.at[0]), (cnt_in.at[pl.ds(0, NX - 1)], cnt_send.at[1])]
    pending += [(m1x, p1_send.at[0]), (r1x.at[0], p1_send.at[1]), (m1y, p1_send.at[3]), (r1y.at[0], p1_send.at[4])]
    pending += [(r1z.at[pl.ds(0, 5)], p1_send.at[6])]

    def relay_x(it):
        _, _, hh, yy = place(it)
        go = 1 + 2 * hh
        wait_recv(m1x.at[hh, yy], m1x_recv.at[hh, yy])
        f1x[hh, yy] = (s1[hh, yy, xs(go), :, :, colx].astype(F32) + m1x[hh, yy].astype(F32)).astype(BF16)
        remote(f1x.at[hh, yy], r1x.at[1, hh, yy], p1_send.at[2], p1x_recv.at[1], dev(xx=xs(go))).start()

    @pl.loop(0, NH)
    def _(hh):
        go = 1 + 2 * hh
        wait_recv(m1y.at[hh], m1y_recv.at[hh])

        @pl.loop(0, NX)
        def _(xx):
            f1y[hh, xx] = (s1[hh, ys(go), xx, :, :, coly].astype(F32) + m1y[hh, xx].astype(F32)).astype(BF16)

        remote(f1y.at[hh], r1y.at[1, hh], p1_send.at[5], p1y_recv.at[1], dev(yy=ys(go))).start()

    pl.loop(0, steps - LAG)(relay_x)

    for slot in (2, 3, 4):
        wait_recv(r1z.at[slot], p1z_recv.at[slot])
    for i, k in ((0, 2), (1, NZ - 2)):
        hh, ll = zat(k)
        for yy in range(NY):
            total = s1[hh, yy, :, ll, :, colz].astype(F32) + r1z[2 + i, yy].astype(F32)
            if (yy < NY // 2) == (i == 0):
                total += r1z[4, yy].astype(F32)
            f1z[i, yy] = total.astype(BF16)
        remote(f1z.at[i], r1z.at[5 + i], p1_send.at[7], p1z_recv.at[5 + i], zdev(k)).start()

    pl.loop(steps - LAG, steps)(relay_x)

    pending += [(f1x, p1_send.at[2]), (f1y, p1_send.at[5]), (f1z, p1_send.at[7])]

    @pl.loop(0, NH * NY * NX)
    def _(i):
        nxt_copy(i).start()

    for copy in adam_copies:
        copy.start()

    for k in range(2):
        wait_recv(r1x.at[k], p1x_recv.at[k])

    @pl.loop(0, NH * NY)
    def _(i):
        hh, yy = lax.div(i, NY), lax.rem(i, NY)
        total = s1[hh, yy, x, :, :, colx].astype(F32)
        for k in range(2):
            total += r1x[k, hh, yy].astype(F32)
        s2x[hh, yy] = total.astype(BF16)

    for k in yd:
        remote(s2x.at[:, ys(k)], r2x.at[k - 1], p2_send.at[0], p2x_recv.at[k - 1], dev(yy=ys(k))).start()

    for k in range(2):
        wait_recv(r1y.at[k], p1y_recv.at[k])

    @pl.loop(0, NH * NX)
    def _(i):
        hh, xx = lax.div(i, NX), lax.rem(i, NX)
        total = s1[hh, y, xx, :, :, coly].astype(F32)
        for k in range(2):
            total += r1y[k, hh, xx].astype(F32)
        s2y[hh, xx] = total.astype(BF16)

    for k in xd:
        remote(s2y.at[:, xs(k)], r2y.at[k - 1], p2_send.at[1], p2y_recv.at[k - 1], dev(xx=xs(k))).start()

    for k in (0, 1, 5, 6):
        wait_recv(r1z.at[k], p1z_recv.at[k])

    @pl.loop(0, NY)
    def _(yy):
        total = s1[h, yy, :, l, :, colz].astype(F32)
        for k in (0, 1, 5, 6):
            total += r1z[k, yy].astype(F32)
        s2z[yy] = total.astype(BF16)

    for k in xd:
        remote(s2z.at[:, xs(k)], r2z.at[k - 1], p2_send.at[2], p2z_recv.at[k - 1], dev(xx=xs(k))).start()

    for k in xd:
        wait_recv(cnt_in.at[k], cnt_recv.at[k])
    cnt[2] = cnt[1] + cnt_in[1] + cnt_in[2] + cnt_in[3]
    for k in yd:
        remote(cnt.at[2], cnt_in.at[NX - 1 + k], cnt_send.at[2], cnt_recv.at[NX - 1 + k], dev(yy=ys(k))).start()

    pending += [(r2x, p2_send.at[0]), (r2y, p2_send.at[1]), (r2z, p2_send.at[2])]
    pending += [(cnt_in.at[pl.ds(0, NY - 1)], cnt_send.at[2])]

    for k in yd:
        wait_recv(r2x.at[k - 1], p2x_recv.at[k - 1])
    total = s2x[:, y].astype(F32)
    for k in yd:
        total += r2x[k - 1].astype(F32)
    s3a[:, :, :, colx] = total.astype(BF16)
    for k in xd:
        wait_recv(r2y.at[k - 1], p2y_recv.at[k - 1])
    total = s2y[:, x].astype(F32)
    for k in xd:
        total += r2y[k - 1].astype(F32)
    s3a[:, :, :, coly] = total.astype(BF16)
    for e, f in zd:
        slot = e * NL + f - 1
        remote(
            s3a.at[hs(e), ls(f)], r3a.at[slot], p3_send.at[0], p3a_recv.at[slot], dev(hh=hs(e), ll=ls(f))
        ).start()
    for k in xd:
        wait_recv(r2z.at[k - 1], p2z_recv.at[k - 1])
    total = s2z[:, x].astype(F32)
    for k in xd:
        total += r2z[k - 1].astype(F32)
    s3z[...] = total.astype(BF16)
    for k in yd:
        remote(s3z.at[ys(k)], r3z.at[k - 1], p3_send.at[1], p3z_recv.at[k - 1], dev(yy=ys(k))).start()

    base = NX + NY - 1
    for k in yd:
        wait_recv(cnt_in.at[NX - 1 + k], cnt_recv.at[NX - 1 + k])
    cnt[3] = cnt[2] + cnt_in[NX] + cnt_in[NX + 1] + cnt_in[NX + 2]
    for e, f in zd:
        slot = base + e * NL + f - 1
        remote(cnt.at[3], cnt_in.at[slot], cnt_send.at[3], cnt_recv.at[slot], dev(hh=hs(e), ll=ls(f))).start()

    for k in range(1, NZ):
        wait_recv(r3a.at[k - 1], p3a_recv.at[k - 1])
    sum_a = s3a[h, l].astype(F32)
    for k in range(1, NZ):
        sum_a += r3a[k - 1].astype(F32)
    for k in yd:
        wait_recv(r3z.at[k - 1], p3z_recv.at[k - 1])
    sum_z = s3z[y].astype(F32)
    for k in yd:
        sum_z += r3z[k - 1].astype(F32)
    for k in range(1, NZ):
        wait_recv(cnt_in.at[base + k - 1], cnt_recv.at[base + k - 1])
    count = cnt[3]
    for k in range(1, NZ):
        count += cnt_in[base + k - 1]
    count = count[0:1, 0:1]

    pending += [(r3a, p3_send.at[0]), (r3z, p3_send.at[1]), (cnt_in.at[pl.ds(0, NZ - 1)], cnt_send.at[3])]

    for copy in adam_copies:
        copy.wait()

    def adam(cols, summed):
        grad = summed / count
        new_first = 0.9 * first[:, cols] + 0.1 * grad
        new_second = 0.95 * second[:, cols] + 0.05 * grad * grad
        update = new_first / (1.0 - 0.9**STEP) / (jnp.sqrt(new_second / (1.0 - 0.95**STEP)) + 1e-08)
        new_master = master[:, cols] - 0.001 * (update + 0.1 * master[:, cols])
        o_first[:, cols] = new_first
        o_second[:, cols] = new_second
        o_master[:, cols] = new_master
        w[h, y, x, l, c, :, cols] = new_master.astype(BF16)

    adam(colxy, sum_a)
    adam(colz, sum_z)

    def gather(ref, send, recv, to):
        remote(ref, ref, send, recv, to).start()

    for e, f in zd:
        gather(w.at[h, y, x, l, c, :, colxy], a3_send.at[0], a3a_recv.at[e * NL + f - 1], dev(hh=hs(e), ll=ls(f)))
    for k in yd:
        gather(w.at[h, y, x, l, c, :, colz], a3_send.at[1], a3z_recv.at[k - 1], dev(yy=ys(k)))
    for k in range(1, NZ):
        wait_recv(r3a.at[k - 1], a3a_recv.at[k - 1])
    for k in yd:
        gather(w.at[:, y, x, :, c, :, colx], a2_send.at[0], a2x_recv.at[k - 1], dev(yy=ys(k)))
    for k in xd:
        gather(w.at[:, y, x, :, c, :, coly], a2_send.at[1], a2y_recv.at[k - 1], dev(xx=xs(k)))
    for k in yd:
        wait_recv(r3z.at[k - 1], a3z_recv.at[k - 1])
    for k in xd:
        gather(w.at[h, :, x, l, c, :, colz], a2_send.at[2], a2z_recv.at[k - 1], dev(xx=xs(k)))

    def xpart(k, hh):
        return w.at[hh, :, xs(k), :, c, :, colx]

    def ypart(k, hh):
        return w.at[hh, ys(k), :, :, c, :, coly]

    def zpart(k):
        hh, ll = zat(k)
        return w.at[hh, :, :, ll, c, :, colz]

    def zhalf(k, i):
        hh, ll = zat(k)
        return w.at[hh, pl.ds(i * (NY // 2), NY // 2), :, ll, c, :, colz]

    pending += [(r3a, a3_send.at[0]), (r3z, a3_send.at[1])]
    pending += [(r2x, a2_send.at[0]), (r2y, a2_send.at[1]), (r2z, a2_send.at[2])]

    def send_x(part, turn):
        for i in range(2):
            to = 1 + 2 * i if turn == 0 else 3 - 2 * i
            gather(w.at[i, part, x, :, c, :, colx], a1_send.at[0], a1x_recv.at[i, turn], dev(xx=xs(to)))

    def send_y(part, turn):
        for i in range(2):
            to = 1 + 2 * i if turn == 0 else 3 - 2 * i
            gather(w.at[i, y, part, :, c, :, coly], a1_send.at[2], a1y_recv.at[i, turn], dev(yy=ys(to)))

    def send_z(part, turn):
        for i in range(2):
            to = (2 - turn) * (1 - 2 * i)
            gather(w.at[h, :, part, l, c, :, colz], a1_send.at[4], a1z_recv.at[2 * turn + i], zdev(to))

    for turn in range(2):
        send_x(y, turn)
        send_y(x, turn)
        send_z(x, turn)
    for k in (1, 3, 2):
        wait_recv(r2x.at[k - 1], a2x_recv.at[k - 1])
        send_x(ys(NY - k), 0)
        wait_recv(r2y.at[k - 1], a2y_recv.at[k - 1])
        send_y(xs(NX - k), 0)
        wait_recv(r2z.at[k - 1], a2z_recv.at[k - 1])
        send_z(xs(NX - k), 0)
    for k in (1, 3, 2):
        send_x(ys(NY - k), 1)
        send_y(xs(NX - k), 1)
        send_z(xs(NX - k), 1)
    for i in range(2):
        gather(xpart(0, i), f_send.at[0], fx_recv.at[0], sib)
        gather(ypart(0, i), f_send.at[1], fy_recv.at[0], sib)
    gather(zpart(0), f_send.at[2], fz_recv.at[0], sib)

    for i in range(2):
        wait_recv(m1x.at[0], a1x_recv.at[i, 0])
        gather(xpart(3 - 2 * i, i), a1_send.at[1], a1x_recv.at[i, 2], dev(xx=xs(1 + 2 * i)))
        wait_recv(m1y.at[0], a1y_recv.at[i, 0])
        gather(ypart(3 - 2 * i, i), a1_send.at[3], a1y_recv.at[i, 2], dev(yy=ys(1 + 2 * i)))
    for i, k in enumerate((-2, 2)):
        wait_recv(r1z.at[0], a1z_recv.at[i])
        gather(zhalf(k, i), a1_send.at[5], a1z_recv.at[4 + i], zdev(-k))
        gather(zpart(k), a1_send.at[5], a1z_recv.at[6 + i], zdev(-k // 2))
    for i in range(2):
        gather(xpart(3 - 2 * i, i), f_send.at[0], fx_recv.at[3 - 2 * i], sib)
        gather(ypart(3 - 2 * i, i), f_send.at[1], fy_recv.at[3 - 2 * i], sib)
    for k in (-2, 2):
        gather(zpart(k), f_send.at[2], fz_recv.at[0], sib)

    pending += [(r1x, a1_send.at[0]), (r1x.at[0], a1_send.at[1]), (r1y, a1_send.at[2]), (r1y.at[0], a1_send.at[3])]
    pending += [(r1z.at[pl.ds(0, 4)], a1_send.at[4]), (r1z.at[pl.ds(0, 3)], a1_send.at[5])]
    pending += [(w.at[:, :, :, :, c, :, cols], f_send.at[i]) for i, cols in enumerate((colx, coly, colz))]

    def project_x(k):
        for hh in range(NH):
            lhs = jnp.concatenate([nxt[(hh * NY + yy) * NX + xs(k)] for yy in range(NY)], axis=1)
            rhs = w[hh, :, xs(k), :, :, :, colx].reshape(NY * NL * NC * rows, ca)
            acc[:, colx] += jnp.dot(lhs, rhs, preferred_element_type=F32)

    def project_y(k):
        for hh in range(NH):
            lhs = jnp.concatenate([nxt[(hh * NY + ys(k)) * NX + xx] for xx in range(NX)], axis=1)
            rhs = w[hh, ys(k), :, :, :, :, coly].reshape(NX * NL * NC * rows, cb - ca)
            acc[:, coly] += jnp.dot(lhs, rhs, preferred_element_type=F32)

    acc[...] = jnp.zeros_like(acc)

    @pl.loop(0, NH * NY * NX)
    def _(i):
        nxt_copy(i).wait()

    wait_recv(r1x.at[0], fx_recv.at[0])
    project_x(0)
    for i in range(2):
        wait_recv(m1x.at[0], a1x_recv.at[i, 1])
        gather(xpart(1 + 2 * i, i), f_send.at[0], fx_recv.at[1 + 2 * i], sib)
        wait_recv(m1y.at[0], a1y_recv.at[i, 1])
        gather(ypart(1 + 2 * i, i), f_send.at[1], fy_recv.at[1 + 2 * i], sib)
    wait_recv(r1y.at[0], fy_recv.at[0])
    project_y(0)
    for i, k in enumerate((-1, 1)):
        wait_recv(r1z.at[0], a1z_recv.at[2 + i])
        gather(zpart(k), f_send.at[2], fz_recv.at[0], sib)
    for k in (1, 3):
        wait_recv(r1x.at[0], fx_recv.at[k])
        project_x(k)
        wait_recv(r1y.at[0], fy_recv.at[k])
        project_y(k)
    for i in range(2):
        wait_recv(m1x.at[0], a1x_recv.at[i, 2])
        gather(xpart(2, i), f_send.at[0], fx_recv.at[2], sib)
        wait_recv(m1y.at[0], a1y_recv.at[i, 2])
        gather(ypart(2, i), f_send.at[1], fy_recv.at[2], sib)
    for i, k in enumerate((-3, 3)):
        wait_recv(r1z.at[0], a1z_recv.at[6 + i])
        gather(zpart(k), f_send.at[2], fz_recv.at[0], sib)
    for i in range(2):
        wait_recv(r1z.at[0, pl.ds(0, NY // 2)], a1z_recv.at[4 + i])
        gather(zhalf(4, i), f_send.at[2], fz_recv.at[0], sib)
    sec_copy = pltpu.make_async_copy(w.at[:, :, :, l, c], o_sec, out_sem.at[0])
    sec_copy.start()
    wait_recv(r1x.at[0], fx_recv.at[2])
    project_x(2)
    o_proj[:, colx] = acc[:, colx].astype(BF16)
    wait_recv(r1y.at[0], fy_recv.at[2])
    project_y(2)
    o_proj[:, coly] = acc[:, coly].astype(BF16)
    wait_recv(w.at[:, :, :, :, 1 - c, :, colz], fz_recv.at[0])

    @pl.loop(0, NH)
    def _(hh):
        lhs = jnp.concatenate([nxt[hh * NY * NX + i] for i in range(NY * NX)], axis=1)
        rhs = w[hh, :, :, :, :, :, colz].reshape(NY * width, kv - cb)
        acc[:, colz] += jnp.dot(lhs, rhs, preferred_element_type=F32)

    o_proj[:, colz] = acc[:, colz].astype(BF16)
    sec_copy.wait()

    drain()


def copy_out(*refs):
    src, dst, sem = refs[:5], refs[5:10], refs[10]
    copies = []
    for i in range(5):
        n, rows = PARTS[i], src[i].shape[0]
        for j in range(n):
            part = pl.ds(j * rows // n, rows // n)
            copies.append(pltpu.make_async_copy(src[i].at[part], dst[i].at[part], sem.at[len(copies)]))
    for copy in copies:
        copy.start()
    for copy in copies:
        copy.wait()


def body(tokens, out_grad, next_tokens, overflow, master, first_moment, second_moment):
    toks, din = tokens.shape
    rows, kv = master.shape
    ca, cb = 3 * kv // 8, 6 * kv // 8
    cx, cy, cz = ca, cb - ca, kv - cb
    width = NX * NL * NC * rows
    vmem, anym = pl.BlockSpec(memory_space=pltpu.VMEM), pl.BlockSpec(memory_space=pl.ANY)
    dma = pltpu.SemaphoreType.DMA
    shapes = (
        jax.ShapeDtypeStruct((rows, kv), F32),
        jax.ShapeDtypeStruct((rows, kv), F32),
        jax.ShapeDtypeStruct((rows, kv), F32),
        jax.ShapeDtypeStruct((NH, NY, NX, rows, kv), BF16),
        jax.ShapeDtypeStruct((toks, kv), BF16),
    )
    scratch = [
        pltpu.SMEM((1,), jnp.int32),
        pltpu.VMEM((rows, kv), F32),
        pltpu.VMEM((rows, kv), F32),
        pltpu.VMEM((rows, kv), F32),
        pltpu.VMEM((NH * NY, toks, width), BF16),
        pltpu.VMEM((toks, kv), BF16),
        pltpu.VMEM((NH * NY * NX, toks, NL * NC * rows), BF16),
        pltpu.VMEM((NH, NY, NX, NL, rows, kv), F32),
        pltpu.VMEM((NH, NY, NX, NL, rows, kv), BF16),
        pltpu.VMEM((NH, NY, NX, NL, rows, kv), BF16),
        pltpu.VMEM((NH, NY, NX, NL, rows, kv), BF16),
        pltpu.VMEM((NH, NY, NL, rows, cx), BF16),
        pltpu.VMEM((NH, NX, NL, rows, cy), BF16),
        pltpu.VMEM((NH, NY, NL, rows, cx), BF16),
        pltpu.VMEM((NH, NX, NL, rows, cy), BF16),
        pltpu.VMEM((2, NY, NX, rows, cz), BF16),
        pltpu.VMEM((2, NH, NY, NL, rows, cx), BF16),
        pltpu.VMEM((2, NH, NX, NL, rows, cy), BF16),
        pltpu.VMEM((7, NY, NX, rows, cz), BF16),
        pltpu.VMEM((NH, NY, NL, rows, cx), BF16),
        pltpu.VMEM((NH, NX, NL, rows, cy), BF16),
        pltpu.VMEM((NY, NX, rows, cz), BF16),
        pltpu.VMEM((NY - 1, NH, NL, rows, cx), BF16),
        pltpu.VMEM((NX - 1, NH, NL, rows, cy), BF16),
        pltpu.VMEM((NX - 1, NY, rows, cz), BF16),
        pltpu.VMEM((NH, NL, rows, cx + cy), BF16),
        pltpu.VMEM((NY, rows, cz), BF16),
        pltpu.VMEM((NZ - 1, rows, cx + cy), BF16),
        pltpu.VMEM((NY - 1, rows, cz), BF16),
        pltpu.VMEM((4, 8, 128), F32),
        pltpu.VMEM((1 + NX - 1 + NY - 1 + NZ - 1, 8, 128), F32),
        pltpu.VMEM((NH, NY, NX, NL, NC, rows, kv), BF16),
        pltpu.VMEM((toks, kv), F32),
    ]
    sems = (
        [(5,), (NH * NY,), (NH * NY * NX,), (1,), (1,), (NH * NY,), (4,), (NX + NY + NZ - 2,)]
        + [(8,), (NH, NY), (NH,), (2,), (2,), (7,)]
        + [(3,), (NY - 1,), (NX - 1,), (NX - 1,)]
        + [(2,), (NZ - 1,), (NY - 1,)]
        + [(2,), (NZ - 1,), (NY - 1,)]
        + [(3,), (NY - 1,), (NX - 1,), (NX - 1,)]
        + [(6,), (2, 3), (2, 3), (8,)]
        + [(3,), (NX,), (NY,), (1,)]
    )
    results = pl.pallas_call(
        kernel,
        out_shape=[pltpu.VMEM(shape.shape, shape.dtype) for shape in shapes],
        in_specs=[anym] * 7,
        out_specs=[vmem] * 5,
        scratch_shapes=scratch + [dma(n) for n in sems],
        compiler_params=pltpu.CompilerParams(
            collective_id=0, has_side_effects=True, vmem_limit_bytes=56 * 2**20
        ),
        cost_estimate=pl.CostEstimate(flops=4 * toks * din * kv, bytes_accessed=12 * 2**20, transcendentals=rows * kv),
    )(overflow, tokens, out_grad, next_tokens, master, first_moment, second_moment)
    new_master, new_first, new_second, sec, proj = pl.pallas_call(
        copy_out,
        out_shape=shapes,
        in_specs=[vmem] * 5,
        out_specs=[anym] * 5,
        scratch_shapes=[dma((sum(PARTS),))],
        compiler_params=pltpu.CompilerParams(vmem_limit_bytes=8 * 2**20),
    )(*results)
    return (new_master, new_first, new_second, sec.reshape(NH * NY * NX, rows, kv), proj)


def solution(mesh):
    return jax.shard_map(
        body,
        mesh=mesh,
        in_specs=(
            P(("node", "local"), None),
            P(("node", "local"), None),
            P(("node", "local"), None),
            P(("node", "local")),
            P(("node", "local"), None),
            P(("node", "local"), None),
            P(("node", "local"), None),
        ),
        out_specs=(
            P(("node", "local"), None),
            P(("node", "local"), None),
            P(("node", "local"), None),
            P(None, "local", None),
            P(("node", "local"), None),
        ),
        check_vma=False,
    )
```

```python
import functools

import jax
import jax.numpy as jnp
from jax import lax
from jax.experimental import pallas as pl
from jax.experimental.pallas import tpu as pltpu
from jax.sharding import PartitionSpec as P

STEP = 10
MESH = pl.DeviceIdType.MESH
NH, NY, NX, NL, NC = 2, 4, 4, 4, 2
NZ = NH * NL
LAG = 2
PARTS = (1, 1, 1, 2, 2)
F32, BF16 = jnp.float32, jnp.bfloat16


def kernel(
    ov_hbm, tok_hbm, og_hbm, nxt_hbm, master_hbm, first_hbm, second_hbm,
    o_master, o_first, o_second, o_sec, o_proj,
    ov, master, first, second, tok, og, nxt, own, sib_out, sib_in, s1,
    m1x, m1y, f1x, f1y, f1z, r1x, r1y, r1z, s2x, s2y, s2z, r2x, r2y, r2z, s3a, s3z, r3a, r3z,
    cnt, cnt_in, w, acc,
    in_sem, tok_sem, nxt_sem, out_sem, sib_send, sib_recv, cnt_send, cnt_recv,
    p1_send, m1x_recv, m1y_recv, p1x_recv, p1y_recv, p1z_recv,
    p2_send, p2x_recv, p2y_recv, p2z_recv, p3_send, p3a_recv, p3z_recv,
    a3_send, a3a_recv, a3z_recv, a2_send, a2x_recv, a2y_recv, a2z_recv,
    a1_send, a1x_recv, a1y_recv, a1z_recv, f_send, fx_recv, fy_recv, fz_recv,
):
    rows, kv = master.shape
    ca, cb = r1x.shape[-1], r1x.shape[-1] + r1y.shape[-1]
    colx, coly, colz, colxy = pl.ds(0, ca), pl.ds(ca, cb - ca), pl.ds(cb, kv - cb), pl.ds(0, cb)
    node, loc = lax.axis_index("node"), lax.axis_index("local")
    x, y, h = lax.rem(node, NX), lax.rem(lax.div(node, NX), NY), lax.div(node, NX * NY)
    c, l = lax.rem(loc, NC), lax.div(loc, NC)

    def dev(hh=h, yy=y, xx=x, ll=l, cc=c):
        return ((hh * NY + yy) * NX + xx, ll * NC + cc)

    def xs(d):
        return lax.rem(x + d, NX)

    def ys(d):
        return lax.rem(y + d, NY)

    def hs(e):
        return lax.rem(h + e, NH)

    def ls(f):
        return lax.rem(l + f, NL)

    def zdev(k):
        zz = lax.rem(h * NL + l + k + NZ, NZ)
        return dev(hh=lax.div(zz, NL), ll=lax.rem(zz, NL))

    def zat(k):
        zz = lax.rem(h * NL + l + k + NZ, NZ)
        return lax.div(zz, NL), lax.rem(zz, NL)

    xd = yd = (2, 1, 3)
    zd = [(1, f) for f in range(NL)] + [(0, f) for f in range(1, NL)]
    sib = dev(cc=1 - c)

    def remote(src, dst, send, recv, to):
        return pltpu.make_async_remote_copy(
            src_ref=src, dst_ref=dst, send_sem=send, recv_sem=recv, device_id=to, device_id_type=MESH
        )

    def wait_recv(ref, sem):
        remote(ref, ref, sem, sem, sib).wait_recv()

    def wait_send(ref, sem):
        remote(ref, ref, sem, sem, sib).wait_send()

    pending = []

    def drain():
        for ref, sem in pending:
            wait_send(ref, sem)

    peers = [sib]
    peers += [dev(xx=xs(d)) for d in xd] + [dev(yy=ys(d)) for d in yd]
    peers += [dev(hh=hs(e), ll=ls(f)) for e, f in zd]
    barrier = pltpu.get_barrier_semaphore()
    for to in peers:
        pl.semaphore_signal(barrier, inc=1, device_id=to, device_id_type=MESH)

    og_copy = pltpu.make_async_copy(og_hbm, og, in_sem.at[0])

    def nxt_copy(i):
        cols = pl.ds(pl.multiple_of(i * NL * NC * rows, NL * NC * rows), NL * NC * rows)
        return pltpu.make_async_copy(nxt_hbm.at[:, cols], nxt.at[i], nxt_sem.at[i])

    ov_copy = pltpu.make_async_copy(ov_hbm, ov, in_sem.at[1])
    adam_copies = [
        pltpu.make_async_copy(src, dst, in_sem.at[2 + i])
        for i, (src, dst) in enumerate(((master_hbm, master), (first_hbm, first), (second_hbm, second)))
    ]
    ov_copy.start()
    og_copy.start()
    width = NX * NL * NC * rows
    steps = NH * NY

    def place(it):
        e, d = lax.rem(it, NH), lax.rem(2 + NY - lax.div(it, NH), NY)
        return e, d, hs(e), ys(d)

    def tok_copy(it):
        _, _, hh, yy = place(it)
        cols = pl.ds(pl.multiple_of((hh * NY + yy) * width, width), width)
        return pltpu.make_async_copy(tok_hbm.at[:, cols], tok.at[it], tok_sem.at[it])

    def start_tok(it):
        tok_copy(it).start()

    pl.loop(0, LAG)(start_tok)
    og_copy.wait()
    pl.loop(LAG, steps)(start_tok)
    ov_copy.wait()
    kept = (1 - ov[0]).astype(F32)
    og[...] = og[...] * kept.astype(BF16)
    cnt[0] = jnp.full(cnt.shape[1:], kept, F32)

    def partial_sum(it):
        _, _, hh, yy = place(it)
        tok_copy(it).wait()
        part = lax.dot_general(tok[it], og[...], (((0,), (0,)), ((), ())), preferred_element_type=F32)
        part = part.reshape(NX, NL, NC, rows, kv)
        even, odd = part[:, :, 0], part[:, :, 1]
        own[hh, yy] = jnp.where(c == 0, even, odd)
        sib_out[hh, yy] = jnp.where(c == 0, odd, even).astype(BF16)

    def send_partial(it):
        _, _, hh, yy = place(it)
        remote(sib_out.at[hh, yy], sib_in.at[hh, yy], sib_send.at[0], sib_recv.at[it], sib).start()

    pl.loop(0, LAG)(partial_sum)
    pl.semaphore_wait(barrier, len(peers))
    remote(cnt.at[0], cnt_in.at[0], cnt_send.at[0], cnt_recv.at[0], sib).start()
    pl.loop(0, LAG)(send_partial)

    def exchange_first(it):
        e, d, hh, yy = place(it)
        wait_recv(sib_in.at[hh, yy], sib_recv.at[it])
        s1[hh, yy] = (own[hh, yy] + sib_in[hh, yy].astype(F32)).astype(BF16)
        go, back = 1 + 2 * hh, NX - 1 - 2 * hh
        remote(
            s1.at[hh, yy, xs(2), :, :, colx], m1x.at[hh, yy], p1_send.at[0], m1x_recv.at[hh, yy], dev(xx=xs(go))
        ).start()
        remote(
            s1.at[hh, yy, xs(back), :, :, colx], r1x.at[0, hh, yy], p1_send.at[1], p1x_recv.at[0], dev(xx=xs(back))
        ).start()

        @pl.when(d == 2)
        def _():
            remote(
                s1.at[hh, yy, :, :, :, coly], m1y.at[hh], p1_send.at[3], m1y_recv.at[hh], dev(yy=ys(go))
            ).start()

        @pl.when(d == back)
        def _():
            remote(
                s1.at[hh, yy, :, :, :, coly], r1y.at[0, hh], p1_send.at[4], p1y_recv.at[0], dev(yy=ys(back))
            ).start()

        @pl.loop(0, NL, unroll=True)
        def _(ll):
            k = lax.rem(hh * NL + ll + NZ - h * NL - l, NZ)
            up = k < 4
            odd = lax.rem(k, 2) == 1
            slot = jnp.where(odd, jnp.where((k == 1) | (k == 7), 0, 2) + jnp.where(up, 0, 1), 4)
            hop = jnp.where(odd, jnp.where(up, 1, NZ - 1), jnp.where(yy < NY // 2, 2, NZ - 2))

            @pl.when(odd | (k == 4))
            def _():
                remote(
                    s1.at[hh, yy, :, ll, :, colz], r1z.at[slot, yy], p1_send.at[6], p1z_recv.at[slot], zdev(hop)
                ).start()

    @pl.loop(LAG, steps)
    def _(it):
        partial_sum(it)
        send_partial(it)
        exchange_first(it - LAG)

    pl.loop(steps - LAG, steps)(exchange_first)

    wait_recv(cnt_in.at[0], cnt_recv.at[0])
    cnt[1] = cnt[0] + cnt_in[0]
    for k in xd:
        remote(cnt.at[1], cnt_in.at[k], cnt_send.at[1], cnt_recv.at[k], dev(xx=xs(k))).start()

    pending += [(sib_out, sib_send.at[0]), (cnt.at[0], cnt_send.at[0]), (cnt_in.at[pl.ds(0, NX - 1)], cnt_send.at[1])]
    pending += [(m1x, p1_send.at[0]), (r1x.at[0], p1_send.at[1]), (m1y, p1_send.at[3]), (r1y.at[0], p1_send.at[4])]
    pending += [(r1z.at[pl.ds(0, 5)], p1_send.at[6])]

    def relay_x(it):
        _, _, hh, yy = place(it)
        go = 1 + 2 * hh
        wait_recv(m1x.at[hh, yy], m1x_recv.at[hh, yy])
        f1x[hh, yy] = (s1[hh, yy, xs(go), :, :, colx].astype(F32) + m1x[hh, yy].astype(F32)).astype(BF16)
        remote(f1x.at[hh, yy], r1x.at[1, hh, yy], p1_send.at[2], p1x_recv.at[1], dev(xx=xs(go))).start()

    @pl.loop(0, NH)
    def _(hh):
        go = 1 + 2 * hh
        wait_recv(m1y.at[hh], m1y_recv.at[hh])

        @pl.loop(0, NX)
        def _(xx):
            f1y[hh, xx] = (s1[hh, ys(go), xx, :, :, coly].astype(F32) + m1y[hh, xx].astype(F32)).astype(BF16)

        remote(f1y.at[hh], r1y.at[1, hh], p1_send.at[5], p1y_recv.at[1], dev(yy=ys(go))).start()

    pl.loop(0, steps - LAG)(relay_x)

    for slot in (2, 3, 4):
        wait_recv(r1z.at[slot], p1z_recv.at[slot])
    for i, k in ((0, 2), (1, NZ - 2)):
        hh, ll = zat(k)
        for yy in range(NY):
            total = s1[hh, yy, :, ll, :, colz].astype(F32) + r1z[2 + i, yy].astype(F32)
            if (yy < NY // 2) == (i == 0):
                total += r1z[4, yy].astype(F32)
            f1z[i, yy] = total.astype(BF16)
        remote(f1z.at[i], r1z.at[5 + i], p1_send.at[7], p1z_recv.at[5 + i], zdev(k)).start()

    pl.loop(steps - LAG, steps)(relay_x)

    pending += [(f1x, p1_send.at[2]), (f1y, p1_send.at[5]), (f1z, p1_send.at[7])]

    @pl.loop(0, NH * NY * NX)
    def _(i):
        nxt_copy(i).start()

    for copy in adam_copies:
        copy.start()

    for k in range(2):
        wait_recv(r1x.at[k], p1x_recv.at[k])

    @pl.loop(0, NH * NY)
    def _(i):
        hh, yy = lax.div(i, NY), lax.rem(i, NY)
        total = s1[hh, yy, x, :, :, colx].astype(F32)
        for k in range(2):
            total += r1x[k, hh, yy].astype(F32)
        s2x[hh, yy] = total.astype(BF16)

    for k in yd:
        remote(s2x.at[:, ys(k)], r2x.at[k - 1], p2_send.at[0], p2x_recv.at[k - 1], dev(yy=ys(k))).start()

    for k in range(2):
        wait_recv(r1y.at[k], p1y_recv.at[k])

    @pl.loop(0, NH * NX)
    def _(i):
        hh, xx = lax.div(i, NX), lax.rem(i, NX)
        total = s1[hh, y, xx, :, :, coly].astype(F32)
        for k in range(2):
            total += r1y[k, hh, xx].astype(F32)
        s2y[hh, xx] = total.astype(BF16)

    for k in xd:
        remote(s2y.at[:, xs(k)], r2y.at[k - 1], p2_send.at[1], p2y_recv.at[k - 1], dev(xx=xs(k))).start()

    for k in (0, 1, 5, 6):
        wait_recv(r1z.at[k], p1z_recv.at[k])

    @pl.loop(0, NY)
    def _(yy):
        total = s1[h, yy, :, l, :, colz].astype(F32)
        for k in (0, 1, 5, 6):
            total += r1z[k, yy].astype(F32)
        s2z[yy] = total.astype(BF16)

    for k in xd:
        remote(s2z.at[:, xs(k)], r2z.at[k - 1], p2_send.at[2], p2z_recv.at[k - 1], dev(xx=xs(k))).start()

    for k in xd:
        wait_recv(cnt_in.at[k], cnt_recv.at[k])
    cnt[2] = cnt[1] + cnt_in[1] + cnt_in[2] + cnt_in[3]
    for k in yd:
        remote(cnt.at[2], cnt_in.at[NX - 1 + k], cnt_send.at[2], cnt_recv.at[NX - 1 + k], dev(yy=ys(k))).start()

    pending += [(r2x, p2_send.at[0]), (r2y, p2_send.at[1]), (r2z, p2_send.at[2])]
    pending += [(cnt_in.at[pl.ds(0, NY - 1)], cnt_send.at[2])]

    for k in yd:
        wait_recv(r2x.at[k - 1], p2x_recv.at[k - 1])
    total = s2x[:, y].astype(F32)
    for k in yd:
        total += r2x[k - 1].astype(F32)
    s3a[:, :, :, colx] = total.astype(BF16)
    for k in xd:
        wait_recv(r2y.at[k - 1], p2y_recv.at[k - 1])
    total = s2y[:, x].astype(F32)
    for k in xd:
        total += r2y[k - 1].astype(F32)
    s3a[:, :, :, coly] = total.astype(BF16)
    for e, f in zd:
        slot = e * NL + f - 1
        remote(
            s3a.at[hs(e), ls(f)], r3a.at[slot], p3_send.at[0], p3a_recv.at[slot], dev(hh=hs(e), ll=ls(f))
        ).start()
    for k in xd:
        wait_recv(r2z.at[k - 1], p2z_recv.at[k - 1])
    total = s2z[:, x].astype(F32)
    for k in xd:
        total += r2z[k - 1].astype(F32)
    s3z[...] = total.astype(BF16)
    for k in yd:
        remote(s3z.at[ys(k)], r3z.at[k - 1], p3_send.at[1], p3z_recv.at[k - 1], dev(yy=ys(k))).start()

    base = NX + NY - 1
    for k in yd:
        wait_recv(cnt_in.at[NX - 1 + k], cnt_recv.at[NX - 1 + k])
    cnt[3] = cnt[2] + cnt_in[NX] + cnt_in[NX + 1] + cnt_in[NX + 2]
    for e, f in zd:
        slot = base + e * NL + f - 1
        remote(cnt.at[3], cnt_in.at[slot], cnt_send.at[3], cnt_recv.at[slot], dev(hh=hs(e), ll=ls(f))).start()

    for k in range(1, NZ):
        wait_recv(r3a.at[k - 1], p3a_recv.at[k - 1])
    sum_a = s3a[h, l].astype(F32)
    for k in range(1, NZ):
        sum_a += r3a[k - 1].astype(F32)
    for k in yd:
        wait_recv(r3z.at[k - 1], p3z_recv.at[k - 1])
    sum_z = s3z[y].astype(F32)
    for k in yd:
        sum_z += r3z[k - 1].astype(F32)
    for k in range(1, NZ):
        wait_recv(cnt_in.at[base + k - 1], cnt_recv.at[base + k - 1])
    count = cnt[3]
    for k in range(1, NZ):
        count += cnt_in[base + k - 1]
    count = count[0:1, 0:1]

    pending += [(r3a, p3_send.at[0]), (r3z, p3_send.at[1]), (cnt_in.at[pl.ds(0, NZ - 1)], cnt_send.at[3])]

    for copy in adam_copies:
        copy.wait()

    def adam(cols, summed):
        grad = summed / count
        new_first = 0.9 * first[:, cols] + 0.1 * grad
        new_second = 0.95 * second[:, cols] + 0.05 * grad * grad
        update = new_first / (1.0 - 0.9**STEP) / (jnp.sqrt(new_second / (1.0 - 0.95**STEP)) + 1e-08)
        new_master = master[:, cols] - 0.001 * (update + 0.1 * master[:, cols])
        o_first[:, cols] = new_first
        o_second[:, cols] = new_second
        o_master[:, cols] = new_master
        w[h, y, x, l, c, :, cols] = new_master.astype(BF16)

    adam(colxy, sum_a)
    adam(colz, sum_z)

    def gather(ref, send, recv, to):
        remote(ref, ref, send, recv, to).start()

    for k in yd:
        gather(w.at[h, y, x, l, c, :, colz], a3_send.at[1], a3z_recv.at[k - 1], dev(yy=ys(k)))
    for e, f in zd:
        gather(w.at[h, y, x, l, c, :, colxy], a3_send.at[0], a3a_recv.at[e * NL + f - 1], dev(hh=hs(e), ll=ls(f)))
    for k in yd:
        wait_recv(r3z.at[k - 1], a3z_recv.at[k - 1])
    for k in xd:
        gather(w.at[h, :, x, l, c, :, colz], a2_send.at[2], a2z_recv.at[k - 1], dev(xx=xs(k)))
    for k in range(1, NZ):
        wait_recv(r3a.at[k - 1], a3a_recv.at[k - 1])
    for k in yd:
        gather(w.at[:, y, x, :, c, :, colx], a2_send.at[0], a2x_recv.at[k - 1], dev(yy=ys(k)))
    for k in xd:
        gather(w.at[:, y, x, :, c, :, coly], a2_send.at[1], a2y_recv.at[k - 1], dev(xx=xs(k)))

    def xpart(k, hh):
        return w.at[hh, :, xs(k), :, c, :, colx]

    def ypart(k, hh):
        return w.at[hh, ys(k), :, :, c, :, coly]

    def zpart(k):
        hh, ll = zat(k)
        return w.at[hh, :, :, ll, c, :, colz]

    def zhalf(k, i):
        hh, ll = zat(k)
        return w.at[hh, pl.ds(i * (NY // 2), NY // 2), :, ll, c, :, colz]

    pending += [(r3a, a3_send.at[0]), (r3z, a3_send.at[1])]
    pending += [(r2x, a2_send.at[0]), (r2y, a2_send.at[1]), (r2z, a2_send.at[2])]

    def send_x(part, turn):
        for i in range(2):
            to = 1 + 2 * i if turn == 0 else 3 - 2 * i
            gather(w.at[i, part, x, :, c, :, colx], a1_send.at[0], a1x_recv.at[i, turn], dev(xx=xs(to)))

    def send_y(part, turn):
        for i in range(2):
            to = 1 + 2 * i if turn == 0 else 3 - 2 * i
            gather(w.at[i, y, part, :, c, :, coly], a1_send.at[2], a1y_recv.at[i, turn], dev(yy=ys(to)))

    def send_z(part, turn):
        for i in range(2):
            to = (2 - turn) * (1 - 2 * i)
            gather(w.at[h, :, part, l, c, :, colz], a1_send.at[4], a1z_recv.at[2 * turn + i, part], zdev(to))

    for turn in range(2):
        send_x(y, turn)
        send_y(x, turn)
        send_z(x, turn)
    for k in (1, 3, 2):
        wait_recv(r2z.at[k - 1], a2z_recv.at[k - 1])
        send_z(xs(NX - k), 0)
    for k in (1, 3, 2):
        wait_recv(r2x.at[k - 1], a2x_recv.at[k - 1])
        send_x(ys(NY - k), 0)
        wait_recv(r2y.at[k - 1], a2y_recv.at[k - 1])
        send_y(xs(NX - k), 0)
    for k in (1, 3, 2):
        send_x(ys(NY - k), 1)
        send_y(xs(NX - k), 1)
        send_z(xs(NX - k), 1)
    for i in range(2):
        gather(xpart(0, i), f_send.at[0], fx_recv.at[0], sib)
        gather(ypart(0, i), f_send.at[1], fy_recv.at[0], sib)
    gather(zpart(0), f_send.at[2], fz_recv.at[0], sib)

    def relay_z(part):
        for i, k in enumerate((-2, 2)):
            wait_recv(r1z.at[0, :, 0], a1z_recv.at[i, part])
            hh, ll = zat(k)
            gather(w.at[hh, :, part, ll, c, :, colz], a1_send.at[5], a1z_recv.at[6 + i, 0], zdev(-k // 2))
            half = pl.ds(i * (NY // 2), NY // 2)
            gather(w.at[hh, half, part, ll, c, :, colz], a1_send.at[5], a1z_recv.at[4 + i, 0], zdev(-k))

    relay_z(x)
    relay_z(xs(NX - 1))
    relay_z(xs(NX - 3))
    relay_z(xs(NX - 2))
    for i in range(2):
        wait_recv(m1x.at[0], a1x_recv.at[i, 0])
        gather(xpart(3 - 2 * i, i), a1_send.at[1], a1x_recv.at[i, 2], dev(xx=xs(1 + 2 * i)))
        wait_recv(m1y.at[0], a1y_recv.at[i, 0])
        gather(ypart(3 - 2 * i, i), a1_send.at[3], a1y_recv.at[i, 2], dev(yy=ys(1 + 2 * i)))
    for i in range(2):
        gather(xpart(3 - 2 * i, i), f_send.at[0], fx_recv.at[3 - 2 * i], sib)
        gather(ypart(3 - 2 * i, i), f_send.at[1], fy_recv.at[3 - 2 * i], sib)
    for k in (-2, 2):
        gather(zpart(k), f_send.at[2], fz_recv.at[0], sib)

    pending += [(r1x, a1_send.at[0]), (r1x.at[0], a1_send.at[1]), (r1y, a1_send.at[2]), (r1y.at[0], a1_send.at[3])]
    pending += [(r1z.at[pl.ds(0, 4)], a1_send.at[4]), (r1z.at[pl.ds(0, 3)], a1_send.at[5])]
    pending += [(w.at[:, :, :, :, c, :, cols], f_send.at[i]) for i, cols in enumerate((colx, coly, colz))]

    def project_x(k):
        for hh in range(NH):
            lhs = jnp.concatenate([nxt[(hh * NY + yy) * NX + xs(k)] for yy in range(NY)], axis=1)
            rhs = w[hh, :, xs(k), :, :, :, colx].reshape(NY * NL * NC * rows, ca)
            acc[:, colx] += jnp.dot(lhs, rhs, preferred_element_type=F32)

    def project_y(k):
        for hh in range(NH):
            lhs = jnp.concatenate([nxt[(hh * NY + ys(k)) * NX + xx] for xx in range(NX)], axis=1)
            rhs = w[hh, ys(k), :, :, :, :, coly].reshape(NX * NL * NC * rows, cb - ca)
            acc[:, coly] += jnp.dot(lhs, rhs, preferred_element_type=F32)

    acc[...] = jnp.zeros_like(acc)

    @pl.loop(0, NH * NY * NX)
    def _(i):
        nxt_copy(i).wait()

    wait_recv(r1x.at[0], fx_recv.at[0])
    project_x(0)
    for i in range(2):
        wait_recv(m1x.at[0], a1x_recv.at[i, 1])
        gather(xpart(1 + 2 * i, i), f_send.at[0], fx_recv.at[1 + 2 * i], sib)
        wait_recv(m1y.at[0], a1y_recv.at[i, 1])
        gather(ypart(1 + 2 * i, i), f_send.at[1], fy_recv.at[1 + 2 * i], sib)
    wait_recv(r1y.at[0], fy_recv.at[0])
    project_y(0)
    for i, k in enumerate((-1, 1)):
        for part in range(NX):
            wait_recv(r1z.at[0, :, 0], a1z_recv.at[2 + i, part])
        gather(zpart(k), f_send.at[2], fz_recv.at[0], sib)
    for k in (1, 3):
        wait_recv(r1x.at[0], fx_recv.at[k])
        project_x(k)
        wait_recv(r1y.at[0], fy_recv.at[k])
        project_y(k)
    for i in range(2):
        wait_recv(m1x.at[0], a1x_recv.at[i, 2])
        gather(xpart(2, i), f_send.at[0], fx_recv.at[2], sib)
        wait_recv(m1y.at[0], a1y_recv.at[i, 2])
        gather(ypart(2, i), f_send.at[1], fy_recv.at[2], sib)
    for i, k in enumerate((-3, 3)):
        wait_recv(r1z.at[0], a1z_recv.at[6 + i, 0])
        gather(zpart(k), f_send.at[2], fz_recv.at[0], sib)
    for i in range(2):
        wait_recv(r1z.at[0, pl.ds(0, NY // 2)], a1z_recv.at[4 + i, 0])
        gather(zhalf(4, i), f_send.at[2], fz_recv.at[0], sib)
    sec_copy = pltpu.make_async_copy(w.at[:, :, :, l, c], o_sec, out_sem.at[0])
    sec_copy.start()
    wait_recv(r1x.at[0], fx_recv.at[2])
    project_x(2)
    o_proj[:, colx] = acc[:, colx].astype(BF16)
    wait_recv(r1y.at[0], fy_recv.at[2])
    project_y(2)
    o_proj[:, coly] = acc[:, coly].astype(BF16)
    wait_recv(w.at[:, :, :, :, 1 - c, :, colz], fz_recv.at[0])

    @pl.loop(0, NH)
    def _(hh):
        lhs = jnp.concatenate([nxt[hh * NY * NX + i] for i in range(NY * NX)], axis=1)
        rhs = w[hh, :, :, :, :, :, colz].reshape(NY * width, kv - cb)
        acc[:, colz] += jnp.dot(lhs, rhs, preferred_element_type=F32)

    o_proj[:, colz] = acc[:, colz].astype(BF16)
    sec_copy.wait()

    drain()


def copy_out(*refs):
    src, dst, sem = refs[:5], refs[5:10], refs[10]
    copies = []
    for i in range(5):
        n, rows = PARTS[i], src[i].shape[0]
        for j in range(n):
            part = pl.ds(j * rows // n, rows // n)
            copies.append(pltpu.make_async_copy(src[i].at[part], dst[i].at[part], sem.at[len(copies)]))
    for copy in copies:
        copy.start()
    for copy in copies:
        copy.wait()


def body(tokens, out_grad, next_tokens, overflow, master, first_moment, second_moment):
    toks, din = tokens.shape
    rows, kv = master.shape
    ca, cb = 3 * kv // 8, 6 * kv // 8
    cx, cy, cz = ca, cb - ca, kv - cb
    width = NX * NL * NC * rows
    vmem, anym = pl.BlockSpec(memory_space=pltpu.VMEM), pl.BlockSpec(memory_space=pl.ANY)
    dma = pltpu.SemaphoreType.DMA
    shapes = (
        jax.ShapeDtypeStruct((rows, kv), F32),
        jax.ShapeDtypeStruct((rows, kv), F32),
        jax.ShapeDtypeStruct((rows, kv), F32),
        jax.ShapeDtypeStruct((NH, NY, NX, rows, kv), BF16),
        jax.ShapeDtypeStruct((toks, kv), BF16),
    )
    scratch = [
        pltpu.SMEM((1,), jnp.int32),
        pltpu.VMEM((rows, kv), F32),
        pltpu.VMEM((rows, kv), F32),
        pltpu.VMEM((rows, kv), F32),
        pltpu.VMEM((NH * NY, toks, width), BF16),
        pltpu.VMEM((toks, kv), BF16),
        pltpu.VMEM((NH * NY * NX, toks, NL * NC * rows), BF16),
        pltpu.VMEM((NH, NY, NX, NL, rows, kv), F32),
        pltpu.VMEM((NH, NY, NX, NL, rows, kv), BF16),
        pltpu.VMEM((NH, NY, NX, NL, rows, kv), BF16),
        pltpu.VMEM((NH, NY, NX, NL, rows, kv), BF16),
        pltpu.VMEM((NH, NY, NL, rows, cx), BF16),
        pltpu.VMEM((NH, NX, NL, rows, cy), BF16),
        pltpu.VMEM((NH, NY, NL, rows, cx), BF16),
        pltpu.VMEM((NH, NX, NL, rows, cy), BF16),
        pltpu.VMEM((2, NY, NX, rows, cz), BF16),
        pltpu.VMEM((2, NH, NY, NL, rows, cx), BF16),
        pltpu.VMEM((2, NH, NX, NL, rows, cy), BF16),
        pltpu.VMEM((7, NY, NX, rows, cz), BF16),
        pltpu.VMEM((NH, NY, NL, rows, cx), BF16),
        pltpu.VMEM((NH, NX, NL, rows, cy), BF16),
        pltpu.VMEM((NY, NX, rows, cz), BF16),
        pltpu.VMEM((NY - 1, NH, NL, rows, cx), BF16),
        pltpu.VMEM((NX - 1, NH, NL, rows, cy), BF16),
        pltpu.VMEM((NX - 1, NY, rows, cz), BF16),
        pltpu.VMEM((NH, NL, rows, cx + cy), BF16),
        pltpu.VMEM((NY, rows, cz), BF16),
        pltpu.VMEM((NZ - 1, rows, cx + cy), BF16),
        pltpu.VMEM((NY - 1, rows, cz), BF16),
        pltpu.VMEM((4, 8, 128), F32),
        pltpu.VMEM((1 + NX - 1 + NY - 1 + NZ - 1, 8, 128), F32),
        pltpu.VMEM((NH, NY, NX, NL, NC, rows, kv), BF16),
        pltpu.VMEM((toks, kv), F32),
    ]
    sems = (
        [(5,), (NH * NY,), (NH * NY * NX,), (1,), (1,), (NH * NY,), (4,), (NX + NY + NZ - 2,)]
        + [(8,), (NH, NY), (NH,), (2,), (2,), (7,)]
        + [(3,), (NY - 1,), (NX - 1,), (NX - 1,)]
        + [(2,), (NZ - 1,), (NY - 1,)]
        + [(2,), (NZ - 1,), (NY - 1,)]
        + [(3,), (NY - 1,), (NX - 1,), (NX - 1,)]
        + [(6,), (2, 3), (2, 3), (8, NX)]
        + [(3,), (NX,), (NY,), (1,)]
    )
    results = pl.pallas_call(
        kernel,
        out_shape=[pltpu.VMEM(shape.shape, shape.dtype) for shape in shapes],
        in_specs=[anym] * 7,
        out_specs=[vmem] * 5,
        scratch_shapes=scratch + [dma(n) for n in sems],
        compiler_params=pltpu.CompilerParams(
            collective_id=0, has_side_effects=True, vmem_limit_bytes=56 * 2**20
        ),
        cost_estimate=pl.CostEstimate(flops=4 * toks * din * kv, bytes_accessed=12 * 2**20, transcendentals=rows * kv),
    )(overflow, tokens, out_grad, next_tokens, master, first_moment, second_moment)
    new_master, new_first, new_second, sec, proj = pl.pallas_call(
        copy_out,
        out_shape=shapes,
        in_specs=[vmem] * 5,
        out_specs=[anym] * 5,
        scratch_shapes=[dma((sum(PARTS),))],
        compiler_params=pltpu.CompilerParams(vmem_limit_bytes=8 * 2**20),
    )(*results)
    return (new_master, new_first, new_second, sec.reshape(NH * NY * NX, rows, kv), proj)


def solution(mesh):
    return jax.shard_map(
        body,
        mesh=mesh,
        in_specs=(
            P(("node", "local"), None),
            P(("node", "local"), None),
            P(("node", "local"), None),
            P(("node", "local")),
            P(("node", "local"), None),
            P(("node", "local"), None),
            P(("node", "local"), None),
        ),
        out_specs=(
            P(("node", "local"), None),
            P(("node", "local"), None),
            P(("node", "local"), None),
            P(None, "local", None),
            P(("node", "local"), None),
        ),
        check_vma=False,
    )
```

```python
import functools

import jax
import jax.numpy as jnp
from jax import lax
from jax.experimental import pallas as pl
from jax.experimental.pallas import tpu as pltpu
from jax.sharding import PartitionSpec as P

STEP = 10
MESH = pl.DeviceIdType.MESH
NH, NY, NX, NL, NC = 2, 4, 4, 4, 2
NZ = NH * NL
LAG = 2
PARTS = (1, 1, 1, 2, 2)
F32, BF16 = jnp.float32, jnp.bfloat16


def kernel(
    ov_hbm, tok_hbm, og_hbm, nxt_hbm, master_hbm, first_hbm, second_hbm,
    o_master, o_first, o_second, o_sec, o_proj,
    ov, master, first, second, tok, og, nxt, own, sib_out, sib_in, s1,
    m1x, m1y, f1x, f1y, f1z, r1x, r1y, r1z, s2x, s2y, s2z, r2x, r2y, r2z, s3a, s3z, r3a, r3z,
    cnt, cnt_in, w, acc,
    in_sem, tok_sem, nxt_sem, out_sem, sib_send, sib_recv, cnt_send, cnt_recv,
    p1_send, m1x_recv, m1y_recv, p1x_recv, p1y_recv, p1z_recv,
    p2_send, p2x_recv, p2y_recv, p2z_recv, p3_send, p3a_recv, p3z_recv,
    a3_send, a3a_recv, a3z_recv, a2_send, a2x_recv, a2y_recv, a2z_recv,
    a1_send, a1x_recv, a1y_recv, a1z_recv, f_send, fx_recv, fy_recv, fz_recv,
):
    rows, kv = master.shape
    ca, cb = r1x.shape[-1], r1x.shape[-1] + r1y.shape[-1]
    colx, coly, colz, colxy = pl.ds(0, ca), pl.ds(ca, cb - ca), pl.ds(cb, kv - cb), pl.ds(0, cb)
    node, loc = lax.axis_index("node"), lax.axis_index("local")
    x, y, h = lax.rem(node, NX), lax.rem(lax.div(node, NX), NY), lax.div(node, NX * NY)
    c, l = lax.rem(loc, NC), lax.div(loc, NC)

    def dev(hh=h, yy=y, xx=x, ll=l, cc=c):
        return ((hh * NY + yy) * NX + xx, ll * NC + cc)

    def xs(d):
        return lax.rem(x + d, NX)

    def ys(d):
        return lax.rem(y + d, NY)

    def hs(e):
        return lax.rem(h + e, NH)

    def ls(f):
        return lax.rem(l + f, NL)

    def zdev(k):
        zz = lax.rem(h * NL + l + k + NZ, NZ)
        return dev(hh=lax.div(zz, NL), ll=lax.rem(zz, NL))

    def zat(k):
        zz = lax.rem(h * NL + l + k + NZ, NZ)
        return lax.div(zz, NL), lax.rem(zz, NL)

    xd = yd = (2, 1, 3)
    zd = [(1, f) for f in range(NL)] + [(0, f) for f in range(1, NL)]
    sib = dev(cc=1 - c)

    def remote(src, dst, send, recv, to):
        return pltpu.make_async_remote_copy(
            src_ref=src, dst_ref=dst, send_sem=send, recv_sem=recv, device_id=to, device_id_type=MESH
        )

    def wait_recv(ref, sem):
        remote(ref, ref, sem, sem, sib).wait_recv()

    def wait_send(ref, sem):
        remote(ref, ref, sem, sem, sib).wait_send()

    pending = []

    def drain():
        for ref, sem in pending:
            wait_send(ref, sem)

    peers = [sib]
    peers += [dev(xx=xs(d)) for d in xd] + [dev(yy=ys(d)) for d in yd]
    peers += [dev(hh=hs(e), ll=ls(f)) for e, f in zd]
    barrier = pltpu.get_barrier_semaphore()
    for to in peers:
        pl.semaphore_signal(barrier, inc=1, device_id=to, device_id_type=MESH)

    og_copy = pltpu.make_async_copy(og_hbm, og, in_sem.at[0])

    def nxt_copy(i):
        cols = pl.ds(pl.multiple_of(i * NL * NC * rows, NL * NC * rows), NL * NC * rows)
        return pltpu.make_async_copy(nxt_hbm.at[:, cols], nxt.at[i], nxt_sem.at[i])

    ov_copy = pltpu.make_async_copy(ov_hbm, ov, in_sem.at[1])
    adam_copies = [
        pltpu.make_async_copy(src, dst, in_sem.at[2 + i])
        for i, (src, dst) in enumerate(((master_hbm, master), (first_hbm, first), (second_hbm, second)))
    ]
    ov_copy.start()
    og_copy.start()
    width = NX * NL * NC * rows
    steps = NH * NY

    def place(it):
        e, d = lax.rem(it, NH), lax.rem(2 + NY - lax.div(it, NH), NY)
        return e, d, hs(e), ys(d)

    def tok_copy(it):
        _, _, hh, yy = place(it)
        cols = pl.ds(pl.multiple_of((hh * NY + yy) * width, width), width)
        return pltpu.make_async_copy(tok_hbm.at[:, cols], tok.at[it], tok_sem.at[it])

    def start_tok(it):
        tok_copy(it).start()

    pl.loop(0, LAG)(start_tok)
    og_copy.wait()
    pl.loop(LAG, steps)(start_tok)
    ov_copy.wait()
    kept = (1 - ov[0]).astype(F32)
    og[...] = og[...] * kept.astype(BF16)
    cnt[0] = jnp.full(cnt.shape[1:], kept, F32)

    def partial_sum(it):
        _, _, hh, yy = place(it)
        tok_copy(it).wait()
        part = lax.dot_general(tok[it], og[...], (((0,), (0,)), ((), ())), preferred_element_type=F32)
        part = part.reshape(NX, NL, NC, rows, kv)
        even, odd = part[:, :, 0], part[:, :, 1]
        own[hh, yy] = jnp.where(c == 0, even, odd)
        sib_out[hh, yy] = jnp.where(c == 0, odd, even).astype(BF16)

    def send_partial(it):
        _, _, hh, yy = place(it)
        remote(sib_out.at[hh, yy], sib_in.at[hh, yy], sib_send.at[0], sib_recv.at[it], sib).start()

    pl.loop(0, LAG)(partial_sum)
    pl.semaphore_wait(barrier, len(peers))
    remote(cnt.at[0], cnt_in.at[0], cnt_send.at[0], cnt_recv.at[0], sib).start()
    pl.loop(0, LAG)(send_partial)

    def exchange_first(it):
        e, d, hh, yy = place(it)
        wait_recv(sib_in.at[hh, yy], sib_recv.at[it])
        s1[hh, yy] = (own[hh, yy] + sib_in[hh, yy].astype(F32)).astype(BF16)
        go, back = 1 + 2 * hh, NX - 1 - 2 * hh
        remote(
            s1.at[hh, yy, xs(2), :, :, colx], m1x.at[hh, yy], p1_send.at[0], m1x_recv.at[hh, yy], dev(xx=xs(go))
        ).start()
        remote(
            s1.at[hh, yy, xs(back), :, :, colx], r1x.at[0, hh, yy], p1_send.at[1], p1x_recv.at[0], dev(xx=xs(back))
        ).start()

        @pl.when(d == 2)
        def _():
            remote(
                s1.at[hh, yy, :, :, :, coly], m1y.at[hh], p1_send.at[3], m1y_recv.at[hh], dev(yy=ys(go))
            ).start()

        @pl.when(d == back)
        def _():
            remote(
                s1.at[hh, yy, :, :, :, coly], r1y.at[0, hh], p1_send.at[4], p1y_recv.at[0], dev(yy=ys(back))
            ).start()

        @pl.loop(0, NL, unroll=True)
        def _(ll):
            k = lax.rem(hh * NL + ll + NZ - h * NL - l, NZ)
            up = k < 4
            odd = lax.rem(k, 2) == 1
            slot = jnp.where(odd, jnp.where((k == 1) | (k == 7), 0, 2) + jnp.where(up, 0, 1), 4)
            hop = jnp.where(odd, jnp.where(up, 1, NZ - 1), jnp.where(yy < NY // 2, 2, NZ - 2))

            @pl.when(odd | (k == 4))
            def _():
                remote(
                    s1.at[hh, yy, :, ll, :, colz], r1z.at[slot, yy], p1_send.at[6], p1z_recv.at[slot], zdev(hop)
                ).start()

    @pl.loop(LAG, steps)
    def _(it):
        partial_sum(it)
        send_partial(it)
        exchange_first(it - LAG)

    pl.loop(steps - LAG, steps)(exchange_first)

    wait_recv(cnt_in.at[0], cnt_recv.at[0])
    cnt[1] = cnt[0] + cnt_in[0]
    for k in xd:
        remote(cnt.at[1], cnt_in.at[k], cnt_send.at[1], cnt_recv.at[k], dev(xx=xs(k))).start()

    pending += [(sib_out, sib_send.at[0]), (cnt.at[0], cnt_send.at[0]), (cnt_in.at[pl.ds(0, NX - 1)], cnt_send.at[1])]
    pending += [(m1x, p1_send.at[0]), (r1x.at[0], p1_send.at[1]), (m1y, p1_send.at[3]), (r1y.at[0], p1_send.at[4])]
    pending += [(r1z.at[pl.ds(0, 5)], p1_send.at[6])]

    def relay_x(it):
        _, _, hh, yy = place(it)
        go = 1 + 2 * hh
        wait_recv(m1x.at[hh, yy], m1x_recv.at[hh, yy])
        f1x[hh, yy] = (s1[hh, yy, xs(go), :, :, colx].astype(F32) + m1x[hh, yy].astype(F32)).astype(BF16)
        remote(f1x.at[hh, yy], r1x.at[1, hh, yy], p1_send.at[2], p1x_recv.at[1], dev(xx=xs(go))).start()

    @pl.loop(0, NH)
    def _(hh):
        go = 1 + 2 * hh
        wait_recv(m1y.at[hh], m1y_recv.at[hh])

        @pl.loop(0, NX)
        def _(xx):
            f1y[hh, xx] = (s1[hh, ys(go), xx, :, :, coly].astype(F32) + m1y[hh, xx].astype(F32)).astype(BF16)

        remote(f1y.at[hh], r1y.at[1, hh], p1_send.at[5], p1y_recv.at[1], dev(yy=ys(go))).start()

    pl.loop(0, steps - LAG)(relay_x)

    for slot in (2, 3, 4):
        wait_recv(r1z.at[slot], p1z_recv.at[slot])
    for i, k in ((0, 2), (1, NZ - 2)):
        hh, ll = zat(k)
        for yy in range(NY):
            total = s1[hh, yy, :, ll, :, colz].astype(F32) + r1z[2 + i, yy].astype(F32)
            if (yy < NY // 2) == (i == 0):
                total += r1z[4, yy].astype(F32)
            f1z[i, yy] = total.astype(BF16)
        remote(f1z.at[i], r1z.at[5 + i], p1_send.at[7], p1z_recv.at[5 + i], zdev(k)).start()

    pl.loop(steps - LAG, steps)(relay_x)

    for k in xd:
        wait_recv(cnt_in.at[k], cnt_recv.at[k])
    cnt[2] = cnt[1] + cnt_in[1] + cnt_in[2] + cnt_in[3]
    for k in yd:
        remote(cnt.at[2], cnt_in.at[NX - 1 + k], cnt_send.at[2], cnt_recv.at[NX - 1 + k], dev(yy=ys(k))).start()

    pending += [(f1x, p1_send.at[2]), (f1y, p1_send.at[5]), (f1z, p1_send.at[7])]

    @pl.loop(0, NH * NY * NX)
    def _(i):
        nxt_copy(i).start()

    for copy in adam_copies:
        copy.start()

    for k in range(2):
        wait_recv(r1x.at[k], p1x_recv.at[k])

    @pl.loop(0, NH * NY)
    def _(i):
        hh, yy = lax.div(i, NY), lax.rem(i, NY)
        total = s1[hh, yy, x, :, :, colx].astype(F32)
        for k in range(2):
            total += r1x[k, hh, yy].astype(F32)
        s2x[hh, yy] = total.astype(BF16)

    for k in yd:
        remote(s2x.at[:, ys(k)], r2x.at[k - 1], p2_send.at[0], p2x_recv.at[k - 1], dev(yy=ys(k))).start()

    for k in range(2):
        wait_recv(r1y.at[k], p1y_recv.at[k])

    @pl.loop(0, NH * NX)
    def _(i):
        hh, xx = lax.div(i, NX), lax.rem(i, NX)
        total = s1[hh, y, xx, :, :, coly].astype(F32)
        for k in range(2):
            total += r1y[k, hh, xx].astype(F32)
        s2y[hh, xx] = total.astype(BF16)

    for k in xd:
        remote(s2y.at[:, xs(k)], r2y.at[k - 1], p2_send.at[1], p2y_recv.at[k - 1], dev(xx=xs(k))).start()

    for k in (0, 1, 5, 6):
        wait_recv(r1z.at[k], p1z_recv.at[k])

    @pl.loop(0, NY)
    def _(yy):
        total = s1[h, yy, :, l, :, colz].astype(F32)
        for k in (0, 1, 5, 6):
            total += r1z[k, yy].astype(F32)
        s2z[yy] = total.astype(BF16)

    for k in xd:
        remote(s2z.at[:, xs(k)], r2z.at[k - 1], p2_send.at[2], p2z_recv.at[k - 1], dev(xx=xs(k))).start()

    base = NX + NY - 1
    for k in yd:
        wait_recv(cnt_in.at[NX - 1 + k], cnt_recv.at[NX - 1 + k])
    cnt[3] = cnt[2] + cnt_in[NX] + cnt_in[NX + 1] + cnt_in[NX + 2]
    for e, f in zd:
        slot = base + e * NL + f - 1
        remote(cnt.at[3], cnt_in.at[slot], cnt_send.at[3], cnt_recv.at[slot], dev(hh=hs(e), ll=ls(f))).start()

    pending += [(r2x, p2_send.at[0]), (r2y, p2_send.at[1]), (r2z, p2_send.at[2])]
    pending += [(cnt_in.at[pl.ds(0, NY - 1)], cnt_send.at[2])]

    for k in yd:
        wait_recv(r2x.at[k - 1], p2x_recv.at[k - 1])
    total = s2x[:, y].astype(F32)
    for k in yd:
        total += r2x[k - 1].astype(F32)
    s3a[:, :, :, colx] = total.astype(BF16)
    for k in xd:
        wait_recv(r2y.at[k - 1], p2y_recv.at[k - 1])
    total = s2y[:, x].astype(F32)
    for k in xd:
        total += r2y[k - 1].astype(F32)
    s3a[:, :, :, coly] = total.astype(BF16)
    for e, f in zd:
        slot = e * NL + f - 1
        remote(
            s3a.at[hs(e), ls(f)], r3a.at[slot], p3_send.at[0], p3a_recv.at[slot], dev(hh=hs(e), ll=ls(f))
        ).start()
    for k in xd:
        wait_recv(r2z.at[k - 1], p2z_recv.at[k - 1])
    total = s2z[:, x].astype(F32)
    for k in xd:
        total += r2z[k - 1].astype(F32)
    s3z[...] = total.astype(BF16)
    for k in yd:
        remote(s3z.at[ys(k)], r3z.at[k - 1], p3_send.at[1], p3z_recv.at[k - 1], dev(yy=ys(k))).start()

    for k in range(1, NZ):
        wait_recv(r3a.at[k - 1], p3a_recv.at[k - 1])
    sum_a = s3a[h, l].astype(F32)
    for k in range(1, NZ):
        sum_a += r3a[k - 1].astype(F32)
    for k in range(1, NZ):
        wait_recv(cnt_in.at[base + k - 1], cnt_recv.at[base + k - 1])
    count = cnt[3]
    for k in range(1, NZ):
        count += cnt_in[base + k - 1]
    count = count[0:1, 0:1]

    pending += [(r3a, p3_send.at[0]), (r3z, p3_send.at[1]), (cnt_in.at[pl.ds(0, NZ - 1)], cnt_send.at[3])]

    for copy in adam_copies:
        copy.wait()

    def adam(cols, summed):
        grad = summed / count
        new_first = 0.9 * first[:, cols] + 0.1 * grad
        new_second = 0.95 * second[:, cols] + 0.05 * grad * grad
        update = new_first / (1.0 - 0.9**STEP) / (jnp.sqrt(new_second / (1.0 - 0.95**STEP)) + 1e-08)
        new_master = master[:, cols] - 0.001 * (update + 0.1 * master[:, cols])
        o_first[:, cols] = new_first
        o_second[:, cols] = new_second
        o_master[:, cols] = new_master
        w[h, y, x, l, c, :, cols] = new_master.astype(BF16)

    adam(colxy, sum_a)

    def gather(ref, send, recv, to):
        remote(ref, ref, send, recv, to).start()

    for e, f in zd:
        gather(w.at[h, y, x, l, c, :, colxy], a3_send.at[0], a3a_recv.at[e * NL + f - 1], dev(hh=hs(e), ll=ls(f)))
    for k in yd:
        wait_recv(r3z.at[k - 1], p3z_recv.at[k - 1])
    sum_z = s3z[y].astype(F32)
    for k in yd:
        sum_z += r3z[k - 1].astype(F32)
    adam(colz, sum_z)
    for k in yd:
        gather(w.at[h, y, x, l, c, :, colz], a3_send.at[1], a3z_recv.at[k - 1], dev(yy=ys(k)))
    for k in yd:
        wait_recv(r3z.at[k - 1], a3z_recv.at[k - 1])
    for k in xd:
        gather(w.at[h, :, x, l, c, :, colz], a2_send.at[2], a2z_recv.at[k - 1], dev(xx=xs(k)))
    for k in range(1, NZ):
        wait_recv(r3a.at[k - 1], a3a_recv.at[k - 1])
    for k in yd:
        gather(w.at[:, y, x, :, c, :, colx], a2_send.at[0], a2x_recv.at[k - 1], dev(yy=ys(k)))
    for k in xd:
        gather(w.at[:, y, x, :, c, :, coly], a2_send.at[1], a2y_recv.at[k - 1], dev(xx=xs(k)))

    def xpart(k, hh):
        return w.at[hh, :, xs(k), :, c, :, colx]

    def ypart(k, hh):
        return w.at[hh, ys(k), :, :, c, :, coly]

    def zpart(k):
        hh, ll = zat(k)
        return w.at[hh, :, :, ll, c, :, colz]

    def zhalf(k, i):
        hh, ll = zat(k)
        return w.at[hh, pl.ds(i * (NY // 2), NY // 2), :, ll, c, :, colz]

    pending += [(r3a, a3_send.at[0]), (r3z, a3_send.at[1])]
    pending += [(r2x, a2_send.at[0]), (r2y, a2_send.at[1]), (r2z, a2_send.at[2])]

    def send_x(part, turn):
        for i in range(2):
            to = 1 + 2 * i if turn == 0 else 3 - 2 * i
            gather(w.at[i, part, x, :, c, :, colx], a1_send.at[0], a1x_recv.at[i, turn], dev(xx=xs(to)))

    def send_y(part, turn):
        for i in range(2):
            to = 1 + 2 * i if turn == 0 else 3 - 2 * i
            gather(w.at[i, y, part, :, c, :, coly], a1_send.at[2], a1y_recv.at[i, turn], dev(yy=ys(to)))

    def send_z(part, turn):
        for i in range(2):
            to = (2 - turn) * (1 - 2 * i)
            gather(w.at[h, :, part, l, c, :, colz], a1_send.at[4], a1z_recv.at[2 * turn + i, part], zdev(to))

    for turn in range(2):
        send_x(y, turn)
        send_y(x, turn)
        send_z(x, turn)
    for k in (1, 3, 2):
        wait_recv(r2z.at[k - 1], a2z_recv.at[k - 1])
        send_z(xs(NX - k), 0)
    for k in (1, 3, 2):
        wait_recv(r2x.at[k - 1], a2x_recv.at[k - 1])
        send_x(ys(NY - k), 0)
        wait_recv(r2y.at[k - 1], a2y_recv.at[k - 1])
        send_y(xs(NX - k), 0)
    for k in (1, 3, 2):
        send_x(ys(NY - k), 1)
        send_y(xs(NX - k), 1)
        send_z(xs(NX - k), 1)
    for i in range(2):
        gather(xpart(0, i), f_send.at[0], fx_recv.at[0], sib)
        gather(ypart(0, i), f_send.at[1], fy_recv.at[0], sib)
    gather(zpart(0), f_send.at[2], fz_recv.at[0], sib)

    def relay_z(part):
        for i, k in enumerate((-2, 2)):
            wait_recv(r1z.at[0, :, 0], a1z_recv.at[i, part])
            hh, ll = zat(k)
            gather(w.at[hh, :, part, ll, c, :, colz], a1_send.at[5], a1z_recv.at[6 + i, 0], zdev(-k // 2))
            half = pl.ds(i * (NY // 2), NY // 2)
            gather(w.at[hh, half, part, ll, c, :, colz], a1_send.at[5], a1z_recv.at[4 + i, 0], zdev(-k))

    relay_z(x)
    relay_z(xs(NX - 1))
    relay_z(xs(NX - 3))
    relay_z(xs(NX - 2))
    for i in range(2):
        wait_recv(m1x.at[0], a1x_recv.at[i, 0])
        gather(xpart(3 - 2 * i, i), a1_send.at[1], a1x_recv.at[i, 2], dev(xx=xs(1 + 2 * i)))
        wait_recv(m1y.at[0], a1y_recv.at[i, 0])
        gather(ypart(3 - 2 * i, i), a1_send.at[3], a1y_recv.at[i, 2], dev(yy=ys(1 + 2 * i)))
    for i in range(2):
        gather(xpart(3 - 2 * i, i), f_send.at[0], fx_recv.at[3 - 2 * i], sib)
        gather(ypart(3 - 2 * i, i), f_send.at[1], fy_recv.at[3 - 2 * i], sib)
    for k in (-2, 2):
        gather(zpart(k), f_send.at[2], fz_recv.at[0], sib)

    pending += [(r1x, a1_send.at[0]), (r1x.at[0], a1_send.at[1]), (r1y, a1_send.at[2]), (r1y.at[0], a1_send.at[3])]
    pending += [(r1z.at[pl.ds(0, 4)], a1_send.at[4]), (r1z.at[pl.ds(0, 3)], a1_send.at[5])]
    pending += [(w.at[:, :, :, :, c, :, cols], f_send.at[i]) for i, cols in enumerate((colx, coly, colz))]

    def project_x(k):
        for hh in range(NH):
            lhs = jnp.concatenate([nxt[(hh * NY + yy) * NX + xs(k)] for yy in range(NY)], axis=1)
            rhs = w[hh, :, xs(k), :, :, :, colx].reshape(NY * NL * NC * rows, ca)
            acc[:, colx] += jnp.dot(lhs, rhs, preferred_element_type=F32)

    def project_y(k):
        for hh in range(NH):
            lhs = jnp.concatenate([nxt[(hh * NY + ys(k)) * NX + xx] for xx in range(NX)], axis=1)
            rhs = w[hh, ys(k), :, :, :, :, coly].reshape(NX * NL * NC * rows, cb - ca)
            acc[:, coly] += jnp.dot(lhs, rhs, preferred_element_type=F32)

    acc[...] = jnp.zeros_like(acc)

    @pl.loop(0, NH * NY * NX)
    def _(i):
        nxt_copy(i).wait()

    wait_recv(r1x.at[0], fx_recv.at[0])
    project_x(0)
    for i in range(2):
        wait_recv(m1x.at[0], a1x_recv.at[i, 1])
        gather(xpart(1 + 2 * i, i), f_send.at[0], fx_recv.at[1 + 2 * i], sib)
        wait_recv(m1y.at[0], a1y_recv.at[i, 1])
        gather(ypart(1 + 2 * i, i), f_send.at[1], fy_recv.at[1 + 2 * i], sib)
    wait_recv(r1y.at[0], fy_recv.at[0])
    project_y(0)
    for i, k in enumerate((-1, 1)):
        for part in range(NX):
            wait_recv(r1z.at[0, :, 0], a1z_recv.at[2 + i, part])
        gather(zpart(k), f_send.at[2], fz_recv.at[0], sib)
    for k in (1, 3):
        wait_recv(r1x.at[0], fx_recv.at[k])
        project_x(k)
        wait_recv(r1y.at[0], fy_recv.at[k])
        project_y(k)
    for i in range(2):
        wait_recv(m1x.at[0], a1x_recv.at[i, 2])
        gather(xpart(2, i), f_send.at[0], fx_recv.at[2], sib)
        wait_recv(m1y.at[0], a1y_recv.at[i, 2])
        gather(ypart(2, i), f_send.at[1], fy_recv.at[2], sib)
    for i, k in enumerate((-3, 3)):
        wait_recv(r1z.at[0], a1z_recv.at[6 + i, 0])
        gather(zpart(k), f_send.at[2], fz_recv.at[0], sib)
    for i in range(2):
        wait_recv(r1z.at[0, pl.ds(0, NY // 2)], a1z_recv.at[4 + i, 0])
        gather(zhalf(4, i), f_send.at[2], fz_recv.at[0], sib)
    sec_copy = pltpu.make_async_copy(w.at[:, :, :, l, c], o_sec, out_sem.at[0])
    sec_copy.start()
    wait_recv(r1x.at[0], fx_recv.at[2])
    project_x(2)
    o_proj[:, colx] = acc[:, colx].astype(BF16)
    wait_recv(r1y.at[0], fy_recv.at[2])
    project_y(2)
    o_proj[:, coly] = acc[:, coly].astype(BF16)
    wait_recv(w.at[:, :, :, :, 1 - c, :, colz], fz_recv.at[0])

    @pl.loop(0, NH)
    def _(hh):
        lhs = jnp.concatenate([nxt[hh * NY * NX + i] for i in range(NY * NX)], axis=1)
        rhs = w[hh, :, :, :, :, :, colz].reshape(NY * width, kv - cb)
        acc[:, colz] += jnp.dot(lhs, rhs, preferred_element_type=F32)

    o_proj[:, colz] = acc[:, colz].astype(BF16)
    sec_copy.wait()

    drain()


def copy_out(*refs):
    src, dst, sem = refs[:5], refs[5:10], refs[10]
    copies = []
    for i in range(5):
        n, rows = PARTS[i], src[i].shape[0]
        for j in range(n):
            part = pl.ds(j * rows // n, rows // n)
            copies.append(pltpu.make_async_copy(src[i].at[part], dst[i].at[part], sem.at[len(copies)]))
    for copy in copies:
        copy.start()
    for copy in copies:
        copy.wait()


def body(tokens, out_grad, next_tokens, overflow, master, first_moment, second_moment):
    toks, din = tokens.shape
    rows, kv = master.shape
    ca, cb = 3 * kv // 8, 6 * kv // 8
    cx, cy, cz = ca, cb - ca, kv - cb
    width = NX * NL * NC * rows
    vmem, anym = pl.BlockSpec(memory_space=pltpu.VMEM), pl.BlockSpec(memory_space=pl.ANY)
    dma = pltpu.SemaphoreType.DMA
    shapes = (
        jax.ShapeDtypeStruct((rows, kv), F32),
        jax.ShapeDtypeStruct((rows, kv), F32),
        jax.ShapeDtypeStruct((rows, kv), F32),
        jax.ShapeDtypeStruct((NH, NY, NX, rows, kv), BF16),
        jax.ShapeDtypeStruct((toks, kv), BF16),
    )
    scratch = [
        pltpu.SMEM((1,), jnp.int32),
        pltpu.VMEM((rows, kv), F32),
        pltpu.VMEM((rows, kv), F32),
        pltpu.VMEM((rows, kv), F32),
        pltpu.VMEM((NH * NY, toks, width), BF16),
        pltpu.VMEM((toks, kv), BF16),
        pltpu.VMEM((NH * NY * NX, toks, NL * NC * rows), BF16),
        pltpu.VMEM((NH, NY, NX, NL, rows, kv), F32),
        pltpu.VMEM((NH, NY, NX, NL, rows, kv), BF16),
        pltpu.VMEM((NH, NY, NX, NL, rows, kv), BF16),
        pltpu.VMEM((NH, NY, NX, NL, rows, kv), BF16),
        pltpu.VMEM((NH, NY, NL, rows, cx), BF16),
        pltpu.VMEM((NH, NX, NL, rows, cy), BF16),
        pltpu.VMEM((NH, NY, NL, rows, cx), BF16),
        pltpu.VMEM((NH, NX, NL, rows, cy), BF16),
        pltpu.VMEM((2, NY, NX, rows, cz), BF16),
        pltpu.VMEM((2, NH, NY, NL, rows, cx), BF16),
        pltpu.VMEM((2, NH, NX, NL, rows, cy), BF16),
        pltpu.VMEM((7, NY, NX, rows, cz), BF16),
        pltpu.VMEM((NH, NY, NL, rows, cx), BF16),
        pltpu.VMEM((NH, NX, NL, rows, cy), BF16),
        pltpu.VMEM((NY, NX, rows, cz), BF16),
        pltpu.VMEM((NY - 1, NH, NL, rows, cx), BF16),
        pltpu.VMEM((NX - 1, NH, NL, rows, cy), BF16),
        pltpu.VMEM((NX - 1, NY, rows, cz), BF16),
        pltpu.VMEM((NH, NL, rows, cx + cy), BF16),
        pltpu.VMEM((NY, rows, cz), BF16),
        pltpu.VMEM((NZ - 1, rows, cx + cy), BF16),
        pltpu.VMEM((NY - 1, rows, cz), BF16),
        pltpu.VMEM((4, 8, 128), F32),
        pltpu.VMEM((1 + NX - 1 + NY - 1 + NZ - 1, 8, 128), F32),
        pltpu.VMEM((NH, NY, NX, NL, NC, rows, kv), BF16),
        pltpu.VMEM((toks, kv), F32),
    ]
    sems = (
        [(5,), (NH * NY,), (NH * NY * NX,), (1,), (1,), (NH * NY,), (4,), (NX + NY + NZ - 2,)]
        + [(8,), (NH, NY), (NH,), (2,), (2,), (7,)]
        + [(3,), (NY - 1,), (NX - 1,), (NX - 1,)]
        + [(2,), (NZ - 1,), (NY - 1,)]
        + [(2,), (NZ - 1,), (NY - 1,)]
        + [(3,), (NY - 1,), (NX - 1,), (NX - 1,)]
        + [(6,), (2, 3), (2, 3), (8, NX)]
        + [(3,), (NX,), (NY,), (1,)]
    )
    results = pl.pallas_call(
        kernel,
        out_shape=[pltpu.VMEM(shape.shape, shape.dtype) for shape in shapes],
        in_specs=[anym] * 7,
        out_specs=[vmem] * 5,
        scratch_shapes=scratch + [dma(n) for n in sems],
        compiler_params=pltpu.CompilerParams(
            collective_id=0, has_side_effects=True, vmem_limit_bytes=56 * 2**20
        ),
        cost_estimate=pl.CostEstimate(flops=4 * toks * din * kv, bytes_accessed=12 * 2**20, transcendentals=rows * kv),
    )(overflow, tokens, out_grad, next_tokens, master, first_moment, second_moment)
    new_master, new_first, new_second, sec, proj = pl.pallas_call(
        copy_out,
        out_shape=shapes,
        in_specs=[vmem] * 5,
        out_specs=[anym] * 5,
        scratch_shapes=[dma((sum(PARTS),))],
        compiler_params=pltpu.CompilerParams(vmem_limit_bytes=8 * 2**20),
    )(*results)
    return (new_master, new_first, new_second, sec.reshape(NH * NY * NX, rows, kv), proj)


def solution(mesh):
    return jax.shard_map(
        body,
        mesh=mesh,
        in_specs=(
            P(("node", "local"), None),
            P(("node", "local"), None),
            P(("node", "local"), None),
            P(("node", "local")),
            P(("node", "local"), None),
            P(("node", "local"), None),
            P(("node", "local"), None),
        ),
        out_specs=(
            P(("node", "local"), None),
            P(("node", "local"), None),
            P(("node", "local"), None),
            P(None, "local", None),
            P(("node", "local"), None),
        ),
        check_vma=False,
    )
```

```python
import functools

import jax
import jax.numpy as jnp
from jax import lax
from jax.experimental import pallas as pl
from jax.experimental.pallas import tpu as pltpu
from jax.sharding import PartitionSpec as P

STEP = 10
MESH = pl.DeviceIdType.MESH
NH, NY, NX, NL, NC = 2, 4, 4, 4, 2
NZ = NH * NL
LAG = 2
PARTS = (1, 1, 1, 2, 2)
F32, BF16 = jnp.float32, jnp.bfloat16


def kernel(
    ov_hbm, tok_hbm, og_hbm, nxt_hbm, master_hbm, first_hbm, second_hbm,
    o_master, o_first, o_second, o_sec, o_proj,
    ov, master, first, second, tok, og, nxt, own, sib_out, sib_in, s1,
    m1x, m1y, f1x, f1y, f1z, r1x, r1y, r1z, s2x, s2y, s2z, r2x, r2y, r2z, s3a, s3z, r3a, r3z,
    cnt, cnt_in, w, acc,
    in_sem, tok_sem, nxt_sem, out_sem, sib_send, sib_recv, cnt_send, cnt_recv,
    p1_send, m1x_recv, m1y_recv, p1x_recv, p1y_recv, p1z_recv,
    p2_send, p2x_recv, p2y_recv, p2z_recv, p3_send, p3a_recv, p3z_recv,
    a3_send, a3a_recv, a3z_recv, a2_send, a2x_recv, a2y_recv, a2z_recv,
    a1_send, a1x_recv, a1y_recv, a1z_recv, f_send, fx_recv, fy_recv, fz_recv,
):
    rows, kv = master.shape
    ca, cb = r1x.shape[-1], r1x.shape[-1] + r1y.shape[-1]
    colx, coly, colz, colxy = pl.ds(0, ca), pl.ds(ca, cb - ca), pl.ds(cb, kv - cb), pl.ds(0, cb)
    node, loc = lax.axis_index("node"), lax.axis_index("local")
    x, y, h = lax.rem(node, NX), lax.rem(lax.div(node, NX), NY), lax.div(node, NX * NY)
    c, l = lax.rem(loc, NC), lax.div(loc, NC)

    def dev(hh=h, yy=y, xx=x, ll=l, cc=c):
        return ((hh * NY + yy) * NX + xx, ll * NC + cc)

    def xs(d):
        return lax.rem(x + d, NX)

    def ys(d):
        return lax.rem(y + d, NY)

    def hs(e):
        return lax.rem(h + e, NH)

    def ls(f):
        return lax.rem(l + f, NL)

    def zdev(k):
        zz = lax.rem(h * NL + l + k + NZ, NZ)
        return dev(hh=lax.div(zz, NL), ll=lax.rem(zz, NL))

    def zat(k):
        zz = lax.rem(h * NL + l + k + NZ, NZ)
        return lax.div(zz, NL), lax.rem(zz, NL)

    xd = yd = (2, 1, 3)
    zd = [(1, f) for f in range(NL)] + [(0, f) for f in range(1, NL)]
    sib = dev(cc=1 - c)

    def remote(src, dst, send, recv, to):
        return pltpu.make_async_remote_copy(
            src_ref=src, dst_ref=dst, send_sem=send, recv_sem=recv, device_id=to, device_id_type=MESH
        )

    def wait_recv(ref, sem):
        remote(ref, ref, sem, sem, sib).wait_recv()

    def wait_send(ref, sem):
        remote(ref, ref, sem, sem, sib).wait_send()

    pending = []

    def drain():
        for ref, sem in pending:
            wait_send(ref, sem)

    peers = [sib]
    peers += [dev(xx=xs(d)) for d in xd] + [dev(yy=ys(d)) for d in yd]
    peers += [dev(hh=hs(e), ll=ls(f)) for e, f in zd]
    barrier = pltpu.get_barrier_semaphore()
    for to in peers:
        pl.semaphore_signal(barrier, inc=1, device_id=to, device_id_type=MESH)

    og_copy = pltpu.make_async_copy(og_hbm, og, in_sem.at[0])

    def nxt_copy(i):
        cols = pl.ds(pl.multiple_of(i * NL * NC * rows, NL * NC * rows), NL * NC * rows)
        return pltpu.make_async_copy(nxt_hbm.at[:, cols], nxt.at[i], nxt_sem.at[i])

    ov_copy = pltpu.make_async_copy(ov_hbm, ov, in_sem.at[1])
    adam_copies = [
        pltpu.make_async_copy(src, dst, in_sem.at[2 + i])
        for i, (src, dst) in enumerate(((master_hbm, master), (first_hbm, first), (second_hbm, second)))
    ]
    ov_copy.start()
    og_copy.start()
    width = NX * NL * NC * rows
    steps = NH * NY

    def place(it):
        e, d = lax.rem(it, NH), lax.rem(2 + NY - lax.div(it, NH), NY)
        return e, d, hs(e), ys(d)

    def tok_copy(it):
        _, _, hh, yy = place(it)
        cols = pl.ds(pl.multiple_of((hh * NY + yy) * width, width), width)
        return pltpu.make_async_copy(tok_hbm.at[:, cols], tok.at[it], tok_sem.at[it])

    def start_tok(it):
        tok_copy(it).start()

    pl.loop(0, LAG)(start_tok)
    og_copy.wait()
    pl.loop(LAG, steps)(start_tok)
    ov_copy.wait()
    kept = (1 - ov[0]).astype(F32)
    og[...] = og[...] * kept.astype(BF16)
    cnt[0] = jnp.full(cnt.shape[1:], kept, F32)

    def partial_sum(it):
        _, _, hh, yy = place(it)
        tok_copy(it).wait()
        part = lax.dot_general(tok[it], og[...], (((0,), (0,)), ((), ())), preferred_element_type=F32)
        part = part.reshape(NX, NL, NC, rows, kv)
        even, odd = part[:, :, 0], part[:, :, 1]
        own[hh, yy] = jnp.where(c == 0, even, odd)
        sib_out[hh, yy] = jnp.where(c == 0, odd, even).astype(BF16)

    def send_partial(it):
        _, _, hh, yy = place(it)
        remote(sib_out.at[hh, yy], sib_in.at[hh, yy], sib_send.at[0], sib_recv.at[it], sib).start()

    pl.loop(0, LAG)(partial_sum)
    pl.semaphore_wait(barrier, len(peers))
    remote(cnt.at[0], cnt_in.at[0], cnt_send.at[0], cnt_recv.at[0], sib).start()
    pl.loop(0, LAG)(send_partial)

    def exchange_first(it):
        e, d, hh, yy = place(it)
        wait_recv(sib_in.at[hh, yy], sib_recv.at[it])
        s1[hh, yy] = (own[hh, yy] + sib_in[hh, yy].astype(F32)).astype(BF16)
        go, back = 1 + 2 * hh, NX - 1 - 2 * hh
        remote(
            s1.at[hh, yy, xs(2), :, :, colx], m1x.at[hh, yy], p1_send.at[0], m1x_recv.at[hh, yy], dev(xx=xs(go))
        ).start()
        remote(
            s1.at[hh, yy, xs(back), :, :, colx], r1x.at[0, hh, yy], p1_send.at[1], p1x_recv.at[0], dev(xx=xs(back))
        ).start()

        @pl.when(d == 2)
        def _():
            remote(
                s1.at[hh, yy, :, :, :, coly], m1y.at[hh], p1_send.at[3], m1y_recv.at[hh], dev(yy=ys(go))
            ).start()

        @pl.when(d == back)
        def _():
            remote(
                s1.at[hh, yy, :, :, :, coly], r1y.at[0, hh], p1_send.at[4], p1y_recv.at[0], dev(yy=ys(back))
            ).start()

        @pl.loop(0, NL, unroll=True)
        def _(ll):
            k = lax.rem(hh * NL + ll + NZ - h * NL - l, NZ)
            up = k < 4
            odd = lax.rem(k, 2) == 1
            slot = jnp.where(odd, jnp.where((k == 1) | (k == 7), 0, 2) + jnp.where(up, 0, 1), 4)
            hop = jnp.where(odd, jnp.where(up, 1, NZ - 1), jnp.where(yy < NY // 2, 2, NZ - 2))

            @pl.when(odd | (k == 4))
            def _():
                remote(
                    s1.at[hh, yy, :, ll, :, colz], r1z.at[slot, yy], p1_send.at[6], p1z_recv.at[slot], zdev(hop)
                ).start()

    @pl.loop(LAG, steps)
    def _(it):
        partial_sum(it)
        send_partial(it)
        exchange_first(it - LAG)

    pl.loop(steps - LAG, steps)(exchange_first)

    wait_recv(cnt_in.at[0], cnt_recv.at[0])
    cnt[1] = cnt[0] + cnt_in[0]
    for k in xd:
        remote(cnt.at[1], cnt_in.at[k], cnt_send.at[1], cnt_recv.at[k], dev(xx=xs(k))).start()

    pending += [(sib_out, sib_send.at[0]), (cnt.at[0], cnt_send.at[0]), (cnt_in.at[pl.ds(0, NX - 1)], cnt_send.at[1])]
    pending += [(m1x, p1_send.at[0]), (r1x.at[0], p1_send.at[1]), (m1y, p1_send.at[3]), (r1y.at[0], p1_send.at[4])]
    pending += [(r1z.at[pl.ds(0, 5)], p1_send.at[6])]

    def relay_x(it):
        _, _, hh, yy = place(it)
        go = 1 + 2 * hh
        wait_recv(m1x.at[hh, yy], m1x_recv.at[hh, yy])
        f1x[hh, yy] = (s1[hh, yy, xs(go), :, :, colx].astype(F32) + m1x[hh, yy].astype(F32)).astype(BF16)
        remote(f1x.at[hh, yy], r1x.at[1, hh, yy], p1_send.at[2], p1x_recv.at[1], dev(xx=xs(go))).start()

    @pl.loop(0, NH)
    def _(hh):
        go = 1 + 2 * hh
        wait_recv(m1y.at[hh], m1y_recv.at[hh])

        @pl.loop(0, NX)
        def _(xx):
            f1y[hh, xx] = (s1[hh, ys(go), xx, :, :, coly].astype(F32) + m1y[hh, xx].astype(F32)).astype(BF16)

        remote(f1y.at[hh], r1y.at[1, hh], p1_send.at[5], p1y_recv.at[1], dev(yy=ys(go))).start()

    pl.loop(0, steps - LAG)(relay_x)

    for slot in (2, 3, 4):
        wait_recv(r1z.at[slot], p1z_recv.at[slot])
    for i, k in ((0, 2), (1, NZ - 2)):
        hh, ll = zat(k)
        for yy in range(NY):
            total = s1[hh, yy, :, ll, :, colz].astype(F32) + r1z[2 + i, yy].astype(F32)
            if (yy < NY // 2) == (i == 0):
                total += r1z[4, yy].astype(F32)
            f1z[i, yy] = total.astype(BF16)
        remote(f1z.at[i], r1z.at[5 + i], p1_send.at[7], p1z_recv.at[5 + i], zdev(k)).start()

    pl.loop(steps - LAG, steps)(relay_x)

    for k in xd:
        wait_recv(cnt_in.at[k], cnt_recv.at[k])
    cnt[2] = cnt[1] + cnt_in[1] + cnt_in[2] + cnt_in[3]
    for k in yd:
        remote(cnt.at[2], cnt_in.at[NX - 1 + k], cnt_send.at[2], cnt_recv.at[NX - 1 + k], dev(yy=ys(k))).start()

    pending += [(f1x, p1_send.at[2]), (f1y, p1_send.at[5]), (f1z, p1_send.at[7])]

    @pl.loop(0, NH * NY * NX)
    def _(i):
        nxt_copy(i).start()

    for copy in adam_copies:
        copy.start()

    for k in range(2):
        wait_recv(r1x.at[k], p1x_recv.at[k])

    @pl.loop(0, NH * NY)
    def _(i):
        hh, yy = lax.div(i, NY), lax.rem(i, NY)
        total = s1[hh, yy, x, :, :, colx].astype(F32)
        for k in range(2):
            total += r1x[k, hh, yy].astype(F32)
        s2x[hh, yy] = total.astype(BF16)

    for k in yd:
        remote(s2x.at[:, ys(k)], r2x.at[k - 1], p2_send.at[0], p2x_recv.at[k - 1], dev(yy=ys(k))).start()

    for k in range(2):
        wait_recv(r1y.at[k], p1y_recv.at[k])

    @pl.loop(0, NH * NX)
    def _(i):
        hh, xx = lax.div(i, NX), lax.rem(i, NX)
        total = s1[hh, y, xx, :, :, coly].astype(F32)
        for k in range(2):
            total += r1y[k, hh, xx].astype(F32)
        s2y[hh, xx] = total.astype(BF16)

    for k in xd:
        remote(s2y.at[:, xs(k)], r2y.at[k - 1], p2_send.at[1], p2y_recv.at[k - 1], dev(xx=xs(k))).start()

    for k in (0, 1, 5, 6):
        wait_recv(r1z.at[k], p1z_recv.at[k])

    @pl.loop(0, NY)
    def _(yy):
        total = s1[h, yy, :, l, :, colz].astype(F32)
        for k in (0, 1, 5, 6):
            total += r1z[k, yy].astype(F32)
        s2z[yy] = total.astype(BF16)

    for k in xd:
        remote(s2z.at[:, xs(k)], r2z.at[k - 1], p2_send.at[2], p2z_recv.at[k - 1], dev(xx=xs(k))).start()

    base = NX + NY - 1
    for k in yd:
        wait_recv(cnt_in.at[NX - 1 + k], cnt_recv.at[NX - 1 + k])
    cnt[3] = cnt[2] + cnt_in[NX] + cnt_in[NX + 1] + cnt_in[NX + 2]
    for e, f in zd:
        slot = base + e * NL + f - 1
        remote(cnt.at[3], cnt_in.at[slot], cnt_send.at[3], cnt_recv.at[slot], dev(hh=hs(e), ll=ls(f))).start()

    pending += [(r2x, p2_send.at[0]), (r2y, p2_send.at[1]), (r2z, p2_send.at[2])]
    pending += [(cnt_in.at[pl.ds(0, NY - 1)], cnt_send.at[2])]

    def send_sums(cols):
        for e, f in zd:
            slot = e * NL + f - 1
            remote(
                s3a.at[hs(e), ls(f), :, cols], r3a.at[slot, :, cols], p3_send.at[0], p3a_recv.at[slot],
                dev(hh=hs(e), ll=ls(f)),
            ).start()

    for k in yd:
        wait_recv(r2x.at[k - 1], p2x_recv.at[k - 1])
    total = s2x[:, y].astype(F32)
    for k in yd:
        total += r2x[k - 1].astype(F32)
    s3a[:, :, :, colx] = total.astype(BF16)
    send_sums(colx)
    for k in xd:
        wait_recv(r2y.at[k - 1], p2y_recv.at[k - 1])
    total = s2y[:, x].astype(F32)
    for k in xd:
        total += r2y[k - 1].astype(F32)
    s3a[:, :, :, coly] = total.astype(BF16)
    send_sums(coly)
    for k in xd:
        wait_recv(r2z.at[k - 1], p2z_recv.at[k - 1])
    total = s2z[:, x].astype(F32)
    for k in xd:
        total += r2z[k - 1].astype(F32)
    s3z[...] = total.astype(BF16)
    for k in yd:
        remote(s3z.at[ys(k)], r3z.at[k - 1], p3_send.at[1], p3z_recv.at[k - 1], dev(yy=ys(k))).start()

    for k in range(1, NZ):
        wait_recv(r3a.at[k - 1], p3a_recv.at[k - 1])
    sum_a = s3a[h, l].astype(F32)
    for k in range(1, NZ):
        sum_a += r3a[k - 1].astype(F32)
    for k in range(1, NZ):
        wait_recv(cnt_in.at[base + k - 1], cnt_recv.at[base + k - 1])
    count = cnt[3]
    for k in range(1, NZ):
        count += cnt_in[base + k - 1]
    count = count[0:1, 0:1]

    pending += [(r3a, p3_send.at[0]), (r3z, p3_send.at[1]), (cnt_in.at[pl.ds(0, NZ - 1)], cnt_send.at[3])]

    for copy in adam_copies:
        copy.wait()

    def adam(cols, summed):
        grad = summed / count
        new_first = 0.9 * first[:, cols] + 0.1 * grad
        new_second = 0.95 * second[:, cols] + 0.05 * grad * grad
        update = new_first / (1.0 - 0.9**STEP) / (jnp.sqrt(new_second / (1.0 - 0.95**STEP)) + 1e-08)
        new_master = master[:, cols] - 0.001 * (update + 0.1 * master[:, cols])
        o_first[:, cols] = new_first
        o_second[:, cols] = new_second
        o_master[:, cols] = new_master
        w[h, y, x, l, c, :, cols] = new_master.astype(BF16)

    adam(colxy, sum_a)

    def gather(ref, send, recv, to):
        remote(ref, ref, send, recv, to).start()

    for e, f in zd:
        gather(w.at[h, y, x, l, c, :, colxy], a3_send.at[0], a3a_recv.at[e * NL + f - 1], dev(hh=hs(e), ll=ls(f)))
    for k in yd:
        wait_recv(r3z.at[k - 1], p3z_recv.at[k - 1])
    sum_z = s3z[y].astype(F32)
    for k in yd:
        sum_z += r3z[k - 1].astype(F32)
    adam(colz, sum_z)
    for k in yd:
        gather(w.at[h, y, x, l, c, :, colz], a3_send.at[1], a3z_recv.at[k - 1], dev(yy=ys(k)))
    for k in yd:
        wait_recv(r3z.at[k - 1], a3z_recv.at[k - 1])
    for k in xd:
        gather(w.at[h, :, x, l, c, :, colz], a2_send.at[2], a2z_recv.at[k - 1], dev(xx=xs(k)))
    for k in range(1, NZ):
        wait_recv(r3a.at[k - 1], a3a_recv.at[k - 1])
    for k in yd:
        gather(w.at[:, y, x, :, c, :, colx], a2_send.at[0], a2x_recv.at[k - 1], dev(yy=ys(k)))
    for k in xd:
        gather(w.at[:, y, x, :, c, :, coly], a2_send.at[1], a2y_recv.at[k - 1], dev(xx=xs(k)))

    def xpart(k, hh):
        return w.at[hh, :, xs(k), :, c, :, colx]

    def ypart(k, hh):
        return w.at[hh, ys(k), :, :, c, :, coly]

    def zpart(k):
        hh, ll = zat(k)
        return w.at[hh, :, :, ll, c, :, colz]

    def zhalf(k, i):
        hh, ll = zat(k)
        return w.at[hh, pl.ds(i * (NY // 2), NY // 2), :, ll, c, :, colz]

    pending += [(r3a, a3_send.at[0]), (r3z, a3_send.at[1])]
    pending += [(r2x, a2_send.at[0]), (r2y, a2_send.at[1]), (r2z, a2_send.at[2])]

    def send_x(part, turn):
        for i in range(2):
            to = 1 + 2 * i if turn == 0 else 3 - 2 * i
            gather(w.at[i, part, x, :, c, :, colx], a1_send.at[0], a1x_recv.at[i, turn], dev(xx=xs(to)))

    def send_y(part, turn):
        for i in range(2):
            to = 1 + 2 * i if turn == 0 else 3 - 2 * i
            gather(w.at[i, y, part, :, c, :, coly], a1_send.at[2], a1y_recv.at[i, turn], dev(yy=ys(to)))

    def send_z(part, turn):
        for i in range(2):
            to = (2 - turn) * (1 - 2 * i)
            gather(w.at[h, :, part, l, c, :, colz], a1_send.at[4], a1z_recv.at[2 * turn + i, part], zdev(to))

    for turn in range(2):
        send_x(y, turn)
        send_y(x, turn)
        send_z(x, turn)
    for k in (1, 3, 2):
        wait_recv(r2z.at[k - 1], a2z_recv.at[k - 1])
        send_z(xs(NX - k), 0)
    for k in (1, 3, 2):
        wait_recv(r2x.at[k - 1], a2x_recv.at[k - 1])
        send_x(ys(NY - k), 0)
        wait_recv(r2y.at[k - 1], a2y_recv.at[k - 1])
        send_y(xs(NX - k), 0)
    for k in (1, 3, 2):
        send_x(ys(NY - k), 1)
        send_y(xs(NX - k), 1)
        send_z(xs(NX - k), 1)
    for i in range(2):
        gather(xpart(0, i), f_send.at[0], fx_recv.at[0], sib)
        gather(ypart(0, i), f_send.at[1], fy_recv.at[0], sib)
    gather(zpart(0), f_send.at[2], fz_recv.at[0], sib)

    def relay_z(part):
        for i, k in enumerate((-2, 2)):
            wait_recv(r1z.at[0, :, 0], a1z_recv.at[i, part])
            hh, ll = zat(k)
            gather(w.at[hh, :, part, ll, c, :, colz], a1_send.at[5], a1z_recv.at[6 + i, 0], zdev(-k // 2))
            half = pl.ds(i * (NY // 2), NY // 2)
            gather(w.at[hh, half, part, ll, c, :, colz], a1_send.at[5], a1z_recv.at[4 + i, 0], zdev(-k))

    relay_z(x)
    relay_z(xs(NX - 1))
    relay_z(xs(NX - 3))
    relay_z(xs(NX - 2))
    for i in range(2):
        wait_recv(m1x.at[0], a1x_recv.at[i, 0])
        gather(xpart(3 - 2 * i, i), a1_send.at[1], a1x_recv.at[i, 2], dev(xx=xs(1 + 2 * i)))
        wait_recv(m1y.at[0], a1y_recv.at[i, 0])
        gather(ypart(3 - 2 * i, i), a1_send.at[3], a1y_recv.at[i, 2], dev(yy=ys(1 + 2 * i)))
    for i in range(2):
        gather(xpart(3 - 2 * i, i), f_send.at[0], fx_recv.at[3 - 2 * i], sib)
        gather(ypart(3 - 2 * i, i), f_send.at[1], fy_recv.at[3 - 2 * i], sib)
    for k in (-2, 2):
        gather(zpart(k), f_send.at[2], fz_recv.at[0], sib)

    pending += [(r1x, a1_send.at[0]), (r1x.at[0], a1_send.at[1]), (r1y, a1_send.at[2]), (r1y.at[0], a1_send.at[3])]
    pending += [(r1z.at[pl.ds(0, 4)], a1_send.at[4]), (r1z.at[pl.ds(0, 3)], a1_send.at[5])]
    pending += [(w.at[:, :, :, :, c, :, cols], f_send.at[i]) for i, cols in enumerate((colx, coly, colz))]

    def project_x(k):
        for hh in range(NH):
            lhs = jnp.concatenate([nxt[(hh * NY + yy) * NX + xs(k)] for yy in range(NY)], axis=1)
            rhs = w[hh, :, xs(k), :, :, :, colx].reshape(NY * NL * NC * rows, ca)
            acc[:, colx] += jnp.dot(lhs, rhs, preferred_element_type=F32)

    def project_y(k):
        for hh in range(NH):
            lhs = jnp.concatenate([nxt[(hh * NY + ys(k)) * NX + xx] for xx in range(NX)], axis=1)
            rhs = w[hh, ys(k), :, :, :, :, coly].reshape(NX * NL * NC * rows, cb - ca)
            acc[:, coly] += jnp.dot(lhs, rhs, preferred_element_type=F32)

    acc[...] = jnp.zeros_like(acc)

    @pl.loop(0, NH * NY * NX)
    def _(i):
        nxt_copy(i).wait()

    wait_recv(r1x.at[0], fx_recv.at[0])
    project_x(0)
    for i in range(2):
        wait_recv(m1x.at[0], a1x_recv.at[i, 1])
        gather(xpart(1 + 2 * i, i), f_send.at[0], fx_recv.at[1 + 2 * i], sib)
        wait_recv(m1y.at[0], a1y_recv.at[i, 1])
        gather(ypart(1 + 2 * i, i), f_send.at[1], fy_recv.at[1 + 2 * i], sib)
    wait_recv(r1y.at[0], fy_recv.at[0])
    project_y(0)
    for i, k in enumerate((-1, 1)):
        for part in range(NX):
            wait_recv(r1z.at[0, :, 0], a1z_recv.at[2 + i, part])
        gather(zpart(k), f_send.at[2], fz_recv.at[0], sib)
    for k in (1, 3):
        wait_recv(r1x.at[0], fx_recv.at[k])
        project_x(k)
        wait_recv(r1y.at[0], fy_recv.at[k])
        project_y(k)
    for i in range(2):
        wait_recv(m1x.at[0], a1x_recv.at[i, 2])
        gather(xpart(2, i), f_send.at[0], fx_recv.at[2], sib)
        wait_recv(m1y.at[0], a1y_recv.at[i, 2])
        gather(ypart(2, i), f_send.at[1], fy_recv.at[2], sib)
    for i, k in enumerate((-3, 3)):
        wait_recv(r1z.at[0], a1z_recv.at[6 + i, 0])
        gather(zpart(k), f_send.at[2], fz_recv.at[0], sib)
    for i in range(2):
        wait_recv(r1z.at[0, pl.ds(0, NY // 2)], a1z_recv.at[4 + i, 0])
        gather(zhalf(4, i), f_send.at[2], fz_recv.at[0], sib)
    sec_copy = pltpu.make_async_copy(w.at[:, :, :, l, c], o_sec, out_sem.at[0])
    sec_copy.start()
    wait_recv(r1x.at[0], fx_recv.at[2])
    project_x(2)
    o_proj[:, colx] = acc[:, colx].astype(BF16)
    wait_recv(r1y.at[0], fy_recv.at[2])
    project_y(2)
    o_proj[:, coly] = acc[:, coly].astype(BF16)
    wait_recv(w.at[:, :, :, :, 1 - c, :, colz], fz_recv.at[0])

    @pl.loop(0, NH)
    def _(hh):
        lhs = jnp.concatenate([nxt[hh * NY * NX + i] for i in range(NY * NX)], axis=1)
        rhs = w[hh, :, :, :, :, :, colz].reshape(NY * width, kv - cb)
        acc[:, colz] += jnp.dot(lhs, rhs, preferred_element_type=F32)

    o_proj[:, colz] = acc[:, colz].astype(BF16)
    sec_copy.wait()

    drain()


def copy_out(*refs):
    src, dst, sem = refs[:5], refs[5:10], refs[10]
    copies = []
    for i in range(5):
        n, rows = PARTS[i], src[i].shape[0]
        for j in range(n):
            part = pl.ds(j * rows // n, rows // n)
            copies.append(pltpu.make_async_copy(src[i].at[part], dst[i].at[part], sem.at[len(copies)]))
    for copy in copies:
        copy.start()
    for copy in copies:
        copy.wait()


def body(tokens, out_grad, next_tokens, overflow, master, first_moment, second_moment):
    toks, din = tokens.shape
    rows, kv = master.shape
    ca, cb = 3 * kv // 8, 6 * kv // 8
    cx, cy, cz = ca, cb - ca, kv - cb
    width = NX * NL * NC * rows
    vmem, anym = pl.BlockSpec(memory_space=pltpu.VMEM), pl.BlockSpec(memory_space=pl.ANY)
    dma = pltpu.SemaphoreType.DMA
    shapes = (
        jax.ShapeDtypeStruct((rows, kv), F32),
        jax.ShapeDtypeStruct((rows, kv), F32),
        jax.ShapeDtypeStruct((rows, kv), F32),
        jax.ShapeDtypeStruct((NH, NY, NX, rows, kv), BF16),
        jax.ShapeDtypeStruct((toks, kv), BF16),
    )
    scratch = [
        pltpu.SMEM((1,), jnp.int32),
        pltpu.VMEM((rows, kv), F32),
        pltpu.VMEM((rows, kv), F32),
        pltpu.VMEM((rows, kv), F32),
        pltpu.VMEM((NH * NY, toks, width), BF16),
        pltpu.VMEM((toks, kv), BF16),
        pltpu.VMEM((NH * NY * NX, toks, NL * NC * rows), BF16),
        pltpu.VMEM((NH, NY, NX, NL, rows, kv), F32),
        pltpu.VMEM((NH, NY, NX, NL, rows, kv), BF16),
        pltpu.VMEM((NH, NY, NX, NL, rows, kv), BF16),
        pltpu.VMEM((NH, NY, NX, NL, rows, kv), BF16),
        pltpu.VMEM((NH, NY, NL, rows, cx), BF16),
        pltpu.VMEM((NH, NX, NL, rows, cy), BF16),
        pltpu.VMEM((NH, NY, NL, rows, cx), BF16),
        pltpu.VMEM((NH, NX, NL, rows, cy), BF16),
        pltpu.VMEM((2, NY, NX, rows, cz), BF16),
        pltpu.VMEM((2, NH, NY, NL, rows, cx), BF16),
        pltpu.VMEM((2, NH, NX, NL, rows, cy), BF16),
        pltpu.VMEM((7, NY, NX, rows, cz), BF16),
        pltpu.VMEM((NH, NY, NL, rows, cx), BF16),
        pltpu.VMEM((NH, NX, NL, rows, cy), BF16),
        pltpu.VMEM((NY, NX, rows, cz), BF16),
        pltpu.VMEM((NY - 1, NH, NL, rows, cx), BF16),
        pltpu.VMEM((NX - 1, NH, NL, rows, cy), BF16),
        pltpu.VMEM((NX - 1, NY, rows, cz), BF16),
        pltpu.VMEM((NH, NL, rows, cx + cy), BF16),
        pltpu.VMEM((NY, rows, cz), BF16),
        pltpu.VMEM((NZ - 1, rows, cx + cy), BF16),
        pltpu.VMEM((NY - 1, rows, cz), BF16),
        pltpu.VMEM((4, 8, 128), F32),
        pltpu.VMEM((1 + NX - 1 + NY - 1 + NZ - 1, 8, 128), F32),
        pltpu.VMEM((NH, NY, NX, NL, NC, rows, kv), BF16),
        pltpu.VMEM((toks, kv), F32),
    ]
    sems = (
        [(5,), (NH * NY,), (NH * NY * NX,), (1,), (1,), (NH * NY,), (4,), (NX + NY + NZ - 2,)]
        + [(8,), (NH, NY), (NH,), (2,), (2,), (7,)]
        + [(3,), (NY - 1,), (NX - 1,), (NX - 1,)]
        + [(2,), (NZ - 1,), (NY - 1,)]
        + [(2,), (NZ - 1,), (NY - 1,)]
        + [(3,), (NY - 1,), (NX - 1,), (NX - 1,)]
        + [(6,), (2, 3), (2, 3), (8, NX)]
        + [(3,), (NX,), (NY,), (1,)]
    )
    results = pl.pallas_call(
        kernel,
        out_shape=[pltpu.VMEM(shape.shape, shape.dtype) for shape in shapes],
        in_specs=[anym] * 7,
        out_specs=[vmem] * 5,
        scratch_shapes=scratch + [dma(n) for n in sems],
        compiler_params=pltpu.CompilerParams(
            collective_id=0, has_side_effects=True, vmem_limit_bytes=56 * 2**20
        ),
        cost_estimate=pl.CostEstimate(flops=4 * toks * din * kv, bytes_accessed=12 * 2**20, transcendentals=rows * kv),
    )(overflow, tokens, out_grad, next_tokens, master, first_moment, second_moment)
    new_master, new_first, new_second, sec, proj = pl.pallas_call(
        copy_out,
        out_shape=shapes,
        in_specs=[vmem] * 5,
        out_specs=[anym] * 5,
        scratch_shapes=[dma((sum(PARTS),))],
        compiler_params=pltpu.CompilerParams(vmem_limit_bytes=8 * 2**20),
    )(*results)
    return (new_master, new_first, new_second, sec.reshape(NH * NY * NX, rows, kv), proj)


def solution(mesh):
    return jax.shard_map(
        body,
        mesh=mesh,
        in_specs=(
            P(("node", "local"), None),
            P(("node", "local"), None),
            P(("node", "local"), None),
            P(("node", "local")),
            P(("node", "local"), None),
            P(("node", "local"), None),
            P(("node", "local"), None),
        ),
        out_specs=(
            P(("node", "local"), None),
            P(("node", "local"), None),
            P(("node", "local"), None),
            P(None, "local", None),
            P(("node", "local"), None),
        ),
        check_vma=False,
    )
```
